32 devices in a mesh: ev: 4 (over y, x), slab: 8 (over z, core).
Axes of the slice: x: 2, y: 2, z: 4, core: 2. Of those that a mesh axis runs over, the one named last changes fastest.
Arguments:
- kernels: float32 [1024, 32, 128], P(('ev', 'slab')), may hold values from -1 to 1
- block_ids: int32 [1024, 32], P(('ev', 'slab')), may hold values from 0 to 8191, as said below
- delays: float32 [1024], P(('ev', 'slab')), may hold values from -240 to 240
Outputs:
- solution: float32 [64, 128, 128], P('slab')
The draws below stay inside these ranges and needn't reach their ends.
Inputs may be any that keep to these rules, and one draw needn't show every extreme that they name: `block_ids`: block b is column (b // 128, b % 128) and lies in slab b // 1024. Of the 1024 ids of one device's rays, exactly 128 lie in each slab; ids may repeat.
All inputs are finite; a program needn't handle non-finite values.
Results may differ from the reference program's by a relative error of at most 0.0001.
Values sent between devices are 32-bit elements; how exact they have to be, the bound alone decides.
A program may use at most 64 MiB of HBM per device.

```python
import jax
import jax.numpy as jnp
from jax import lax

BLOCK = 128
K = 32
RAYS_DEV = 32
CX = 8
NY = 128
ITERS = 2
RAYS = 1024
NX = 64


def draw_block_ids(key, part):
    slab_count = NX // CX
    per_device = RAYS_DEV * K
    per_slab = per_device // slab_count
    device_count = RAYS // RAYS_DEV
    cells_slab = CX * NY
    owners_base = jnp.repeat(jnp.arange(slab_count, dtype=jnp.int32), per_slab)
    key_list = jax.random.split(jax.random.fold_in(key, 11), device_count)

    def shuffle(one_key):
        return jax.random.permutation(one_key, owners_base)
    owners = jax.vmap(shuffle)(key_list)
    inside = jax.random.randint(jax.random.fold_in(key, 12), (device_count, per_device), 0, cells_slab, dtype=jnp.int32)
    first_low = jnp.argmax(owners == 0, axis=1)
    first_high = jnp.argmax(owners == slab_count - 1, axis=1)
    rows_index = jnp.arange(device_count)
    inside = inside.at[rows_index, first_high].set(cells_slab - 1)
    inside = inside.at[rows_index, first_low].set(0)
    block_list = owners * cells_slab + inside
    return block_list.reshape(RAYS, K).astype(jnp.int32)


def draw_kernels(key, part):
    slab_count = NX // CX
    cells_slab = CX * NY
    ids = draw_block_ids(key, part)
    owner = (ids // cells_slab).astype(jnp.float32)
    ramp = 1.0 + 2.0 * owner / max(slab_count - 1, 1)
    base_key = jax.random.fold_in(key, 31)
    scale = (K * BLOCK) ** (-0.5)
    values = jnp.clip(jax.random.normal(base_key, (RAYS, K, BLOCK), jnp.float32), -6.0, 6.0)
    factor = ramp
    return jnp.clip(values * factor[:, :, None] * scale, -1.0, 1.0).astype(jnp.float32)


def draw_delays(key, part):
    ramp = 1.0 + 2.0 * jnp.arange(RAYS, dtype=jnp.float32) / (RAYS - 1)
    noise = jnp.clip(jax.random.normal(key, (RAYS,), jnp.float32), -4.5, 4.5)
    return 16.0 * ramp * noise


def setup_inputs(seed: int = 0) -> dict:
    streams_of = jax.random.split(jax.random.key(seed), 4)
    return {
        "kernels": draw_kernels(jax.random.fold_in(streams_of[3], 71), 0),
        "block_ids": draw_block_ids(jax.random.fold_in(streams_of[3], 71), 0),
        "delays": draw_delays(jax.random.fold_in(streams_of[3], 71), 0),
    }


damping = 0.3
norm_epsilon = 1e-06

def laplace_grid(field_in):
    rolled = jnp.roll(field_in, 1, 0) + jnp.roll(field_in, -1, 0)
    beside_all = jnp.pad(field_in, ((0, 0), (1, 1), (1, 1)))
    beside = rolled + beside_all[:, 2:, 1:-1] + beside_all[:, :-2, 1:-1] + beside_all[:, 1:-1, 2:] + beside_all[:, 1:-1, :-2]
    return 6.0 * field_in - beside

def ray_apply(model_in, block_ids, kernels):
    groups = RAYS // RAYS_DEV
    table = model_in.reshape(NX * NY, BLOCK)

    def per_group(pair):
        group_ids, group_kernels = pair
        return lax.optimization_barrier(jnp.sum(table[group_ids] * group_kernels, axis=(1, 2)))
    result = lax.map(per_group, (block_ids.reshape(groups, RAYS_DEV, K), kernels.reshape(groups, RAYS_DEV, K, BLOCK)))
    return result.reshape(RAYS)

def ray_transpose(ray_weights, block_ids, kernels):
    groups = RAYS // RAYS_DEV

    def add_group(summed, triple):
        group_ids, group_kernels, group_weights = triple
        terms = group_kernels * group_weights[:, None, None]
        return (summed.at[group_ids.reshape(-1)].add(terms.reshape(-1, BLOCK)), None)
    start = jnp.zeros((NX * NY, BLOCK), jnp.float32)
    summed, leftover = lax.scan(add_group, start, (block_ids.reshape(groups, RAYS_DEV, K), kernels.reshape(groups, RAYS_DEV, K, BLOCK), ray_weights.reshape(groups, RAYS_DEV)))
    return summed.reshape(NX, NY, BLOCK)

def reference(kernels, block_ids, delays):
    beta_now = jnp.sqrt(jnp.sum(delays * delays) + norm_epsilon)
    ray_part = delays / beta_now
    model_part = jnp.zeros((NX, NY, BLOCK), jnp.float32)
    direction = ray_transpose(ray_part, block_ids, kernels)
    alpha_now = jnp.sqrt(jnp.sum(direction * direction) + norm_epsilon)
    direction = direction / alpha_now
    search = direction
    solution = jnp.zeros((NX, NY, BLOCK), jnp.float32)
    phi_bar = beta_now
    rho_bar = alpha_now
    for iteration in range(ITERS):
        ray_part = ray_apply(direction, block_ids, kernels) - alpha_now * ray_part
        model_part = damping * laplace_grid(direction) - alpha_now * model_part
        beta_now = jnp.sqrt(jnp.sum(ray_part * ray_part) + jnp.sum(model_part * model_part) + norm_epsilon)
        ray_part = ray_part / beta_now
        model_part = model_part / beta_now
        rho_now = jnp.sqrt(rho_bar * rho_bar + beta_now * beta_now)
        cosine = rho_bar / rho_now
        sine_part = beta_now / rho_now
        phi_now = cosine * phi_bar
        phi_bar = sine_part * phi_bar
        solution = solution + phi_now / rho_now * search
        if iteration + 1 < ITERS:
            direction = ray_transpose(ray_part, block_ids, kernels) + damping * laplace_grid(model_part) - beta_now * direction
            alpha_now = jnp.sqrt(jnp.sum(direction * direction) + norm_epsilon)
            direction = direction / alpha_now
            theta_now = sine_part * alpha_now
            rho_bar = -cosine * alpha_now
            search = direction - theta_now / rho_now * search
    return solution
```

```python
import functools

import jax
import jax.numpy as jnp
from jax import lax
from jax.experimental import pallas as pl
from jax.experimental.pallas import tpu as pltpu
from jax.sharding import PartitionSpec as P

CX = 8
NY = 128
LANES = 128
MESH = pl.DeviceIdType.MESH

damping = 0.3
norm_epsilon = 1e-06


def iota(shape, dim):
    return lax.broadcasted_iota(jnp.int32, shape, dim).astype(jnp.float32)


def total(x):
    return jnp.sum(jnp.sum(x, axis=0, keepdims=True), axis=1, keepdims=True)


def one_hot(mask):
    return jnp.where(mask, 1.0, 0.0).astype(jnp.bfloat16)


def two_parts(x):
    high = x.astype(jnp.bfloat16)
    low = (x - high.astype(jnp.float32)).astype(jnp.bfloat16)
    return jnp.concatenate([high, low], axis=1)


def plane_laplace(ref, p):
    x = ref[p]
    ny, nz = x.shape
    row = lax.broadcasted_iota(jnp.int32, x.shape, 0)
    lane = lax.broadcasted_iota(jnp.int32, x.shape, 1)
    beside = ref[p + 1] + ref[p - 1]
    beside = beside + jnp.where(row < ny - 1, pltpu.roll(x, ny - 1, 0), 0.0)
    beside = beside + jnp.where(row > 0, pltpu.roll(x, 1, 0), 0.0)
    beside = beside + jnp.where(lane < nz - 1, pltpu.roll(x, nz - 1, 1), 0.0)
    beside = beside + jnp.where(lane > 0, pltpu.roll(x, 1, 1), 0.0)
    return 6.0 * x - beside


def kernel(
    ne, n, ps, rays,
    kern_ref, meta_ref, delay_ref, out_ref,
    send, recv, pieces, s_mat, st_mat, contrib, ray_col, acc, table2,
    d0, m1, d1, y0, y1, q1, q2, u0_ref, u1_ref,
    s1_send, s2_send, rsem, halo_send, halo_recv, bsend, brecv,
):
    nd = ne * n
    g = LANES // ps
    cpg = n // g
    entries = n * ps
    cells = CX * NY
    e = lax.axis_index("ev")
    s = lax.axis_index("slab")
    me = e * n + s

    barrier = pltpu.get_barrier_semaphore()

    def greet(k, c):
        other = lax.rem(me + k, nd)
        pl.semaphore_signal(
            barrier, inc=1, device_id=(other // n, lax.rem(other, n)), device_id_type=MESH
        )
        return c

    lax.fori_loop(1, nd, greet, 0)

    slab_row = meta_ref[3:4, :]
    owner = slab_row == iota((n, entries), 0)
    before = one_hot(iota((entries, entries), 0) < iota((entries, entries), 1))
    counts = jnp.dot(one_hot(owner), before, preferred_element_type=jnp.float32)
    rank = jnp.sum(jnp.where(owner, counts, 0.0), axis=0, keepdims=True)
    position = slab_row * ps + rank

    x = kern_ref[...]
    k1 = x.astype(jnp.bfloat16)
    x = x - k1.astype(jnp.float32)
    k2 = x.astype(jnp.bfloat16)
    x = x - k2.astype(jnp.float32)
    pieces[:, :LANES] = k1
    pieces[:, LANES : 2 * LANES] = k2
    pieces[:, 2 * LANES :] = x.astype(jnp.bfloat16)
    meta = meta_ref[...].astype(jnp.bfloat16)

    def sort_tile(t, c):
        pm = one_hot(iota((LANES, entries), 0) + (t * LANES).astype(jnp.float32) == position)
        rows = jnp.dot(pm, pieces[...], preferred_element_type=jnp.float32)
        rows = rows[:, :LANES] + rows[:, LANES : 2 * LANES] + rows[:, 2 * LANES :]
        tile = lax.dot_general(
            meta, pm, (((1,), (1,)), ((), ())), preferred_element_type=jnp.float32
        )
        for j in range(g):
            send[t * g + j, :ps] = rows[j * ps : (j + 1) * ps]
            part = tile if j == 0 else pltpu.roll(tile, LANES - j * ps, 1)
            send[t * g + j, ps:] = jnp.where(iota(part.shape, 0) == 3.0, delay_ref[...], part)
        return c

    lax.fori_loop(0, entries // LANES, sort_tile, 0)
    pl.semaphore_wait(barrier, nd - 1)

    def stage1(k):
        t = lax.rem(s + k, n)
        return pltpu.make_async_remote_copy(
            src_ref=send.at[t], dst_ref=recv.at[me], send_sem=s1_send.at[k], recv_sem=rsem.at[me],
            device_id=(e, t), device_id_type=MESH,
        )

    def start1(k, c):
        stage1(k).start()
        return c

    lax.fori_loop(1, n, start1, 0)
    recv[me] = send[s]

    def stage2(slot, k, j):
        return pltpu.make_async_remote_copy(
            src_ref=recv.at[slot], dst_ref=recv.at[slot], send_sem=s2_send.at[k * ne + j],
            recv_sem=rsem.at[slot], device_id=(lax.rem(e + j, ne), s), device_id_type=MESH,
        )

    for j in range(1, ne):
        stage2(me, 0, j).start()

    def forward(k, c):
        slot = e * n + lax.rem(s - k + n, n)
        stage2(slot, k, 1).wait_recv()
        for j in range(1, ne):
            stage2(slot, k, j).start()
        return c

    lax.fori_loop(1, n, forward, 0)

    acc[...] = jnp.zeros_like(acc)

    def as_column(row):
        return jnp.broadcast_to(row, (LANES, LANES)).T[:ps]

    def slot_terms(slot, weights):
        base = pl.multiple_of(slot * ps, ps)
        match = iota((ps, LANES), 1) == ray_col[pl.ds(base, ps), :]
        w = jnp.sum(jnp.where(match, weights, 0.0), axis=1, keepdims=True)
        contrib[pl.ds(base, ps), :] = two_parts(recv[slot, :ps] * w)

    def chunk(group, cc):
        row_i = recv[cc * g, ps : ps + 1]
        row_j = recv[cc * g, ps + 1 : ps + 2]
        for j in range(1, g):
            here = (lax.broadcasted_iota(jnp.int32, (1, LANES), 1) // ps) == j
            row_i = jnp.where(here, pltpu.roll(recv[cc * g + j, ps:], j * ps, 1)[0:1], row_i)
            row_j = jnp.where(here, pltpu.roll(recv[cc * g + j, ps:], j * ps, 1)[1:2], row_j)
        for j in range(g):
            slot = cc * g + j
            base = pl.multiple_of(slot * ps, ps)
            ray_col[pl.ds(base, ps), :] = as_column(recv[slot, ps + 2 : ps + 3])
            slot_terms(slot, recv[slot, ps + 3 : ps + 4])
        first = pl.multiple_of(cc * LANES, LANES)
        hot = one_hot(iota((cells, LANES), 0) == row_i * NY + row_j)
        s_mat[:, pl.ds(first, LANES)] = hot
        acc[group] += jnp.dot(
            hot, contrib[pl.ds(first, LANES), :], preferred_element_type=jnp.float32
        )

    def own_chunk(k, c):
        inner = lax.rem(s // g - k + cpg, cpg)
        chunk(e, e * cpg + inner)
        for j in range(g):
            slot = inner * g + j
            tile = recv[e * n + slot, ps:]
            cell = as_column(tile[0:1] * NY + tile[1:2])
            for b in range(cells // LANES):
                st_mat[pl.ds(pl.multiple_of(slot * ps, ps), ps), b * LANES : (b + 1) * LANES] = (
                    one_hot(iota((ps, LANES), 1) + float(b * LANES) == cell)
                )
        return c

    lax.fori_loop(0, cpg, own_chunk, 0)

    def other_chunk(k, c):
        inner = lax.rem(s // g - k + cpg, cpg)

        def per_group(j, c):
            group = lax.rem(e + j, ne)
            for i in range(g):
                stage2((group * cpg + inner) * g + i, 0, 1).wait_recv()
            chunk(group, group * cpg + inner)
            return c

        return lax.fori_loop(1, ne, per_group, c)

    lax.fori_loop(0, cpg, other_chunk, 0)

    def all_delays():
        rows = [recv[d, ps + 3 : ps + 4] for d in range(nd)]
        return jnp.concatenate(rows, axis=0)

    delays = jnp.where(iota((nd, LANES), 1) < float(rays), all_delays(), 0.0)
    beta0 = jnp.sqrt(total(delays * delays) + norm_epsilon)
    u0 = delays / beta0
    u0_ref[...] = u0

    def apply_rays(tiles, squares):
        def slot_rows(k, c):
            base = pl.multiple_of(k * ps, ps)
            picked = jnp.dot(
                st_mat[pl.ds(base, ps), :], table2[...], preferred_element_type=jnp.float32
            )
            picked = picked[:, :LANES] + picked[:, LANES:]
            sums = jnp.sum(picked * recv[e * n + k, :ps], axis=1, keepdims=True)
            rows = pl.multiple_of((e * n + k) * ps, ps)
            match = iota((ps, LANES), 1) == ray_col[pl.ds(rows, ps), :]
            tiles[me, pl.ds(k, 1)] = jnp.sum(jnp.where(match, sums, 0.0), axis=0, keepdims=True)
            return c

        lax.fori_loop(0, n, slot_rows, 0)
        at = (iota((n, LANES), 0) == 0.0) & (iota((n, LANES), 1) == float(rays))
        tiles[me] = jnp.where(at, squares, tiles[me])

    def share_all(tiles, r):
        def copy(k):
            other = lax.rem(me + k, nd)
            return pltpu.make_async_remote_copy(
                src_ref=tiles.at[me], dst_ref=tiles.at[me], send_sem=bsend.at[r], recv_sem=brecv.at[r],
                device_id=(other // n, lax.rem(other, n)), device_id_type=MESH,
            )

        def start(k, c):
            copy(k).start()
            return c

        lax.fori_loop(1, nd, start, 0)
        rest = tiles.at[pl.ds(0, nd - 1)]
        both = pltpu.make_async_remote_copy(
            src_ref=rest, dst_ref=rest, send_sem=bsend.at[r], recv_sem=brecv.at[r],
            device_id=(e, s), device_id_type=MESH,
        )
        return both

    def share_slab(tiles, r):
        def start(k, c):
            pltpu.make_async_remote_copy(
                src_ref=tiles.at[s], dst_ref=tiles.at[s], send_sem=bsend.at[r], recv_sem=brecv.at[r],
                device_id=(e, lax.rem(s + k, n)), device_id_type=MESH,
            ).start()
            return c

        lax.fori_loop(1, n, start, 0)
        rest = tiles.at[pl.ds(0, n - 1)]
        return pltpu.make_async_remote_copy(
            src_ref=rest, dst_ref=rest, send_sem=bsend.at[r], recv_sem=brecv.at[r],
            device_id=(e, s), device_id_type=MESH,
        )

    def ray_sums(tiles):
        groups = []
        for k in range(ne):
            part = tiles[k * n]
            for j in range(1, n):
                part = part + tiles[k * n + j]
            groups.append(part)
        value = jnp.concatenate(groups, axis=0)
        at = (iota((nd, LANES), 0) == 0.0) & (iota((nd, LANES), 1) == float(rays))
        square = total(jnp.where(at, value, 0.0))
        return jnp.where(iota((nd, LANES), 1) < float(rays), value, 0.0), square

    def slab_sum(tiles):
        part = tiles[0]
        for j in range(1, n):
            part = part + tiles[j]
        return part[0:1, 0:1]

    def halo(ref, width, r):
        right, left = lax.rem(s + 1, n), lax.rem(s - 1 + n, n)
        up = pltpu.make_async_remote_copy(
            src_ref=ref.at[pl.ds(CX, width)], dst_ref=ref.at[pl.ds(0, width)],
            send_sem=halo_send.at[2 * r], recv_sem=halo_recv.at[2 * r],
            device_id=(e, right), device_id_type=MESH,
        )
        down = pltpu.make_async_remote_copy(
            src_ref=ref.at[pl.ds(width, width)], dst_ref=ref.at[pl.ds(CX + width, width)],
            send_sem=halo_send.at[2 * r + 1], recv_sem=halo_recv.at[2 * r + 1],
            device_id=(e, left), device_id_type=MESH,
        )
        up.start()
        down.start()
        return up, down

    def zero():
        return jnp.zeros((1, 1), jnp.float32)

    def plane_rows(p):
        return pl.ds(pl.multiple_of(p * NY, NY), NY)

    def first_plane(p, square):
        value = acc[0, plane_rows(p)]
        for k in range(1, ne):
            value = value + acc[k, plane_rows(p)]
        value = (value[:, :LANES] + value[:, LANES:]) / beta0
        d0[p + 2] = value
        table2[plane_rows(p), :] = two_parts(value)
        return square + total(value * value)

    square = lax.fori_loop(0, CX, first_plane, zero())
    up, down = halo(d0, 2, 0)
    apply_rays(y0, square)
    rays_done = share_all(y0, 0)
    rays_done.wait_recv()
    up.wait()
    down.wait()
    sums, square = ray_sums(y0)
    alpha0 = jnp.sqrt(square + norm_epsilon)

    u1 = sums / alpha0 - alpha0 * u0_ref[...]
    u1_ref[...] = u1
    ray_square = total(u1 * u1)

    def model_plane(p, square):
        value = damping * plane_laplace(d0, p + 1) / alpha0
        m1[p] = value
        inside = jnp.where((p > 0) & (p < CX + 1), 1.0, 0.0)
        return square + inside * total(value * value)

    square = lax.fori_loop(0, CX + 2, model_plane, zero())
    q1[s] = jnp.broadcast_to(square, (8, LANES))
    part_done = share_slab(q1, 2)

    def again(slot, c):
        slot_terms(slot, u1_ref[pl.ds(slot, 1), :])
        return c

    lax.fori_loop(0, nd, again, 0)

    def scatter_plane(p, c):
        acc[0, plane_rows(p)] = jnp.dot(
            s_mat[plane_rows(p), :], contrib[...], preferred_element_type=jnp.float32
        )
        return c

    lax.fori_loop(0, CX, scatter_plane, 0)
    part_done.wait_recv()
    beta1 = jnp.sqrt(ray_square + slab_sum(q1) + norm_epsilon)
    u1 = u1_ref[...] / beta1

    def next_plane(p, square):
        value = acc[0, plane_rows(p)]
        value = (value[:, :LANES] + value[:, LANES:]) / beta1
        value = value + damping * plane_laplace(m1, p + 1) / beta1 - beta1 / alpha0 * d0[p + 2]
        d1[p + 1] = value
        table2[plane_rows(p), :] = two_parts(value)
        return square + total(value * value)

    square = lax.fori_loop(0, CX, next_plane, zero())
    up1, down1 = halo(d1, 1, 1)
    apply_rays(y1, square)
    rays_done1 = share_all(y1, 1)
    rho1 = jnp.sqrt(alpha0 * alpha0 + beta1 * beta1)
    cosine1 = alpha0 / rho1
    sine1 = beta1 / rho1
    phi1 = cosine1 * beta0
    phi_bar = sine1 * beta0
    rays_done1.wait_recv()
    up1.wait()
    down1.wait()
    sums, square = ray_sums(y1)
    alpha1 = jnp.sqrt(square + norm_epsilon)
    theta1 = sine1 * alpha1
    rho_bar = -cosine1 * alpha1

    u2 = sums / alpha1 - alpha1 * u1

    def last_plane(p, square):
        value = damping * plane_laplace(d1, p + 1) / alpha1 - alpha1 / beta1 * m1[p + 1]
        return square + total(value * value)

    square = lax.fori_loop(0, CX, last_plane, zero())
    q2[s] = jnp.broadcast_to(square, (8, LANES))
    last_done = share_slab(q2, 3)
    ray_square = total(u2 * u2)
    last_done.wait_recv()
    beta2 = jnp.sqrt(ray_square + slab_sum(q2) + norm_epsilon)
    rho2 = jnp.sqrt(rho_bar * rho_bar + beta2 * beta2)
    phi2 = rho_bar / rho2 * phi_bar

    def finish(p, c):
        first = d0[p + 2] / alpha0
        search = d1[p + 1] / alpha1 - theta1 / rho1 * first
        out_ref[p] = phi1 / rho1 * first + phi2 / rho2 * search
        return c

    lax.fori_loop(0, CX, finish, 0)

    def sent1(k, c):
        stage1(k).wait_send()
        return c

    lax.fori_loop(1, n, sent1, 0)

    def sent2(k, c):
        for j in range(1, ne):
            stage2(me, k, j).wait_send()
        return c

    lax.fori_loop(0, n, sent2, 0)
    rays_done.wait_send()
    part_done.wait_send()
    rays_done1.wait_send()
    last_done.wait_send()


def solution(mesh):
    ne, n = mesh.shape["ev"], mesh.shape["slab"]

    def on_device(kernels, block_ids, delays):
        rays, per_ray, width = kernels.shape
        entries = rays * per_ray
        ps = entries // n
        nd = ne * n
        cells = CX * NY
        flat = block_ids.reshape(1, entries)
        ray = lax.broadcasted_iota(jnp.int32, (1, entries), 1) // per_ray
        rest = jnp.zeros((4, entries), jnp.int32)
        meta = jnp.concatenate(
            [flat % cells // NY, flat % NY, ray, flat // cells, rest], axis=0
        ).astype(jnp.float32)
        delay_row = jnp.pad(delays.reshape(1, rays), ((0, 0), (0, LANES - rays)))
        f32, bf16 = jnp.float32, jnp.bfloat16
        vmem = pl.BlockSpec(memory_space=pltpu.VMEM)
        return pl.pallas_call(
            functools.partial(kernel, ne, n, ps, rays),
            out_shape=jax.ShapeDtypeStruct((CX, NY, width), f32),
            in_specs=[vmem] * 3,
            out_specs=vmem,
            scratch_shapes=[
                pltpu.VMEM((n, ps + 8, width), f32),
                pltpu.VMEM((nd, ps + 8, width), f32),
                pltpu.VMEM((entries, 3 * width), bf16),
                pltpu.VMEM((cells, nd * ps), bf16),
                pltpu.VMEM((entries, cells), bf16),
                pltpu.VMEM((nd * ps, 2 * width), bf16),
                pltpu.VMEM((nd * ps, width), f32),
                pltpu.VMEM((ne, cells, 2 * width), f32),
                pltpu.VMEM((cells, 2 * width), bf16),
                pltpu.VMEM((CX + 4, NY, width), f32),
                pltpu.VMEM((CX + 2, NY, width), f32),
                pltpu.VMEM((CX + 2, NY, width), f32),
                pltpu.VMEM((nd, n, width), f32),
                pltpu.VMEM((nd, n, width), f32),
                pltpu.VMEM((n, 8, width), f32),
                pltpu.VMEM((n, 8, width), f32),
                pltpu.VMEM((nd, width), f32),
                pltpu.VMEM((nd, width), f32),
                pltpu.SemaphoreType.DMA((n,)),
                pltpu.SemaphoreType.DMA((n * ne,)),
                pltpu.SemaphoreType.DMA((nd,)),
                pltpu.SemaphoreType.DMA((4,)),
                pltpu.SemaphoreType.DMA((4,)),
                pltpu.SemaphoreType.DMA((4,)),
                pltpu.SemaphoreType.DMA((4,)),
            ],
            compiler_params=pltpu.CompilerParams(
                collective_id=0, has_side_effects=True, vmem_limit_bytes=60 * 1024 * 1024
            ),
        )(kernels.reshape(entries, width), meta, delay_row)

    in_specs = (P(("ev", "slab"), None, None), P(("ev", "slab"), None), P(("ev", "slab")))
    return jax.shard_map(
        on_device, mesh=mesh, in_specs=in_specs, out_specs=P("slab", None, None), check_vma=False
    )
```

```python
import functools

import jax
import jax.numpy as jnp
from jax import lax
from jax.experimental import pallas as pl
from jax.experimental.pallas import tpu as pltpu
from jax.sharding import PartitionSpec as P

CX = 8
NY = 128
LANES = 128
MESH = pl.DeviceIdType.MESH

damping = 0.3
norm_epsilon = 1e-06


def iota(shape, dim):
    return lax.broadcasted_iota(jnp.int32, shape, dim).astype(jnp.float32)


def total(x):
    return jnp.sum(jnp.sum(x, axis=0, keepdims=True), axis=1, keepdims=True)


def one_hot(mask):
    return jnp.where(mask, 1.0, 0.0).astype(jnp.bfloat16)


def two_parts(x):
    high = x.astype(jnp.bfloat16)
    low = (x - high.astype(jnp.float32)).astype(jnp.bfloat16)
    return jnp.concatenate([high, low], axis=0)


PAD = 8


def kernel(
    ne, n, ps, rays, cw,
    kern_ref, meta_ref, delay_ref, out_ref,
    send, recv, pieces, s_mat, contrib, kt, table2, rr_ref, w_ref, e_ref, u_ref,
    d0, m1, d1, full0, full1, y0, y1, q0, q1, q2, q3,
    ssem, rsem, halo_send, halo_recv, full_send, full_recv, bsend, brecv,
):
    nd = ne * n
    g = LANES // ps
    cpg = n // g
    nc = nd // g
    entries = n * ps
    cells = CX * NY
    pack = LANES // rays
    packed = nd // pack
    e = lax.axis_index("ev")
    s = lax.axis_index("slab")
    me = e * n + s

    barrier = pltpu.get_barrier_semaphore()

    def greet(k, c):
        other = lax.rem(me + k, nd)
        pl.semaphore_signal(
            barrier, inc=1, device_id=(other // n, lax.rem(other, n)), device_id_type=MESH
        )
        return c

    lax.fori_loop(1, nd, greet, 0)

    slab_row = meta_ref[3:4, :]
    owner = slab_row == iota((n, entries), 0)
    before = one_hot(iota((entries, entries), 0) < iota((entries, entries), 1))
    counts = jnp.dot(one_hot(owner), before, preferred_element_type=jnp.float32)
    rank = jnp.sum(jnp.where(owner, counts, 0.0), axis=0, keepdims=True)
    position = slab_row * ps + rank

    x = kern_ref[...]
    k1 = x.astype(jnp.bfloat16)
    x = x - k1.astype(jnp.float32)
    k2 = x.astype(jnp.bfloat16)
    x = x - k2.astype(jnp.float32)
    pieces[:, :LANES] = k1
    pieces[:, LANES : 2 * LANES] = k2
    pieces[:, 2 * LANES :] = x.astype(jnp.bfloat16)
    meta = meta_ref[...].astype(jnp.bfloat16)
    pl.semaphore_wait(barrier, nd - 1)

    def rows_to(dest):
        return pltpu.make_async_remote_copy(
            src_ref=send.at[dest], dst_ref=recv.at[me], send_sem=ssem.at[dest], recv_sem=rsem.at[me],
            device_id=(dest // n, lax.rem(dest, n)), device_id_type=MESH,
        )

    def sort_tile(k, c):
        t = lax.rem(s // g + cpg // 2 + k, cpg)
        pm = one_hot(iota((LANES, entries), 0) + (t * LANES).astype(jnp.float32) == position)
        rows = jnp.dot(pm, pieces[...], preferred_element_type=jnp.float32)
        rows = (rows[:, :LANES] + rows[:, LANES : 2 * LANES] + rows[:, 2 * LANES :]).T
        tile = lax.dot_general(
            meta, pm, (((1,), (1,)), ((), ())), preferred_element_type=jnp.float32
        )
        for j in range(g):
            part = tile if j == 0 else pltpu.roll(tile, LANES - j * ps, 1)
            part = jnp.where(iota(part.shape, 0) == 3.0, delay_ref[...], part)
            block = rows if j == 0 else pltpu.roll(rows, LANES - j * ps, 1)
            for i in range(ne):
                dest = i * n + t * g + j
                send[dest, :cw] = block[i * cw : (i + 1) * cw]
                send[dest, cw:] = part

                @pl.when(dest != me)
                def _():
                    rows_to(dest).start()

        return c

    lax.fori_loop(0, cpg, sort_tile, 0)
    recv[me] = send[me]

    def chunk(cc):
        for j in range(g):
            slot = cc * g + j

            @pl.when(slot != me)
            def _():
                pltpu.make_async_remote_copy(
                    src_ref=recv.at[slot], dst_ref=recv.at[slot], send_sem=ssem.at[slot],
                    recv_sem=rsem.at[slot], device_id=(e, s), device_id_type=MESH,
                ).wait_recv()

            u_ref[pl.ds(slot, 1), :] = recv[slot, cw + 3 : cw + 4]
        block = recv[cc * g]
        for j in range(1, g):
            here = (lax.broadcasted_iota(jnp.int32, block.shape, 1) // ps) == j
            block = jnp.where(here, pltpu.roll(recv[cc * g + j], j * ps, 1), block)
        first = pl.multiple_of(cc * LANES, LANES)
        kt[:, pl.ds(first, LANES)] = block[:cw]
        rr_ref[pl.ds(cc, 1), :] = block[cw + 2 : cw + 3]
        cell = block[cw : cw + 1] * NY + block[cw + 1 : cw + 2]
        s_mat[:, pl.ds(first, LANES)] = one_hot(iota((cells, LANES), 0) == cell)

    def arrivals(k, c):
        inner = lax.rem(s // g - cpg // 2 - k + 2 * cpg, cpg)

        def per_group(j, c):
            chunk(lax.rem(e + j, ne) * cpg + inner)
            return c

        return lax.fori_loop(0, ne, per_group, c)

    lax.fori_loop(0, cpg, arrivals, 0)

    delays = u_ref[...]
    beta0 = jnp.sqrt(total(delays * delays) + norm_epsilon)
    u0 = delays / beta0
    lane = lax.broadcasted_iota(jnp.int32, (nc, LANES), 1)

    def rays_of(j):
        return pl.ds(j, nc, stride=g) if g > 1 else pl.ds(0, nc)

    def spread_rays():
        ray = rr_ref[...]
        spread = jnp.zeros((nc, LANES), jnp.float32)
        for j in range(g):
            weights = u_ref[rays_of(j), :]
            mine = jnp.zeros((nc, LANES), jnp.float32)
            for r in range(rays):
                mine = jnp.where(ray == float(r), weights[:, r : r + 1], mine)
            spread = jnp.where(lane // ps == j, mine, spread)
        w_ref[:nc] = spread

        def weigh(cc, c):
            at = pl.ds(pl.multiple_of(cc * LANES, LANES), LANES)
            contrib[:, at] = two_parts(kt[:, at] * w_ref[pl.ds(cc, 1), :])
            return c

        lax.fori_loop(0, nc, weigh, 0, unroll=4)

    def plane_lanes(p):
        return pl.ds(pl.multiple_of(p * NY, NY), NY)

    def scatter_plane(p):
        both = lax.dot_general(
            contrib[...], s_mat[plane_lanes(p), :], (((1,), (1,)), ((), ())),
            preferred_element_type=jnp.float32,
        )
        return both[:cw] + both[cw:]

    def laplace(ref, p):
        x = ref[p, PAD : PAD + cw]
        row = lax.broadcasted_iota(jnp.int32, x.shape, 0) + e * cw
        col = lax.broadcasted_iota(jnp.int32, x.shape, 1)
        beside = ref[p + 1, PAD : PAD + cw] + ref[p - 1, PAD : PAD + cw]
        beside = beside + jnp.where(col < NY - 1, pltpu.roll(x, NY - 1, 1), 0.0)
        beside = beside + jnp.where(col > 0, pltpu.roll(x, 1, 1), 0.0)
        beside = beside + jnp.where(row < cw * ne - 1, ref[p, PAD + 1 : PAD + cw + 1], 0.0)
        beside = beside + jnp.where(row > 0, ref[p, PAD - 1 : PAD + cw - 1], 0.0)
        return 6.0 * x - beside

    def halo(ref, r):
        own, planes = pl.ds(PAD, cw), pl.ds(1, CX)
        moves = [
            (ref.at[CX, own], ref.at[0, own], (e, lax.rem(s + 1, n))),
            (ref.at[1, own], ref.at[CX + 1, own], (e, lax.rem(s - 1 + n, n))),
            (ref.at[planes, pl.ds(cw, PAD)], ref.at[planes, pl.ds(0, PAD)], (lax.rem(e + 1, ne), s)),
            (
                ref.at[planes, pl.ds(PAD, PAD)],
                ref.at[planes, pl.ds(PAD + cw, PAD)],
                (lax.rem(e - 1 + ne, ne), s),
            ),
        ]
        copies = [
            pltpu.make_async_remote_copy(
                src_ref=a, dst_ref=b, send_sem=halo_send.at[4 * r + i],
                recv_sem=halo_recv.at[4 * r + i], device_id=to, device_id_type=MESH,
            )
            for i, (a, b, to) in enumerate(moves)
        ]
        for copy in copies:
            copy.start()
        return copies

    def gather_parts(full, r):
        copies = [
            pltpu.make_async_remote_copy(
                src_ref=full.at[e], dst_ref=full.at[e], send_sem=full_send.at[ne * r + j],
                recv_sem=full_recv.at[r], device_id=(lax.rem(e + j, ne), s), device_id_type=MESH,
            )
            for j in range(1, ne)
        ]
        for copy in copies:
            copy.start()
        return copies

    def share(tiles, r):
        def start(k, c):
            other = lax.rem(me + k, nd)
            pltpu.make_async_remote_copy(
                src_ref=tiles.at[me], dst_ref=tiles.at[me], send_sem=bsend.at[r], recv_sem=brecv.at[r],
                device_id=(other // n, lax.rem(other, n)), device_id_type=MESH,
            ).start()
            return c

        lax.fori_loop(1, nd, start, 0)
        rest = tiles.at[pl.ds(0, nd - 1)]
        return pltpu.make_async_remote_copy(
            src_ref=rest, dst_ref=rest, send_sem=bsend.at[r], recv_sem=brecv.at[r],
            device_id=(e, s), device_id_type=MESH,
        )

    def share_square(tiles, square, r):
        tiles[me] = jnp.broadcast_to(square, (1, LANES))
        return share(tiles, r)

    def tile_sum(tiles):
        parts = [tiles[k] for k in range(nd)]
        while len(parts) > 1:
            parts = [a + b for a, b in zip(parts[::2], parts[1::2])]
        return parts[0]

    def square_sum(tiles):
        return tile_sum(tiles)[0:1, 0:1]

    def apply_rays(tiles):
        wide = 4 * LANES

        def block(b, c):
            at = pl.ds(pl.multiple_of(b * wide, wide), wide)
            picked = jnp.dot(table2[...], s_mat[:, at], preferred_element_type=jnp.float32)
            sums = jnp.sum((picked[:cw] + picked[cw:]) * kt[:, at], axis=0, keepdims=True)
            for i in range(4):
                e_ref[pl.ds(b * 4 + i, 1), :] = sums[:, i * LANES : (i + 1) * LANES]
            return c

        lax.fori_loop(0, nc // 4, block, 0)
        ray = rr_ref[...]
        for j in range(g):
            terms = jnp.where(lane // ps == j, e_ref[...], 0.0)
            value = jnp.zeros((nc, LANES), jnp.float32)
            for r in range(rays):
                one = jnp.sum(jnp.where(ray == float(r), terms, 0.0), axis=1, keepdims=True)
                value = jnp.where(lane == r, one, value)
            w_ref[rays_of(j), :] = value
        value = w_ref[:packed]
        for q in range(1, pack):
            value = value + pltpu.roll(w_ref[q * packed : (q + 1) * packed], q * rays, 1)
        tiles[me] = value

    def ray_sums(tiles):
        value = tile_sum(tiles)
        parts = [value] + [pltpu.roll(value, LANES - q * rays, 1) for q in range(1, pack)]
        value = jnp.concatenate(parts, axis=0)
        return jnp.where(lax.broadcasted_iota(jnp.int32, value.shape, 1) < rays, value, 0.0)

    def zero():
        return jnp.zeros((1, 1), jnp.float32)

    spread_rays()

    def first_plane(p, square):
        value = scatter_plane(p) / beta0
        d0[p + 1, PAD : PAD + cw] = value
        full0[e, p] = value
        table2[:, plane_lanes(p)] = two_parts(value)
        return square + total(value * value)

    square = lax.fori_loop(0, CX, first_plane, zero())
    halos0 = halo(d0, 0)
    square0 = share_square(q0, square, 2)
    apply_rays(y0)
    rays0 = share(y0, 0)
    gather0 = gather_parts(full0, 0)
    square0.wait_recv()
    alpha0 = jnp.sqrt(square_sum(q0) + norm_epsilon)

    for copy in halos0:
        copy.wait()

    def model_plane(p, square):
        value = damping * laplace(d0, p + 1) / alpha0
        m1[p + 1, PAD : PAD + cw] = value
        return square + total(value * value)

    square = lax.fori_loop(0, CX, model_plane, zero())
    square1 = share_square(q1, square, 3)
    halos1 = halo(m1, 1)
    rays0.wait_recv()
    u1 = ray_sums(y0) / alpha0 - alpha0 * u0
    u_ref[...] = u1
    ray_square = total(u1 * u1)
    spread_rays()
    square1.wait_recv()
    beta1 = jnp.sqrt(ray_square + square_sum(q1) + norm_epsilon)
    for copy in halos1:
        copy.wait()

    def next_plane(p, square):
        value = scatter_plane(p) / beta1 + damping * laplace(m1, p + 1) / beta1
        value = value - beta1 / alpha0 * d0[p + 1, PAD : PAD + cw]
        d1[p + 1, PAD : PAD + cw] = value
        full1[e, p] = value
        table2[:, plane_lanes(p)] = two_parts(value)
        return square + total(value * value)

    square = lax.fori_loop(0, CX, next_plane, zero())
    halos2 = halo(d1, 2)
    square2 = share_square(q2, square, 4)
    apply_rays(y1)
    rays1 = share(y1, 1)
    gather1 = gather_parts(full1, 1)
    rho1 = jnp.sqrt(alpha0 * alpha0 + beta1 * beta1)
    cosine1 = alpha0 / rho1
    sine1 = beta1 / rho1
    phi1 = cosine1 * beta0
    phi_bar = sine1 * beta0
    square2.wait_recv()
    alpha1 = jnp.sqrt(square_sum(q2) + norm_epsilon)
    theta1 = sine1 * alpha1
    rho_bar = -cosine1 * alpha1

    for copy in halos2:
        copy.wait()

    def last_plane(p, square):
        value = damping * laplace(d1, p + 1) / alpha1
        value = value - alpha1 / beta1 * m1[p + 1, PAD : PAD + cw]
        return square + total(value * value)

    square = lax.fori_loop(0, CX, last_plane, zero())
    square3 = share_square(q3, square, 5)
    rays1.wait_recv()
    u2 = ray_sums(y1) / alpha1 - alpha1 * (u1 / beta1)
    ray_square = total(u2 * u2)

    def gathered(full, r):
        rest = full.at[pl.ds(0, ne - 1)]
        pltpu.make_async_remote_copy(
            src_ref=rest, dst_ref=rest, send_sem=full_send.at[ne * r], recv_sem=full_recv.at[r],
            device_id=(e, s), device_id_type=MESH,
        ).wait_recv()

    gathered(full0, 0)
    gathered(full1, 1)
    square3.wait_recv()
    beta2 = jnp.sqrt(ray_square + square_sum(q3) + norm_epsilon)
    rho2 = jnp.sqrt(rho_bar * rho_bar + beta2 * beta2)
    phi2 = rho_bar / rho2 * phi_bar

    def finish(p, c):
        first = jnp.concatenate([full0[i, p] for i in range(ne)], axis=0) / alpha0
        second = jnp.concatenate([full1[i, p] for i in range(ne)], axis=0) / alpha1
        search = second - theta1 / rho1 * first
        out_ref[p] = (phi1 / rho1 * first + phi2 / rho2 * search).T
        return c

    lax.fori_loop(0, CX, finish, 0)

    def sent(k, c):
        rows_to(lax.rem(me + k, nd)).wait_send()
        return c

    lax.fori_loop(1, nd, sent, 0)
    for copy in gather0 + gather1 + [rays0, rays1, square0, square1, square2, square3]:
        copy.wait_send()


def solution(mesh):
    ne, n = mesh.shape["ev"], mesh.shape["slab"]

    def on_device(kernels, block_ids, delays):
        rays, per_ray, width = kernels.shape
        entries = rays * per_ray
        ps = entries // n
        nd = ne * n
        cw = width // ne
        rows = nd * ps
        cells = CX * NY
        flat = block_ids.reshape(1, entries)
        ray = lax.broadcasted_iota(jnp.int32, (1, entries), 1) // per_ray
        rest = jnp.zeros((4, entries), jnp.int32)
        meta = jnp.concatenate(
            [flat % cells // NY, flat % NY, ray, flat // cells, rest], axis=0
        ).astype(jnp.float32)
        delay_row = jnp.pad(delays.reshape(1, rays), ((0, 0), (0, LANES - rays)))
        f32, bf16 = jnp.float32, jnp.bfloat16
        vmem = pl.BlockSpec(memory_space=pltpu.VMEM)
        model = pltpu.VMEM((CX + 2, cw + 2 * PAD, NY), f32)
        full = pltpu.VMEM((ne, CX, cw, NY), f32)
        tiles = pltpu.VMEM((nd, nd * rays // LANES, LANES), f32)
        scalar = pltpu.VMEM((nd, 1, LANES), f32)
        small = pltpu.VMEM((rows // LANES, LANES), f32)
        by_device = pltpu.VMEM((nd, LANES), f32)
        return pl.pallas_call(
            functools.partial(kernel, ne, n, ps, rays, cw),
            out_shape=jax.ShapeDtypeStruct((CX, NY, width), f32),
            in_specs=[vmem] * 3,
            out_specs=vmem,
            scratch_shapes=[
                pltpu.VMEM((nd, cw + 8, LANES), f32),
                pltpu.VMEM((nd, cw + 8, LANES), f32),
                pltpu.VMEM((entries, 3 * width), bf16),
                pltpu.VMEM((cells, rows), bf16),
                pltpu.VMEM((2 * cw, rows), bf16),
                pltpu.VMEM((cw, rows), f32),
                pltpu.VMEM((2 * cw, cells), bf16),
                small,
                by_device,
                small,
                by_device,
                model, model, model, full, full,
                tiles, tiles, scalar, scalar, scalar, scalar,
                pltpu.SemaphoreType.DMA((nd,)),
                pltpu.SemaphoreType.DMA((nd,)),
                pltpu.SemaphoreType.DMA((12,)),
                pltpu.SemaphoreType.DMA((12,)),
                pltpu.SemaphoreType.DMA((2 * ne,)),
                pltpu.SemaphoreType.DMA((2,)),
                pltpu.SemaphoreType.DMA((6,)),
                pltpu.SemaphoreType.DMA((6,)),
            ],
            compiler_params=pltpu.CompilerParams(
                collective_id=0, has_side_effects=True, vmem_limit_bytes=60 * 1024 * 1024
            ),
        )(kernels.reshape(entries, width), meta, delay_row)

    in_specs = (P(("ev", "slab"), None, None), P(("ev", "slab"), None), P(("ev", "slab")))
    return jax.shard_map(
        on_device, mesh=mesh, in_specs=in_specs, out_specs=P("slab", None, None), check_vma=False
    )
```

```python
import functools

import jax
import jax.numpy as jnp
from jax import lax
from jax.experimental import pallas as pl
from jax.experimental.pallas import tpu as pltpu
from jax.sharding import PartitionSpec as P

CX = 8
NY = 128
LANES = 128
MESH = pl.DeviceIdType.MESH

damping = 0.3
norm_epsilon = 1e-06


def iota(shape, dim):
    return lax.broadcasted_iota(jnp.int32, shape, dim).astype(jnp.float32)


def total(x):
    return jnp.sum(jnp.sum(x, axis=0, keepdims=True), axis=1, keepdims=True)


def one_hot(mask):
    return jnp.where(mask, 1.0, 0.0).astype(jnp.bfloat16)


def two_parts(x):
    high = x.astype(jnp.bfloat16)
    low = (x - high.astype(jnp.float32)).astype(jnp.bfloat16)
    return jnp.concatenate([high, low], axis=0)


PAD = 8


def kernel(
    ne, n, ps, rays, cw,
    kern_ref, ids_ref, delay_ref, out_ref,
    send, recv, pieces, s_mat, contrib, kt, table2, acc, rr_ref, w_ref, e_ref, u_ref,
    ids_wide, delay_wide, d0, m1, d1, full0, full1, y0, y1, q0, q1,
    ssem, rsem, halo_send, halo_recv, full_send, full_recv, bsend, brecv,
):
    nd = ne * n
    g = LANES // ps
    cpg = n // g
    nc = nd // g
    entries = n * ps
    cells = CX * NY
    pack = LANES // rays
    packed = nd // pack
    e = lax.axis_index("ev")
    s = lax.axis_index("slab")
    me = e * n + s

    barrier = pltpu.get_barrier_semaphore()

    def each_other(act):
        if nd <= 32:
            for k in range(1, nd):
                act(lax.rem(me + k, nd))
        else:

            def step(k, c):
                act(lax.rem(me + k, nd))
                return c

            lax.fori_loop(1, nd, step, 0)

    def place(device):
        return (device // n, lax.rem(device, n))

    each_other(
        lambda other: pl.semaphore_signal(
            barrier, inc=1, device_id=place(other), device_id_type=MESH
        )
    )

    per_ray = ids_ref.shape[1]
    some = LANES // per_ray
    ids_wide[...] = jnp.zeros_like(ids_wide)
    ids_wide[:, :per_ray] = ids_ref[...].astype(jnp.float32)
    delay_wide[...] = jnp.zeros_like(delay_wide)
    delay_wide[:, :rays] = delay_ref[...]
    wide_ids = ids_wide[...]
    ray_index = lax.broadcasted_iota(jnp.int32, wide_ids.shape, 0)
    moved = wide_ids
    for i in range(1, some):
        moved = jnp.where(ray_index % some == i, pltpu.roll(wide_ids, i * per_ray, 1), moved)
    tiles_own = entries // LANES
    id_rows = [
        jnp.sum(moved[q * some : (q + 1) * some], axis=0, keepdims=True) for q in range(tiles_own)
    ]

    earlier = one_hot(iota((LANES, LANES), 0) < iota((LANES, LANES), 1))
    taken = jnp.zeros((n, 1), jnp.float32)
    positions = []
    for q, ids in enumerate(id_rows):
        at = slice(q * LANES, (q + 1) * LANES)
        slab_row = jnp.floor(ids * (1.0 / cells))
        inside = ids - slab_row * cells
        row_i = jnp.floor(inside * (1.0 / NY))
        owner = slab_row == iota((n, LANES), 0)
        counts = jnp.dot(one_hot(owner), earlier, preferred_element_type=jnp.float32) + taken
        rank = jnp.sum(jnp.where(owner, counts, 0.0), axis=0, keepdims=True)
        taken = taken + jnp.sum(jnp.where(owner, 1.0, 0.0), axis=1, keepdims=True)
        positions.append(slab_row * ps + rank)
        ray_row = jnp.floor(iota((1, LANES), 1) * (1.0 / per_ray)) + float(q * some)
        kind = iota((2 * PAD, LANES), 0)
        facts = jnp.where(kind == 0.0, row_i, 0.0)
        facts = jnp.where(kind == 1.0, inside - row_i * NY, facts)
        facts = jnp.where(kind == 2.0, ray_row, facts)
        pieces[: 2 * LANES, at] = two_parts(kern_ref[at, :].T)
        pieces[2 * LANES :, at] = facts.astype(jnp.bfloat16)
    position = jnp.concatenate(positions, axis=1)
    acc[...] = jnp.zeros_like(acc)
    pl.semaphore_wait(barrier, nd - 1)

    def rows_to(dest):
        return pltpu.make_async_remote_copy(
            src_ref=send.at[dest], dst_ref=recv.at[me], send_sem=ssem.at[0], recv_sem=rsem.at[me],
            device_id=place(dest), device_id_type=MESH,
        )

    def sort_tile(k, c):
        t = lax.rem(s // g + cpg // 2 + k, cpg)
        pm = one_hot(iota((LANES, entries), 0) + (t * LANES).astype(jnp.float32) == position)
        both = lax.dot_general(
            pieces[...], pm, (((1,), (1,)), ((), ())), preferred_element_type=jnp.float32
        )
        rows = both[:LANES] + both[LANES : 2 * LANES]
        tile = both[2 * LANES : 2 * LANES + PAD]
        for j in range(g):
            part = tile if j == 0 else pltpu.roll(tile, LANES - j * ps, 1)
            part = jnp.where(iota(part.shape, 0) == 3.0, delay_wide[...], part)
            block = rows if j == 0 else pltpu.roll(rows, LANES - j * ps, 1)
            for i in range(ne):
                dest = i * n + t * g + j
                send[dest, :cw] = block[i * cw : (i + 1) * cw]
                send[dest, cw:] = part

                @pl.when(dest != me)
                def _():
                    rows_to(dest).start()

        return c

    lax.fori_loop(0, cpg, sort_tile, 0)
    recv[me] = send[me]

    def chunk(cc):
        delay_rows = []
        for j in range(g):
            slot = cc * g + j

            @pl.when(slot != me)
            def _():
                pltpu.make_async_remote_copy(
                    src_ref=recv.at[slot], dst_ref=recv.at[slot], send_sem=ssem.at[0],
                    recv_sem=rsem.at[slot], device_id=(e, s), device_id_type=MESH,
                ).wait_recv()

            delay_rows.append(recv[slot, cw + 3 : cw + 4])
            u_ref[pl.ds(slot, 1), :] = delay_rows[-1]
        block = recv[cc * g]
        for j in range(1, g):
            here = (lax.broadcasted_iota(jnp.int32, block.shape, 1) // ps) == j
            block = jnp.where(here, pltpu.roll(recv[cc * g + j], j * ps, 1), block)
        first = pl.multiple_of(cc * LANES, LANES)
        kt[:, pl.ds(first, LANES)] = block[:cw]
        rr_ref[pl.ds(cc, 1), :] = block[cw + 2 : cw + 3]
        cell = block[cw : cw + 1] * NY + block[cw + 1 : cw + 2]
        s_mat[:, pl.ds(first, LANES)] = one_hot(iota((cells, LANES), 0) == cell)

        return block[cw + 2 : cw + 3], delay_rows

    def spread(ray, weights):
        lane = lax.broadcasted_iota(jnp.int32, ray.shape, 1)
        result = jnp.zeros(ray.shape, jnp.float32)
        for j in range(g):
            mine = jnp.zeros(ray.shape, jnp.float32)
            for r in range(rays):
                mine = jnp.where(ray == float(r), weights[j][:, r : r + 1], mine)
            result = jnp.where(lane // ps == j, mine, result)
        return result

    def arrivals(k, c):
        inner = lax.rem(s // g - cpg // 2 - k + 2 * cpg, cpg)
        chunks = [lax.rem(e + j, ne) * cpg + inner for j in range(ne)]
        found = [chunk(cc) for cc in chunks]
        ray = jnp.concatenate([f[0] for f in found], axis=0)
        weights = [jnp.concatenate([f[1][j] for f in found], axis=0) for j in range(g)]
        w = spread(ray, weights)
        for j, cc in enumerate(chunks):
            at = pl.ds(pl.multiple_of(cc * LANES, LANES), LANES)
            acc[...] += lax.dot_general(
                two_parts(kt[:, at] * w[j : j + 1]), s_mat[:, at], (((1,), (1,)), ((), ())),
                preferred_element_type=jnp.float32,
            )
        return c

    lax.fori_loop(0, cpg, arrivals, 0)

    delays = u_ref[...]
    beta0 = jnp.sqrt(total(delays * delays) + norm_epsilon)
    u0 = delays / beta0
    lane = lax.broadcasted_iota(jnp.int32, (nc, LANES), 1)

    def rays_of(j):
        return pl.ds(j, nc, stride=g) if g > 1 else pl.ds(0, nc)

    def spread_rays():
        w_ref[:nc] = spread(rr_ref[...], [u_ref[rays_of(j), :] for j in range(g)])

        def weigh(cc, c):
            at = pl.ds(pl.multiple_of(cc * LANES, LANES), LANES)
            contrib[:, at] = two_parts(kt[:, at] * w_ref[pl.ds(cc, 1), :])
            return c

        lax.fori_loop(0, nc, weigh, 0, unroll=4)

    def plane_lanes(p):
        return pl.ds(pl.multiple_of(p * NY, NY), NY)

    def scatter(p, c):
        acc[:, plane_lanes(p)] = lax.dot_general(
            contrib[...], s_mat[plane_lanes(p), :], (((1,), (1,)), ((), ())),
            preferred_element_type=jnp.float32,
        )
        return c

    def scattered(p):
        at = slice(p * NY, (p + 1) * NY)
        return acc[:cw, at] + acc[cw:, at]

    def laplace(ref, p):
        x = ref[p, PAD : PAD + cw]
        row = lax.broadcasted_iota(jnp.int32, x.shape, 0) + e * cw
        col = lax.broadcasted_iota(jnp.int32, x.shape, 1)
        beside = ref[p + 1, PAD : PAD + cw] + ref[p - 1, PAD : PAD + cw]
        beside = beside + jnp.where(col < NY - 1, pltpu.roll(x, NY - 1, 1), 0.0)
        beside = beside + jnp.where(col > 0, pltpu.roll(x, 1, 1), 0.0)
        beside = beside + jnp.where(row < cw * ne - 1, ref[p, PAD + 1 : PAD + cw + 1], 0.0)
        beside = beside + jnp.where(row > 0, ref[p, PAD - 1 : PAD + cw - 1], 0.0)
        return 6.0 * x - beside

    def halo(ref, r):
        own, planes = pl.ds(PAD, cw), pl.ds(1, CX)
        moves = [
            (ref.at[CX, own], ref.at[0, own], (e, lax.rem(s + 1, n))),
            (ref.at[1, own], ref.at[CX + 1, own], (e, lax.rem(s - 1 + n, n))),
            (ref.at[planes, pl.ds(cw, PAD)], ref.at[planes, pl.ds(0, PAD)], (lax.rem(e + 1, ne), s)),
            (
                ref.at[planes, pl.ds(PAD, PAD)],
                ref.at[planes, pl.ds(PAD + cw, PAD)],
                (lax.rem(e - 1 + ne, ne), s),
            ),
        ]
        copies = [
            pltpu.make_async_remote_copy(
                src_ref=a, dst_ref=b, send_sem=halo_send.at[4 * r + i],
                recv_sem=halo_recv.at[4 * r + i], device_id=to, device_id_type=MESH,
            )
            for i, (a, b, to) in enumerate(moves)
        ]
        for copy in copies:
            copy.start()
        return copies

    def gather_parts(full, r):
        copies = [
            pltpu.make_async_remote_copy(
                src_ref=full.at[e], dst_ref=full.at[e], send_sem=full_send.at[ne * r + j],
                recv_sem=full_recv.at[r], device_id=(lax.rem(e + j, ne), s), device_id_type=MESH,
            )
            for j in range(1, ne)
        ]
        for copy in copies:
            copy.start()
        return copies

    def share(tiles, numbers, squares, r):
        lane = lax.broadcasted_iota(jnp.int32, (1, LANES), 1)
        row = jnp.zeros((1, LANES), jnp.float32)
        for i, square in enumerate(squares):
            row = jnp.where(lane == i, square, row)
        numbers[me] = row

        def act(other):
            for i, ref in enumerate((tiles, numbers)):
                pltpu.make_async_remote_copy(
                    src_ref=ref.at[me], dst_ref=ref.at[me], send_sem=bsend.at[2 * r + i],
                    recv_sem=brecv.at[2 * r + i], device_id=place(other), device_id_type=MESH,
                ).start()

        each_other(act)
        done = []
        for i, ref in enumerate((tiles, numbers)):
            rest = ref.at[pl.ds(0, nd - 1)]
            done.append(
                pltpu.make_async_remote_copy(
                    src_ref=rest, dst_ref=rest, send_sem=bsend.at[2 * r + i],
                    recv_sem=brecv.at[2 * r + i], device_id=(e, s), device_id_type=MESH,
                )
            )
        return done

    def tile_sum(tiles):
        parts = [tiles[k] for k in range(nd)]
        while len(parts) > 1:
            parts = [a + b for a, b in zip(parts[::2], parts[1::2])]
        return parts[0]

    def apply_rays(tiles):
        wide = 4 * LANES

        def block(b, c):
            at = pl.ds(pl.multiple_of(b * wide, wide), wide)
            picked = jnp.dot(table2[...], s_mat[:, at], preferred_element_type=jnp.float32)
            sums = jnp.sum((picked[:cw] + picked[cw:]) * kt[:, at], axis=0, keepdims=True)
            for i in range(4):
                e_ref[pl.ds(b * 4 + i, 1), :] = sums[:, i * LANES : (i + 1) * LANES]
            return c

        lax.fori_loop(0, nc // 4, block, 0)
        ray = rr_ref[...]
        for j in range(g):
            terms = jnp.where(lane // ps == j, e_ref[...], 0.0)
            value = jnp.zeros((nc, LANES), jnp.float32)
            for r in range(rays):
                one = jnp.sum(jnp.where(ray == float(r), terms, 0.0), axis=1, keepdims=True)
                value = jnp.where(lane == r, one, value)
            w_ref[rays_of(j), :] = value
        value = w_ref[:packed]
        for q in range(1, pack):
            value = value + pltpu.roll(w_ref[q * packed : (q + 1) * packed], q * rays, 1)
        tiles[me] = value

    def ray_sums(tiles):
        value = tile_sum(tiles)
        parts = [value] + [pltpu.roll(value, LANES - q * rays, 1) for q in range(1, pack)]
        value = jnp.concatenate(parts, axis=0)
        return jnp.where(lax.broadcasted_iota(jnp.int32, value.shape, 1) < rays, value, 0.0)

    def nothing():
        return jnp.zeros((cw, NY), jnp.float32)

    square = nothing()
    for p in range(CX):
        value = scattered(p) / beta0
        d0[p + 1, PAD : PAD + cw] = value
        full0[e, p] = value
        table2[:, p * NY : (p + 1) * NY] = two_parts(value)
        square = square + value * value
    halos0 = halo(d0, 0)
    apply_rays(y0)
    for copy in halos0:
        copy.wait()
    curved = nothing()
    for p in range(CX):
        value = laplace(d0, p + 1)
        m1[p + 1, PAD : PAD + cw] = value
        curved = curved + value * value
    shared0 = share(y0, q0, [total(square), total(curved)], 0)
    halos1 = halo(m1, 1)
    gather0 = gather_parts(full0, 0)
    for copy in shared0:
        copy.wait_recv()
    numbers = tile_sum(q0)
    alpha0 = jnp.sqrt(numbers[:, 0:1] + norm_epsilon)
    curved0 = numbers[:, 1:2]

    u1 = ray_sums(y0) / alpha0 - alpha0 * u0
    u_ref[...] = u1
    model_square = damping * damping * (curved0 / (alpha0 * alpha0))
    beta1 = jnp.sqrt(total(u1 * u1) + model_square + norm_epsilon)
    scale1 = damping / alpha0 / beta1
    spread_rays()
    lax.fori_loop(0, CX, scatter, 0)
    for copy in halos1:
        copy.wait()
    square = nothing()
    for p in range(CX):
        value = scattered(p) / beta1 + damping * scale1 * laplace(m1, p + 1)
        value = value - beta1 / alpha0 * d0[p + 1, PAD : PAD + cw]
        d1[p + 1, PAD : PAD + cw] = value
        full1[e, p] = value
        table2[:, p * NY : (p + 1) * NY] = two_parts(value)
        square = square + value * value
    halos2 = halo(d1, 2)
    apply_rays(y1)
    for copy in halos2:
        copy.wait()
    curved = nothing()
    cross = nothing()
    for p in range(CX):
        value = laplace(d1, p + 1)
        curved = curved + value * value
        cross = cross + value * m1[p + 1, PAD : PAD + cw]
    shared1 = share(y1, q1, [total(square), total(curved), total(cross)], 1)
    gather1 = gather_parts(full1, 1)
    rho1 = jnp.sqrt(alpha0 * alpha0 + beta1 * beta1)
    cosine1 = alpha0 / rho1
    sine1 = beta1 / rho1
    phi1 = cosine1 * beta0
    phi_bar = sine1 * beta0
    for copy in shared1:
        copy.wait_recv()
    numbers = tile_sum(q1)
    alpha1 = jnp.sqrt(numbers[:, 0:1] + norm_epsilon)
    theta1 = sine1 * alpha1
    rho_bar = -cosine1 * alpha1

    u2 = ray_sums(y1) / alpha1 - alpha1 * (u1 / beta1)
    a, b = damping / alpha1, alpha1 * scale1
    model_square = a * a * numbers[:, 1:2] - 2.0 * a * b * numbers[:, 2:3] + b * b * curved0
    model_square = jnp.maximum(model_square, 0.0)
    beta2 = jnp.sqrt(total(u2 * u2) + model_square + norm_epsilon)
    rho2 = jnp.sqrt(rho_bar * rho_bar + beta2 * beta2)
    phi2 = rho_bar / rho2 * phi_bar

    for r, full in enumerate((full0, full1)):
        rest = full.at[pl.ds(0, ne - 1)]
        pltpu.make_async_remote_copy(
            src_ref=rest, dst_ref=rest, send_sem=full_send.at[ne * r], recv_sem=full_recv.at[r],
            device_id=(e, s), device_id_type=MESH,
        ).wait_recv()

    def finish(p, c):
        for i in range(ne):
            first = full0[i, p] / alpha0
            search = full1[i, p] / alpha1 - theta1 / rho1 * first
            out_ref[p, i * cw : (i + 1) * cw] = phi1 / rho1 * first + phi2 / rho2 * search
        return c

    lax.fori_loop(0, CX, finish, 0)

    rest = send.at[pl.ds(0, nd - 1)]
    pltpu.make_async_remote_copy(
        src_ref=rest, dst_ref=rest, send_sem=ssem.at[0], recv_sem=rsem.at[0],
        device_id=(e, s), device_id_type=MESH,
    ).wait_send()
    for copy in gather0 + gather1 + shared0 + shared1:
        copy.wait_send()


def solution(mesh):
    ne, n = mesh.shape["ev"], mesh.shape["slab"]

    def on_device(kernels, block_ids, delays):
        rays, per_ray, width = kernels.shape
        entries = rays * per_ray
        ps = entries // n
        nd = ne * n
        cw = width // ne
        rows = nd * ps
        cells = CX * NY
        f32, bf16 = jnp.float32, jnp.bfloat16
        vmem = pl.BlockSpec(memory_space=pltpu.VMEM)
        model = pltpu.VMEM((CX + 2, cw + 2 * PAD, NY), f32)
        full = pltpu.VMEM((ne, CX, cw, NY), f32)
        tiles = pltpu.VMEM((nd, nd * rays // LANES, LANES), f32)
        scalar = pltpu.VMEM((nd, 1, LANES), f32)
        small = pltpu.VMEM((rows // LANES, LANES), f32)
        by_device = pltpu.VMEM((nd, LANES), f32)
        result = pl.pallas_call(
            functools.partial(kernel, ne, n, ps, rays, cw),
            out_shape=jax.ShapeDtypeStruct((CX, width, NY), f32),
            in_specs=[vmem] * 3,
            out_specs=vmem,
            scratch_shapes=[
                pltpu.VMEM((nd, cw + 8, LANES), f32),
                pltpu.VMEM((nd, cw + 8, LANES), f32),
                pltpu.VMEM((2 * width + 2 * PAD, entries), bf16),
                pltpu.VMEM((cells, rows), bf16),
                pltpu.VMEM((2 * cw, rows), bf16),
                pltpu.VMEM((cw, rows), f32),
                pltpu.VMEM((2 * cw, cells), bf16),
                pltpu.VMEM((2 * cw, cells), f32),
                small,
                by_device,
                small,
                by_device,
                pltpu.VMEM((rays, LANES), f32),
                pltpu.VMEM((1, LANES), f32),
                model, model, model, full, full, tiles, tiles, scalar, scalar,
                pltpu.SemaphoreType.DMA((1,)),
                pltpu.SemaphoreType.DMA((nd,)),
                pltpu.SemaphoreType.DMA((12,)),
                pltpu.SemaphoreType.DMA((12,)),
                pltpu.SemaphoreType.DMA((2 * ne,)),
                pltpu.SemaphoreType.DMA((2,)),
                pltpu.SemaphoreType.DMA((4,)),
                pltpu.SemaphoreType.DMA((4,)),
            ],
            compiler_params=pltpu.CompilerParams(
                collective_id=0, has_side_effects=True, vmem_limit_bytes=60 * 1024 * 1024
            ),
        )(kernels.reshape(entries, width), block_ids, delays.reshape(1, rays))
        return jnp.swapaxes(result, 1, 2)

    in_specs = (P(("ev", "slab"), None, None), P(("ev", "slab"), None), P(("ev", "slab")))
    return jax.shard_map(
        on_device, mesh=mesh, in_specs=in_specs, out_specs=P("slab", None, None), check_vma=False
    )
```

```python
import functools

import jax
import jax.numpy as jnp
from jax import lax
from jax.experimental import pallas as pl
from jax.experimental.pallas import tpu as pltpu
from jax.sharding import PartitionSpec as P

CX = 8
NY = 128
LANES = 128
MESH = pl.DeviceIdType.MESH

damping = 0.3
norm_epsilon = 1e-06


def iota(shape, dim):
    return lax.broadcasted_iota(jnp.int32, shape, dim).astype(jnp.float32)


def total(x):
    return jnp.sum(jnp.sum(x, axis=0, keepdims=True), axis=1, keepdims=True)


def one_hot(mask):
    return jnp.where(mask, 1.0, 0.0).astype(jnp.bfloat16)


def two_parts(x):
    high = x.astype(jnp.bfloat16)
    low = (x - high.astype(jnp.float32)).astype(jnp.bfloat16)
    return jnp.concatenate([high, low], axis=0)


PAD = 8


def kernel(
    ne, n, ps, rays, cw,
    kern_ref, ids_ref, delay_ref, out_ref,
    kern_rows, send, recv, pieces, s_mat, kt, plane_ref, table2, acc, rr_ref, w_ref, e_ref, u_ref,
    ids_wide, delay_wide, d0, m1, d1, full0, full1, y0, y1, q0, q1,
    ssem, rsem, halo_send, halo_recv, full_send, full_recv, bsend, brecv, load_sem,
):
    nd = ne * n
    g = LANES // ps
    cpg = n // g
    nc = nd // g
    entries = n * ps
    cells = CX * NY
    pack = LANES // rays
    packed = nd // pack
    e = lax.axis_index("ev")
    s = lax.axis_index("slab")
    me = e * n + s

    load = pltpu.make_async_copy(kern_ref, kern_rows, load_sem)
    load.start()
    barrier = pltpu.get_barrier_semaphore()

    def each_other(act):
        if nd <= 32:
            for k in range(1, nd):
                act(lax.rem(me + k, nd))
        else:

            def step(k, c):
                act(lax.rem(me + k, nd))
                return c

            lax.fori_loop(1, nd, step, 0)

    def place(device):
        return (device // n, lax.rem(device, n))

    each_other(
        lambda other: pl.semaphore_signal(
            barrier, inc=1, device_id=place(other), device_id_type=MESH
        )
    )

    per_ray = ids_ref.shape[1]
    some = LANES // per_ray
    ids_wide[...] = jnp.zeros_like(ids_wide)
    ids_wide[:, :per_ray] = ids_ref[...].astype(jnp.float32)
    delay_wide[...] = jnp.zeros_like(delay_wide)
    delay_wide[:, :rays] = delay_ref[...]
    wide_ids = ids_wide[...]
    ray_index = lax.broadcasted_iota(jnp.int32, wide_ids.shape, 0)
    moved = wide_ids
    for i in range(1, some):
        moved = jnp.where(ray_index % some == i, pltpu.roll(wide_ids, i * per_ray, 1), moved)
    tiles_own = entries // LANES
    id_rows = [
        jnp.sum(moved[q * some : (q + 1) * some], axis=0, keepdims=True) for q in range(tiles_own)
    ]

    earlier = one_hot(iota((LANES, LANES), 0) < iota((LANES, LANES), 1))
    taken = jnp.zeros((n, 1), jnp.float32)
    positions = []
    load.wait()
    for q, ids in enumerate(id_rows):
        at = slice(q * LANES, (q + 1) * LANES)
        slab_row = jnp.floor(ids * (1.0 / cells))
        inside = ids - slab_row * cells
        row_i = jnp.floor(inside * (1.0 / NY))
        owner = slab_row == iota((n, LANES), 0)
        counts = jnp.dot(one_hot(owner), earlier, preferred_element_type=jnp.float32) + taken
        rank = jnp.sum(jnp.where(owner, counts, 0.0), axis=0, keepdims=True)
        taken = taken + jnp.sum(jnp.where(owner, 1.0, 0.0), axis=1, keepdims=True)
        positions.append(slab_row * ps + rank)
        ray_row = jnp.floor(iota((1, LANES), 1) * (1.0 / per_ray)) + float(q * some)
        kind = iota((2 * PAD, LANES), 0)
        facts = jnp.where(kind == 0.0, row_i, 0.0)
        facts = jnp.where(kind == 1.0, inside - row_i * NY, facts)
        facts = jnp.where(kind == 2.0, ray_row, facts)
        pieces[: 2 * LANES, at] = two_parts(kern_rows[at, :].T)
        pieces[2 * LANES :, at] = facts.astype(jnp.bfloat16)
    position = jnp.concatenate(positions, axis=1)
    acc[...] = jnp.zeros_like(acc)
    pl.semaphore_wait(barrier, nd - 1)

    def rows_to(dest):
        return pltpu.make_async_remote_copy(
            src_ref=send.at[dest], dst_ref=recv.at[me], send_sem=ssem.at[0], recv_sem=rsem.at[me],
            device_id=place(dest), device_id_type=MESH,
        )

    def sort_tile(k, c):
        t = lax.rem(s // g + cpg // 2 + k, cpg)
        pm = one_hot(iota((LANES, entries), 0) + (t * LANES).astype(jnp.float32) == position)
        both = lax.dot_general(
            pieces[...], pm, (((1,), (1,)), ((), ())), preferred_element_type=jnp.float32
        )
        rows = both[:LANES] + both[LANES : 2 * LANES]
        tile = both[2 * LANES : 2 * LANES + PAD]
        for j in range(g):
            part = tile if j == 0 else pltpu.roll(tile, LANES - j * ps, 1)
            part = jnp.where(iota(part.shape, 0) == 3.0, delay_wide[...], part)
            block = rows if j == 0 else pltpu.roll(rows, LANES - j * ps, 1)
            for i in range(ne):
                dest = i * n + t * g + j
                send[dest, :cw] = block[i * cw : (i + 1) * cw]
                send[dest, cw:] = part

                @pl.when(dest != me)
                def _():
                    rows_to(dest).start()

        return c

    lax.fori_loop(0, cpg, sort_tile, 0)
    recv[me] = send[me]

    def chunk(cc):
        delay_rows = []
        for j in range(g):
            slot = cc * g + j

            @pl.when(slot != me)
            def _():
                pltpu.make_async_remote_copy(
                    src_ref=recv.at[slot], dst_ref=recv.at[slot], send_sem=ssem.at[0],
                    recv_sem=rsem.at[slot], device_id=(e, s), device_id_type=MESH,
                ).wait_recv()

            delay_rows.append(recv[slot, cw + 3 : cw + 4])
            u_ref[pl.ds(slot, 1), :] = delay_rows[-1]
        block = recv[cc * g]
        for j in range(1, g):
            here = (lax.broadcasted_iota(jnp.int32, block.shape, 1) // ps) == j
            block = jnp.where(here, pltpu.roll(recv[cc * g + j], j * ps, 1), block)
        first = pl.multiple_of(cc * LANES, LANES)
        kt[:, pl.ds(first, LANES)] = block[:cw]
        plane_ref[:, pl.ds(first, LANES)] = block[cw : cw + 1]
        rr_ref[pl.ds(cc, 1), :] = block[cw + 2 : cw + 3]
        hot = one_hot(iota((NY, LANES), 0) == block[cw + 1 : cw + 2])
        s_mat[:, pl.ds(first, LANES)] = hot
        return block[cw + 2 : cw + 3], delay_rows, hot, block

    def by_plane(rows, plane):
        high = rows.astype(jnp.bfloat16).astype(jnp.float32)
        both = jnp.concatenate([high, rows - high], axis=0)
        return jnp.concatenate(
            [jnp.where(plane == float(i), both, 0.0).astype(jnp.bfloat16) for i in range(CX)], axis=0
        )

    def add_rows(terms, hot):
        acc[...] += lax.dot_general(
            terms, hot, (((1,), (1,)), ((), ())), preferred_element_type=jnp.float32
        )

    def spread(ray, weights):
        lane = lax.broadcasted_iota(jnp.int32, ray.shape, 1)
        result = jnp.zeros(ray.shape, jnp.float32)
        for j in range(g):
            mine = jnp.zeros(ray.shape, jnp.float32)
            for r in range(rays):
                mine = jnp.where(ray == float(r), weights[j][:, r : r + 1], mine)
            result = jnp.where(lane // ps == j, mine, result)
        return result

    def arrivals(k, c):
        inner = lax.rem(s // g - cpg // 2 - k + 2 * cpg, cpg)
        chunks = [lax.rem(e + j, ne) * cpg + inner for j in range(ne)]
        found = [chunk(cc) for cc in chunks]
        ray = jnp.concatenate([f[0] for f in found], axis=0)
        weights = [jnp.concatenate([f[1][j] for f in found], axis=0) for j in range(g)]
        w = spread(ray, weights)
        terms = [
            by_plane(f[3][:cw] * w[j : j + 1], f[3][cw : cw + 1]) for j, f in enumerate(found)
        ]
        add_rows(jnp.concatenate(terms, axis=1), jnp.concatenate([f[2] for f in found], axis=1))
        return c

    lax.fori_loop(0, cpg, arrivals, 0)

    delays = u_ref[...]
    beta0 = jnp.sqrt(total(delays * delays) + norm_epsilon)
    u0 = delays / beta0
    lane = lax.broadcasted_iota(jnp.int32, (nc, LANES), 1)

    def rays_of(j):
        return pl.ds(j, nc, stride=g) if g > 1 else pl.ds(0, nc)

    wide = 4 * LANES

    def scatter_rays():
        w_ref[:nc] = spread(rr_ref[...], [u_ref[rays_of(j), :] for j in range(g)])
        acc[...] = jnp.zeros_like(acc)

        def block(b, c):
            at = pl.ds(pl.multiple_of(b * wide, wide), wide)
            w = jnp.concatenate([w_ref[pl.ds(b * 4 + i, 1), :] for i in range(4)], axis=1)
            add_rows(by_plane(kt[:, at] * w, plane_ref[:, at]), s_mat[:, at])
            return c

        lax.fori_loop(0, nc // 4, block, 0)

    def scattered(p):
        return acc[2 * cw * p : 2 * cw * p + cw] + acc[2 * cw * p + cw : 2 * cw * (p + 1)]

    def laplace(ref, p):
        x = ref[p, PAD : PAD + cw]
        row = lax.broadcasted_iota(jnp.int32, x.shape, 0) + e * cw
        col = lax.broadcasted_iota(jnp.int32, x.shape, 1)
        beside = ref[p + 1, PAD : PAD + cw] + ref[p - 1, PAD : PAD + cw]
        beside = beside + jnp.where(col < NY - 1, pltpu.roll(x, NY - 1, 1), 0.0)
        beside = beside + jnp.where(col > 0, pltpu.roll(x, 1, 1), 0.0)
        beside = beside + jnp.where(row < cw * ne - 1, ref[p, PAD + 1 : PAD + cw + 1], 0.0)
        beside = beside + jnp.where(row > 0, ref[p, PAD - 1 : PAD + cw - 1], 0.0)
        return 6.0 * x - beside

    def halo(ref, r):
        own, planes = pl.ds(PAD, cw), pl.ds(1, CX)
        moves = [
            (ref.at[CX, own], ref.at[0, own], (e, lax.rem(s + 1, n))),
            (ref.at[1, own], ref.at[CX + 1, own], (e, lax.rem(s - 1 + n, n))),
            (ref.at[planes, pl.ds(cw, PAD)], ref.at[planes, pl.ds(0, PAD)], (lax.rem(e + 1, ne), s)),
            (
                ref.at[planes, pl.ds(PAD, PAD)],
                ref.at[planes, pl.ds(PAD + cw, PAD)],
                (lax.rem(e - 1 + ne, ne), s),
            ),
        ]
        copies = [
            pltpu.make_async_remote_copy(
                src_ref=a, dst_ref=b, send_sem=halo_send.at[4 * r + i],
                recv_sem=halo_recv.at[4 * r + i], device_id=to, device_id_type=MESH,
            )
            for i, (a, b, to) in enumerate(moves)
        ]
        for copy in copies:
            copy.start()
        return copies

    def gather_parts(full, r):
        copies = [
            pltpu.make_async_remote_copy(
                src_ref=full.at[e], dst_ref=full.at[e], send_sem=full_send.at[ne * r + j],
                recv_sem=full_recv.at[r], device_id=(lax.rem(e + j, ne), s), device_id_type=MESH,
            )
            for j in range(1, ne)
        ]
        for copy in copies:
            copy.start()
        return copies

    def share(tiles, numbers, squares, r):
        lane = lax.broadcasted_iota(jnp.int32, (1, LANES), 1)
        row = jnp.zeros((1, LANES), jnp.float32)
        for i, square in enumerate(squares):
            row = jnp.where(lane == i, square, row)
        numbers[me] = row

        def act(other):
            for i, ref in enumerate((tiles, numbers)):
                pltpu.make_async_remote_copy(
                    src_ref=ref.at[me], dst_ref=ref.at[me], send_sem=bsend.at[2 * r + i],
                    recv_sem=brecv.at[2 * r + i], device_id=place(other), device_id_type=MESH,
                ).start()

        each_other(act)
        done = []
        for i, ref in enumerate((tiles, numbers)):
            rest = ref.at[pl.ds(0, nd - 1)]
            done.append(
                pltpu.make_async_remote_copy(
                    src_ref=rest, dst_ref=rest, send_sem=bsend.at[2 * r + i],
                    recv_sem=brecv.at[2 * r + i], device_id=(e, s), device_id_type=MESH,
                )
            )
        return done

    def tile_sum(tiles):
        parts = [tiles[k] for k in range(nd)]
        while len(parts) > 1:
            parts = [a + b for a, b in zip(parts[::2], parts[1::2])]
        return parts[0]

    def apply_rays(tiles):
        def block(b, c):
            at = pl.ds(pl.multiple_of(b * wide, wide), wide)
            picked = jnp.dot(table2[...], s_mat[:, at], preferred_element_type=jnp.float32)
            plane = plane_ref[:, at]
            mine = picked[: 2 * cw]
            for i in range(1, CX):
                mine = jnp.where(plane == float(i), picked[2 * cw * i : 2 * cw * (i + 1)], mine)
            sums = jnp.sum((mine[:cw] + mine[cw:]) * kt[:, at], axis=0, keepdims=True)
            for i in range(4):
                e_ref[pl.ds(b * 4 + i, 1), :] = sums[:, i * LANES : (i + 1) * LANES]
            return c

        lax.fori_loop(0, nc // 4, block, 0)
        ray = rr_ref[...]
        for j in range(g):
            terms = jnp.where(lane // ps == j, e_ref[...], 0.0)
            value = jnp.zeros((nc, LANES), jnp.float32)
            for r in range(rays):
                one = jnp.sum(jnp.where(ray == float(r), terms, 0.0), axis=1, keepdims=True)
                value = jnp.where(lane == r, one, value)
            w_ref[rays_of(j), :] = value
        value = w_ref[:packed]
        for q in range(1, pack):
            value = value + pltpu.roll(w_ref[q * packed : (q + 1) * packed], q * rays, 1)
        tiles[me] = value

    def ray_sums(tiles):
        value = tile_sum(tiles)
        parts = [value] + [pltpu.roll(value, LANES - q * rays, 1) for q in range(1, pack)]
        value = jnp.concatenate(parts, axis=0)
        return jnp.where(lax.broadcasted_iota(jnp.int32, value.shape, 1) < rays, value, 0.0)

    def nothing():
        return jnp.zeros((cw, NY), jnp.float32)

    square = nothing()
    for p in range(CX):
        value = scattered(p) / beta0
        d0[p + 1, PAD : PAD + cw] = value
        full0[e, p] = value
        table2[2 * cw * p : 2 * cw * (p + 1)] = two_parts(value)
        square = square + value * value
    halos0 = halo(d0, 0)
    apply_rays(y0)
    for copy in halos0:
        copy.wait()
    curved = nothing()
    for p in range(CX):
        value = laplace(d0, p + 1)
        m1[p + 1, PAD : PAD + cw] = value
        curved = curved + value * value
    shared0 = share(y0, q0, [total(square), total(curved)], 0)
    halos1 = halo(m1, 1)
    gather0 = gather_parts(full0, 0)
    for copy in shared0:
        copy.wait_recv()
    numbers = tile_sum(q0)
    alpha0 = jnp.sqrt(numbers[:, 0:1] + norm_epsilon)
    curved0 = numbers[:, 1:2]

    u1 = ray_sums(y0) / alpha0 - alpha0 * u0
    u_ref[...] = u1
    model_square = damping * damping * (curved0 / (alpha0 * alpha0))
    beta1 = jnp.sqrt(total(u1 * u1) + model_square + norm_epsilon)
    scale1 = damping / alpha0 / beta1
    scatter_rays()
    for copy in halos1:
        copy.wait()
    square = nothing()
    for p in range(CX):
        value = scattered(p) / beta1 + damping * scale1 * laplace(m1, p + 1)
        value = value - beta1 / alpha0 * d0[p + 1, PAD : PAD + cw]
        d1[p + 1, PAD : PAD + cw] = value
        full1[e, p] = value
        table2[2 * cw * p : 2 * cw * (p + 1)] = two_parts(value)
        square = square + value * value
    halos2 = halo(d1, 2)
    apply_rays(y1)
    for copy in halos2:
        copy.wait()
    curved = nothing()
    cross = nothing()
    for p in range(CX):
        value = laplace(d1, p + 1)
        curved = curved + value * value
        cross = cross + value * m1[p + 1, PAD : PAD + cw]
    shared1 = share(y1, q1, [total(square), total(curved), total(cross)], 1)
    gather1 = gather_parts(full1, 1)
    rho1 = jnp.sqrt(alpha0 * alpha0 + beta1 * beta1)
    cosine1 = alpha0 / rho1
    sine1 = beta1 / rho1
    phi1 = cosine1 * beta0
    phi_bar = sine1 * beta0
    for copy in shared1:
        copy.wait_recv()
    numbers = tile_sum(q1)
    alpha1 = jnp.sqrt(numbers[:, 0:1] + norm_epsilon)
    theta1 = sine1 * alpha1
    rho_bar = -cosine1 * alpha1

    u2 = ray_sums(y1) / alpha1 - alpha1 * (u1 / beta1)
    a, b = damping / alpha1, alpha1 * scale1
    model_square = a * a * numbers[:, 1:2] - 2.0 * a * b * numbers[:, 2:3] + b * b * curved0
    model_square = jnp.maximum(model_square, 0.0)
    beta2 = jnp.sqrt(total(u2 * u2) + model_square + norm_epsilon)
    rho2 = jnp.sqrt(rho_bar * rho_bar + beta2 * beta2)
    phi2 = rho_bar / rho2 * phi_bar

    for r, full in enumerate((full0, full1)):
        rest = full.at[pl.ds(0, ne - 1)]
        pltpu.make_async_remote_copy(
            src_ref=rest, dst_ref=rest, send_sem=full_send.at[ne * r], recv_sem=full_recv.at[r],
            device_id=(e, s), device_id_type=MESH,
        ).wait_recv()

    def finish(p, c):
        for i in range(ne):
            first = full0[i, p] / alpha0
            search = full1[i, p] / alpha1 - theta1 / rho1 * first
            out_ref[p, i * cw : (i + 1) * cw] = phi1 / rho1 * first + phi2 / rho2 * search
        return c

    lax.fori_loop(0, CX, finish, 0)

    rest = send.at[pl.ds(0, nd - 1)]
    pltpu.make_async_remote_copy(
        src_ref=rest, dst_ref=rest, send_sem=ssem.at[0], recv_sem=rsem.at[0],
        device_id=(e, s), device_id_type=MESH,
    ).wait_send()
    for copy in gather0 + gather1 + shared0 + shared1:
        copy.wait_send()


def solution(mesh):
    ne, n = mesh.shape["ev"], mesh.shape["slab"]

    def on_device(kernels, block_ids, delays):
        rays, per_ray, width = kernels.shape
        entries = rays * per_ray
        ps = entries // n
        nd = ne * n
        cw = width // ne
        rows = nd * ps
        cells = CX * NY
        f32, bf16 = jnp.float32, jnp.bfloat16
        vmem = pl.BlockSpec(memory_space=pltpu.VMEM)
        model = pltpu.VMEM((CX + 2, cw + 2 * PAD, NY), f32)
        full = pltpu.VMEM((ne, CX, cw, NY), f32)
        tiles = pltpu.VMEM((nd, nd * rays // LANES, LANES), f32)
        scalar = pltpu.VMEM((nd, 1, LANES), f32)
        small = pltpu.VMEM((rows // LANES, LANES), f32)
        by_device = pltpu.VMEM((nd, LANES), f32)
        result = pl.pallas_call(
            functools.partial(kernel, ne, n, ps, rays, cw),
            out_shape=jax.ShapeDtypeStruct((CX, width, NY), f32),
            in_specs=[pl.BlockSpec(memory_space=pl.ANY), vmem, vmem],
            out_specs=vmem,
            scratch_shapes=[
                pltpu.VMEM((entries, width), f32),
                pltpu.VMEM((nd, cw + 8, LANES), f32),
                pltpu.VMEM((nd, cw + 8, LANES), f32),
                pltpu.VMEM((2 * width + 2 * PAD, entries), bf16),
                pltpu.VMEM((NY, rows), bf16),
                pltpu.VMEM((cw, rows), f32),
                pltpu.VMEM((1, rows), f32),
                pltpu.VMEM((2 * cw * CX, NY), bf16),
                pltpu.VMEM((2 * cw * CX, NY), f32),
                small,
                by_device,
                small,
                by_device,
                pltpu.VMEM((rays, LANES), f32),
                pltpu.VMEM((1, LANES), f32),
                model, model, model, full, full, tiles, tiles, scalar, scalar,
                pltpu.SemaphoreType.DMA((1,)),
                pltpu.SemaphoreType.DMA((nd,)),
                pltpu.SemaphoreType.DMA((12,)),
                pltpu.SemaphoreType.DMA((12,)),
                pltpu.SemaphoreType.DMA((2 * ne,)),
                pltpu.SemaphoreType.DMA((2,)),
                pltpu.SemaphoreType.DMA((4,)),
                pltpu.SemaphoreType.DMA((4,)),
                pltpu.SemaphoreType.DMA,
            ],
            compiler_params=pltpu.CompilerParams(
                collective_id=0, has_side_effects=True, vmem_limit_bytes=60 * 1024 * 1024
            ),
        )(kernels.reshape(entries, width), block_ids, delays.reshape(1, rays))
        return jnp.swapaxes(result, 1, 2)

    in_specs = (P(("ev", "slab"), None, None), P(("ev", "slab"), None), P(("ev", "slab")))
    return jax.shard_map(
        on_device, mesh=mesh, in_specs=in_specs, out_specs=P("slab", None, None), check_vma=False
    )
```

```python
import functools

import jax
import jax.numpy as jnp
from jax import lax
from jax.experimental import pallas as pl
from jax.experimental.pallas import tpu as pltpu
from jax.sharding import PartitionSpec as P

CX = 8
NY = 128
LANES = 128
MESH = pl.DeviceIdType.MESH

damping = 0.3
norm_epsilon = 1e-06


def iota(shape, dim):
    return lax.broadcasted_iota(jnp.int32, shape, dim).astype(jnp.float32)


def total(x):
    return jnp.sum(jnp.sum(x, axis=0, keepdims=True), axis=1, keepdims=True)


def one_hot(mask):
    return jnp.where(mask, 1.0, 0.0).astype(jnp.bfloat16)


def two_parts(x):
    high = x.astype(jnp.bfloat16)
    low = (x - high.astype(jnp.float32)).astype(jnp.bfloat16)
    return jnp.concatenate([high, low], axis=0)


PAD = 8


def kernel(
    ne, n, ps, rays, cw,
    kern_ref, ids_ref, delay_ref, out_ref,
    kern_rows, send, recv, facts_out, facts_in, pieces, s_mat, kt, plane_ref, table2, acc, rr_ref, w_ref, e_ref, u_ref,
    ids_wide, delay_wide, d0, m1, d1, full0, full1, y0, y1, q0, q1,
    ssem, rsem, fssem, frsem, halo_send, halo_recv, full_send, full_recv, bsend, brecv, load_sem,
):
    nd = ne * n
    g = LANES // ps
    cpg = n // g
    nc = nd // g
    entries = n * ps
    cells = CX * NY
    pack = LANES // rays
    packed = nd // pack
    e = lax.axis_index("ev")
    s = lax.axis_index("slab")
    me = e * n + s

    load = pltpu.make_async_copy(kern_ref, kern_rows, load_sem)
    load.start()
    barrier = pltpu.get_barrier_semaphore()

    def each_other(act):
        if nd <= 32:
            for k in range(1, nd):
                act(lax.rem(me + k, nd))
        else:

            def step(k, c):
                act(lax.rem(me + k, nd))
                return c

            lax.fori_loop(1, nd, step, 0)

    def place(device):
        return (device // n, lax.rem(device, n))

    each_other(
        lambda other: pl.semaphore_signal(
            barrier, inc=1, device_id=place(other), device_id_type=MESH
        )
    )

    per_ray = ids_ref.shape[1]
    some = LANES // per_ray
    ids_wide[...] = jnp.zeros_like(ids_wide)
    ids_wide[:, :per_ray] = ids_ref[...].astype(jnp.float32)
    delay_wide[...] = jnp.zeros_like(delay_wide)
    delay_wide[:, :rays] = delay_ref[...]
    wide_ids = ids_wide[...]
    ray_index = lax.broadcasted_iota(jnp.int32, wide_ids.shape, 0)
    moved = wide_ids
    for i in range(1, some):
        moved = jnp.where(ray_index % some == i, pltpu.roll(wide_ids, i * per_ray, 1), moved)
    tiles_own = entries // LANES
    id_rows = [
        jnp.sum(moved[q * some : (q + 1) * some], axis=0, keepdims=True) for q in range(tiles_own)
    ]

    earlier = one_hot(iota((LANES, LANES), 0) < iota((LANES, LANES), 1))
    taken = jnp.zeros((n, 1), jnp.float32)
    positions = []
    load.wait()
    for q, ids in enumerate(id_rows):
        at = slice(q * LANES, (q + 1) * LANES)
        slab_row = jnp.floor(ids * (1.0 / cells))
        inside = ids - slab_row * cells
        row_i = jnp.floor(inside * (1.0 / NY))
        owner = slab_row == iota((n, LANES), 0)
        counts = jnp.dot(one_hot(owner), earlier, preferred_element_type=jnp.float32) + taken
        rank = jnp.sum(jnp.where(owner, counts, 0.0), axis=0, keepdims=True)
        taken = taken + jnp.sum(jnp.where(owner, 1.0, 0.0), axis=1, keepdims=True)
        positions.append(slab_row * ps + rank)
        ray_row = jnp.floor(iota((1, LANES), 1) * (1.0 / per_ray)) + float(q * some)
        kind = iota((2 * PAD, LANES), 0)
        facts = jnp.where(kind == 0.0, row_i, 0.0)
        facts = jnp.where(kind == 1.0, inside - row_i * NY, facts)
        facts = jnp.where(kind == 2.0, ray_row, facts)
        pieces[: 2 * LANES, at] = two_parts(kern_rows[at, :].T)
        pieces[2 * LANES :, at] = facts.astype(jnp.bfloat16)
    position = jnp.concatenate(positions, axis=1)
    acc[...] = jnp.zeros_like(acc)
    pl.semaphore_wait(barrier, nd - 1)

    def rows_to(dest):
        pairs = ((send, recv, ssem, rsem), (facts_out, facts_in, fssem, frsem))
        return [
            pltpu.make_async_remote_copy(
                src_ref=a.at[dest], dst_ref=b.at[me], send_sem=left.at[0], recv_sem=landed.at[me],
                device_id=place(dest), device_id_type=MESH,
            )
            for a, b, left, landed in pairs
        ]

    def sort_tile(k, c):
        t = lax.rem(s // g + cpg // 2 + k, cpg)
        pm = one_hot(iota((LANES, entries), 0) + (t * LANES).astype(jnp.float32) == position)
        both = lax.dot_general(
            pieces[...], pm, (((1,), (1,)), ((), ())), preferred_element_type=jnp.float32
        )
        rows = both[:LANES] + both[LANES : 2 * LANES]
        tile = both[2 * LANES : 2 * LANES + PAD]
        code = (tile[2:3] * CX + tile[0:1]) * NY + tile[1:2]
        code = jnp.broadcast_to(code, (PAD, LANES))
        for j in range(g):
            part = code if j == 0 else pltpu.roll(code, LANES - j * ps, 1)
            block = rows if j == 0 else pltpu.roll(rows, LANES - j * ps, 1)
            for i in range(ne):
                dest = i * n + t * g + j
                send[dest] = block[i * cw : (i + 1) * cw]
                facts_out[dest, 0:1] = part[0:1]
                facts_out[dest, 1:2] = delay_wide[...]

                @pl.when(dest != me)
                def _():
                    for copy in rows_to(dest):
                        copy.start()

        return c

    lax.fori_loop(0, cpg, sort_tile, 0)
    recv[me] = send[me]
    facts_in[me] = facts_out[me]

    def chunk(cc):
        delay_rows = []
        for j in range(g):
            slot = cc * g + j

            @pl.when(slot != me)
            def _():
                for ref, left, landed in ((recv, ssem, rsem), (facts_in, fssem, frsem)):
                    pltpu.make_async_remote_copy(
                        src_ref=ref.at[slot], dst_ref=ref.at[slot], send_sem=left.at[0],
                        recv_sem=landed.at[slot], device_id=(e, s), device_id_type=MESH,
                    ).wait_recv()

            delay_rows.append(facts_in[slot, 1:2])
            u_ref[pl.ds(slot, 1), :] = delay_rows[-1]
        block = recv[cc * g]
        code = jnp.broadcast_to(facts_in[cc * g, 0:1], (PAD, LANES))
        at_lane = lax.broadcasted_iota(jnp.int32, (1, LANES), 1) // ps
        for j in range(1, g):
            other = jnp.broadcast_to(facts_in[cc * g + j, 0:1], (PAD, LANES))
            block = jnp.where(at_lane == j, pltpu.roll(recv[cc * g + j], j * ps, 1), block)
            code = jnp.where(at_lane == j, pltpu.roll(other, j * ps, 1), code)
        code = code[0:1]
        ray = jnp.floor(code * (1.0 / cells))
        inside = code - ray * cells
        plane = jnp.floor(inside * (1.0 / NY))
        first = pl.multiple_of(cc * LANES, LANES)
        kt[:, pl.ds(first, LANES)] = block
        plane_ref[:, pl.ds(first, LANES)] = plane
        rr_ref[pl.ds(cc, 1), :] = ray
        hot = one_hot(iota((NY, LANES), 0) == inside - plane * NY)
        s_mat[:, pl.ds(first, LANES)] = hot
        return ray, delay_rows, hot, block, plane

    def by_plane(rows, plane):
        high = rows.astype(jnp.bfloat16).astype(jnp.float32)
        both = jnp.concatenate([high, rows - high], axis=0)
        return jnp.concatenate(
            [jnp.where(plane == float(i), both, 0.0).astype(jnp.bfloat16) for i in range(CX)], axis=0
        )

    def add_rows(terms, hot):
        acc[...] += lax.dot_general(
            terms, hot, (((1,), (1,)), ((), ())), preferred_element_type=jnp.float32
        )

    def spread(ray, weights):
        lane = lax.broadcasted_iota(jnp.int32, ray.shape, 1)
        result = jnp.zeros(ray.shape, jnp.float32)
        for j in range(g):
            mine = jnp.zeros(ray.shape, jnp.float32)
            for r in range(rays):
                mine = jnp.where(ray == float(r), weights[j][:, r : r + 1], mine)
            result = jnp.where(lane // ps == j, mine, result)
        return result

    def arrivals(k, c):
        inner = lax.rem(s // g - cpg // 2 - k + 2 * cpg, cpg)
        chunks = [lax.rem(e + j, ne) * cpg + inner for j in range(ne)]
        found = [chunk(cc) for cc in chunks]
        ray = jnp.concatenate([f[0] for f in found], axis=0)
        weights = [jnp.concatenate([f[1][j] for f in found], axis=0) for j in range(g)]
        w = spread(ray, weights)
        terms = [
            by_plane(f[3] * w[j : j + 1], f[4]) for j, f in enumerate(found)
        ]
        add_rows(jnp.concatenate(terms, axis=1), jnp.concatenate([f[2] for f in found], axis=1))
        return c

    lax.fori_loop(0, cpg, arrivals, 0)

    delays = u_ref[...]
    beta0 = jnp.sqrt(total(delays * delays) + norm_epsilon)
    u0 = delays / beta0
    lane = lax.broadcasted_iota(jnp.int32, (nc, LANES), 1)

    def rays_of(j):
        return pl.ds(j, nc, stride=g) if g > 1 else pl.ds(0, nc)

    wide = 4 * LANES

    def scatter_rays():
        w_ref[:nc] = spread(rr_ref[...], [u_ref[rays_of(j), :] for j in range(g)])
        acc[...] = jnp.zeros_like(acc)

        def block(b, c):
            at = pl.ds(pl.multiple_of(b * wide, wide), wide)
            w = jnp.concatenate([w_ref[pl.ds(b * 4 + i, 1), :] for i in range(4)], axis=1)
            add_rows(by_plane(kt[:, at] * w, plane_ref[:, at]), s_mat[:, at])
            return c

        lax.fori_loop(0, nc // 4, block, 0)

    def scattered(p):
        return acc[2 * cw * p : 2 * cw * p + cw] + acc[2 * cw * p + cw : 2 * cw * (p + 1)]

    def laplace(ref, p):
        x = ref[p, PAD : PAD + cw]
        row = lax.broadcasted_iota(jnp.int32, x.shape, 0) + e * cw
        col = lax.broadcasted_iota(jnp.int32, x.shape, 1)
        beside = ref[p + 1, PAD : PAD + cw] + ref[p - 1, PAD : PAD + cw]
        beside = beside + jnp.where(col < NY - 1, pltpu.roll(x, NY - 1, 1), 0.0)
        beside = beside + jnp.where(col > 0, pltpu.roll(x, 1, 1), 0.0)
        beside = beside + jnp.where(row < cw * ne - 1, ref[p, PAD + 1 : PAD + cw + 1], 0.0)
        beside = beside + jnp.where(row > 0, ref[p, PAD - 1 : PAD + cw - 1], 0.0)
        return 6.0 * x - beside

    def halo(ref, r):
        own, planes = pl.ds(PAD, cw), pl.ds(1, CX)
        moves = [
            (ref.at[CX, own], ref.at[0, own], (e, lax.rem(s + 1, n))),
            (ref.at[1, own], ref.at[CX + 1, own], (e, lax.rem(s - 1 + n, n))),
            (ref.at[planes, pl.ds(cw, PAD)], ref.at[planes, pl.ds(0, PAD)], (lax.rem(e + 1, ne), s)),
            (
                ref.at[planes, pl.ds(PAD, PAD)],
                ref.at[planes, pl.ds(PAD + cw, PAD)],
                (lax.rem(e - 1 + ne, ne), s),
            ),
        ]
        copies = [
            pltpu.make_async_remote_copy(
                src_ref=a, dst_ref=b, send_sem=halo_send.at[4 * r + i],
                recv_sem=halo_recv.at[4 * r + i], device_id=to, device_id_type=MESH,
            )
            for i, (a, b, to) in enumerate(moves)
        ]
        for copy in copies:
            copy.start()
        return copies

    def gather_parts(full, r):
        copies = [
            pltpu.make_async_remote_copy(
                src_ref=full.at[e], dst_ref=full.at[e], send_sem=full_send.at[ne * r + j],
                recv_sem=full_recv.at[r], device_id=(lax.rem(e + j, ne), s), device_id_type=MESH,
            )
            for j in range(1, ne)
        ]
        for copy in copies:
            copy.start()
        return copies

    def share(tiles, squares, r):
        lane = lax.broadcasted_iota(jnp.int32, (PAD, LANES), 1)
        rows = jnp.zeros((PAD, LANES), jnp.float32)
        for i, square in enumerate(squares):
            rows = jnp.where(lane == i, square, rows)
        tiles[s, packed:] = rows
        return spread_out(tiles, n, s, lambda t: (e, t), 2 * r)

    def spread_out(tiles, count, mine, device, sem):
        def copy(ref, to):
            return pltpu.make_async_remote_copy(
                src_ref=ref, dst_ref=ref, send_sem=bsend.at[sem], recv_sem=brecv.at[sem],
                device_id=to, device_id_type=MESH,
            )

        for k in range(1, count):
            copy(tiles.at[mine], device(lax.rem(mine + k, count))).start()
        return copy(tiles.at[pl.ds(0, count - 1)], (e, s))

    def finish_share(tiles, sums, r, first):
        first.wait_recv()
        sums[e] = tile_sum(tiles, n)
        second = spread_out(sums, ne, e, lambda t: (t, s), 2 * r + 1)
        second.wait_recv()
        return tile_sum(sums, ne), second

    def tile_sum(tiles, count):
        parts = [tiles[k] for k in range(count)]
        while len(parts) > 1:
            odd = parts[len(parts) // 2 * 2 :]
            parts = [a + b for a, b in zip(parts[::2], parts[1::2])] + odd
        return parts[0]

    def apply_rays(tiles):
        def block(b, c):
            at = pl.ds(pl.multiple_of(b * wide, wide), wide)
            picked = jnp.dot(table2[...], s_mat[:, at], preferred_element_type=jnp.float32)
            plane = plane_ref[:, at]
            mine = picked[: 2 * cw]
            for i in range(1, CX):
                mine = jnp.where(plane == float(i), picked[2 * cw * i : 2 * cw * (i + 1)], mine)
            sums = jnp.sum((mine[:cw] + mine[cw:]) * kt[:, at], axis=0, keepdims=True)
            for i in range(4):
                e_ref[pl.ds(b * 4 + i, 1), :] = sums[:, i * LANES : (i + 1) * LANES]
            return c

        lax.fori_loop(0, nc // 4, block, 0)
        ray = rr_ref[...]
        for j in range(g):
            terms = jnp.where(lane // ps == j, e_ref[...], 0.0)
            value = jnp.zeros((nc, LANES), jnp.float32)
            for r in range(rays):
                one = jnp.sum(jnp.where(ray == float(r), terms, 0.0), axis=1, keepdims=True)
                value = jnp.where(lane == r, one, value)
            w_ref[rays_of(j), :] = value
        value = w_ref[:packed]
        for q in range(1, pack):
            value = value + pltpu.roll(w_ref[q * packed : (q + 1) * packed], q * rays, 1)
        tiles[s, :packed] = value

    def ray_sums(value):
        parts = [value] + [pltpu.roll(value, LANES - q * rays, 1) for q in range(1, pack)]
        value = jnp.concatenate(parts, axis=0)
        return jnp.where(lax.broadcasted_iota(jnp.int32, value.shape, 1) < rays, value, 0.0)

    def nothing():
        return jnp.zeros((cw, NY), jnp.float32)

    square = nothing()
    for p in range(CX):
        value = scattered(p) / beta0
        d0[p + 1, PAD : PAD + cw] = value
        full0[e, p] = value
        table2[2 * cw * p : 2 * cw * (p + 1)] = two_parts(value)
        square = square + value * value
    halos0 = halo(d0, 0)
    apply_rays(y0)
    for copy in halos0:
        copy.wait()
    curved = nothing()
    for p in range(CX):
        value = laplace(d0, p + 1)
        m1[p + 1, PAD : PAD + cw] = value
        curved = curved + value * value
    shared0 = share(y0, [total(square), total(curved)], 0)
    halos1 = halo(m1, 1)
    gather0 = gather_parts(full0, 0)
    sums, passed0 = finish_share(y0, q0, 0, shared0)
    numbers = sums[packed : packed + 1]
    alpha0 = jnp.sqrt(numbers[:, 0:1] + norm_epsilon)
    curved0 = numbers[:, 1:2]

    u1 = ray_sums(sums[:packed]) / alpha0 - alpha0 * u0
    u_ref[...] = u1
    model_square = damping * damping * (curved0 / (alpha0 * alpha0))
    beta1 = jnp.sqrt(total(u1 * u1) + model_square + norm_epsilon)
    scale1 = damping / alpha0 / beta1
    scatter_rays()
    for copy in halos1:
        copy.wait()
    square = nothing()
    for p in range(CX):
        value = scattered(p) / beta1 + damping * scale1 * laplace(m1, p + 1)
        value = value - beta1 / alpha0 * d0[p + 1, PAD : PAD + cw]
        d1[p + 1, PAD : PAD + cw] = value
        full1[e, p] = value
        table2[2 * cw * p : 2 * cw * (p + 1)] = two_parts(value)
        square = square + value * value
    halos2 = halo(d1, 2)
    gather1 = gather_parts(full1, 1)
    apply_rays(y1)
    for copy in halos2:
        copy.wait()
    curved = nothing()
    cross = nothing()
    for p in range(CX):
        value = laplace(d1, p + 1)
        curved = curved + value * value
        cross = cross + value * m1[p + 1, PAD : PAD + cw]
    shared1 = share(y1, [total(square), total(curved), total(cross)], 1)
    rho1 = jnp.sqrt(alpha0 * alpha0 + beta1 * beta1)
    cosine1 = alpha0 / rho1
    sine1 = beta1 / rho1
    phi1 = cosine1 * beta0
    phi_bar = sine1 * beta0
    sums, passed1 = finish_share(y1, q1, 1, shared1)
    numbers = sums[packed : packed + 1]
    alpha1 = jnp.sqrt(numbers[:, 0:1] + norm_epsilon)
    theta1 = sine1 * alpha1
    rho_bar = -cosine1 * alpha1

    u2 = ray_sums(sums[:packed]) / alpha1 - alpha1 * (u1 / beta1)
    a, b = damping / alpha1, alpha1 * scale1
    model_square = a * a * numbers[:, 1:2] - 2.0 * a * b * numbers[:, 2:3] + b * b * curved0
    model_square = jnp.maximum(model_square, 0.0)
    beta2 = jnp.sqrt(total(u2 * u2) + model_square + norm_epsilon)
    rho2 = jnp.sqrt(rho_bar * rho_bar + beta2 * beta2)
    phi2 = rho_bar / rho2 * phi_bar

    for r, full in enumerate((full0, full1)):
        rest = full.at[pl.ds(0, ne - 1)]
        pltpu.make_async_remote_copy(
            src_ref=rest, dst_ref=rest, send_sem=full_send.at[ne * r], recv_sem=full_recv.at[r],
            device_id=(e, s), device_id_type=MESH,
        ).wait_recv()

    def finish(p, c):
        for i in range(ne):
            first = full0[i, p] / alpha0
            search = full1[i, p] / alpha1 - theta1 / rho1 * first
            out_ref[p, i * cw : (i + 1) * cw] = phi1 / rho1 * first + phi2 / rho2 * search
        return c

    lax.fori_loop(0, CX, finish, 0)

    rest = send.at[pl.ds(0, nd - 1)]
    pltpu.make_async_remote_copy(
        src_ref=rest, dst_ref=rest, send_sem=ssem.at[0], recv_sem=rsem.at[0],
        device_id=(e, s), device_id_type=MESH,
    ).wait_send()
    rest = facts_out.at[pl.ds(0, nd - 1)]
    pltpu.make_async_remote_copy(
        src_ref=rest, dst_ref=rest, send_sem=fssem.at[0], recv_sem=frsem.at[0],
        device_id=(e, s), device_id_type=MESH,
    ).wait_send()
    for copy in gather0 + gather1 + [shared0, shared1, passed0, passed1]:
        copy.wait_send()


def solution(mesh):
    ne, n = mesh.shape["ev"], mesh.shape["slab"]

    def on_device(kernels, block_ids, delays):
        rays, per_ray, width = kernels.shape
        entries = rays * per_ray
        ps = entries // n
        nd = ne * n
        cw = width // ne
        rows = nd * ps
        cells = CX * NY
        f32, bf16 = jnp.float32, jnp.bfloat16
        vmem = pl.BlockSpec(memory_space=pltpu.VMEM)
        model = pltpu.VMEM((CX + 2, cw + 2 * PAD, NY), f32)
        full = pltpu.VMEM((ne, CX, cw, NY), f32)
        high = nd * rays // LANES + PAD
        tiles = pltpu.VMEM((n, high, LANES), f32)
        tile_sums = pltpu.VMEM((ne, high, LANES), f32)
        small = pltpu.VMEM((rows // LANES, LANES), f32)
        by_device = pltpu.VMEM((nd, LANES), f32)
        result = pl.pallas_call(
            functools.partial(kernel, ne, n, ps, rays, cw),
            out_shape=jax.ShapeDtypeStruct((CX, width, NY), f32),
            in_specs=[pl.BlockSpec(memory_space=pl.ANY), vmem, vmem],
            out_specs=vmem,
            scratch_shapes=[
                pltpu.VMEM((entries, width), f32),
                pltpu.VMEM((nd, cw, LANES), f32),
                pltpu.VMEM((nd, cw, LANES), f32),
                pltpu.VMEM((nd, 2, LANES), f32),
                pltpu.VMEM((nd, 2, LANES), f32),
                pltpu.VMEM((2 * width + 2 * PAD, entries), bf16),
                pltpu.VMEM((NY, rows), bf16),
                pltpu.VMEM((cw, rows), f32),
                pltpu.VMEM((1, rows), f32),
                pltpu.VMEM((2 * cw * CX, NY), bf16),
                pltpu.VMEM((2 * cw * CX, NY), f32),
                small,
                by_device,
                small,
                by_device,
                pltpu.VMEM((rays, LANES), f32),
                pltpu.VMEM((1, LANES), f32),
                model, model, model, full, full, tiles, tiles, tile_sums, tile_sums,
                pltpu.SemaphoreType.DMA((1,)),
                pltpu.SemaphoreType.DMA((nd,)),
                pltpu.SemaphoreType.DMA((1,)),
                pltpu.SemaphoreType.DMA((nd,)),
                pltpu.SemaphoreType.DMA((12,)),
                pltpu.SemaphoreType.DMA((12,)),
                pltpu.SemaphoreType.DMA((2 * ne,)),
                pltpu.SemaphoreType.DMA((2,)),
                pltpu.SemaphoreType.DMA((4,)),
                pltpu.SemaphoreType.DMA((4,)),
                pltpu.SemaphoreType.DMA,
            ],
            compiler_params=pltpu.CompilerParams(
                collective_id=0, has_side_effects=True, vmem_limit_bytes=60 * 1024 * 1024
            ),
        )(kernels.reshape(entries, width), block_ids, delays.reshape(1, rays))
        return jnp.swapaxes(result, 1, 2)

    in_specs = (P(("ev", "slab"), None, None), P(("ev", "slab"), None), P(("ev", "slab")))
    return jax.shard_map(
        on_device, mesh=mesh, in_specs=in_specs, out_specs=P("slab", None, None), check_vma=False
    )
```

```python
import functools

import jax
import jax.numpy as jnp
from jax import lax
from jax.experimental import pallas as pl
from jax.experimental.pallas import tpu as pltpu
from jax.sharding import PartitionSpec as P

CX = 8
NY = 128
LANES = 128
MESH = pl.DeviceIdType.MESH

damping = 0.3
norm_epsilon = 1e-06


def iota(shape, dim):
    return lax.broadcasted_iota(jnp.int32, shape, dim).astype(jnp.float32)


def total(x):
    return jnp.sum(jnp.sum(x, axis=0, keepdims=True), axis=1, keepdims=True)


def one_hot(mask):
    return jnp.where(mask, 1.0, 0.0).astype(jnp.bfloat16)


def two_parts(x):
    high = x.astype(jnp.bfloat16)
    low = (x - high.astype(jnp.float32)).astype(jnp.bfloat16)
    return jnp.concatenate([high, low], axis=0)


PAD = 8


def kernel(
    ne, n, ps, rays, cw,
    kern_ref, ids_ref, delay_ref, out_ref,
    kern_rows, send, recv, facts_out, facts_in, pieces, s_mat, kt, plane_ref, table2, acc, rr_ref, w_ref, e_ref, u_ref,
    ids_wide, delay_wide, d0, m1, d1, full0, full1, y0, y1, q0, q1,
    ssem, rsem, fssem, frsem, halo_send, halo_recv, full_send, full_recv, bsend, brecv, load_sem,
):
    nd = ne * n
    g = LANES // ps
    cpg = n // g
    nc = nd // g
    entries = n * ps
    cells = CX * NY
    pack = LANES // rays
    packed = nd // pack
    e = lax.axis_index("ev")
    s = lax.axis_index("slab")
    me = e * n + s

    load = pltpu.make_async_copy(kern_ref, kern_rows, load_sem)
    load.start()
    barrier = pltpu.get_barrier_semaphore()

    def each_other(act):
        if nd <= 32:
            for k in range(1, nd):
                act(lax.rem(me + k, nd))
        else:

            def step(k, c):
                act(lax.rem(me + k, nd))
                return c

            lax.fori_loop(1, nd, step, 0)

    def place(device):
        return (device // n, lax.rem(device, n))

    each_other(
        lambda other: pl.semaphore_signal(
            barrier, inc=1, device_id=place(other), device_id_type=MESH
        )
    )

    per_ray = ids_ref.shape[1]
    some = LANES // per_ray
    ids_wide[...] = jnp.zeros_like(ids_wide)
    ids_wide[:, :per_ray] = ids_ref[...].astype(jnp.float32)
    delay_wide[...] = jnp.zeros_like(delay_wide)
    delay_wide[:, :rays] = delay_ref[...]
    wide_ids = ids_wide[...]
    ray_index = lax.broadcasted_iota(jnp.int32, wide_ids.shape, 0)
    moved = wide_ids
    for i in range(1, some):
        moved = jnp.where(ray_index % some == i, pltpu.roll(wide_ids, i * per_ray, 1), moved)
    tiles_own = entries // LANES
    id_rows = [
        jnp.sum(moved[q * some : (q + 1) * some], axis=0, keepdims=True) for q in range(tiles_own)
    ]

    earlier = one_hot(iota((LANES, LANES), 0) < iota((LANES, LANES), 1))
    taken = jnp.zeros((n, 1), jnp.float32)
    positions = []
    load.wait()
    for q, ids in enumerate(id_rows):
        at = slice(q * LANES, (q + 1) * LANES)
        slab_row = jnp.floor(ids * (1.0 / cells))
        inside = ids - slab_row * cells
        row_i = jnp.floor(inside * (1.0 / NY))
        owner = slab_row == iota((n, LANES), 0)
        counts = jnp.dot(one_hot(owner), earlier, preferred_element_type=jnp.float32) + taken
        rank = jnp.sum(jnp.where(owner, counts, 0.0), axis=0, keepdims=True)
        taken = taken + jnp.sum(jnp.where(owner, 1.0, 0.0), axis=1, keepdims=True)
        positions.append(slab_row * ps + rank)
        ray_row = jnp.floor(iota((1, LANES), 1) * (1.0 / per_ray)) + float(q * some)
        kind = iota((2 * PAD, LANES), 0)
        facts = jnp.where(kind == 0.0, row_i, 0.0)
        facts = jnp.where(kind == 1.0, inside - row_i * NY, facts)
        facts = jnp.where(kind == 2.0, ray_row, facts)
        pieces[: 2 * LANES, at] = two_parts(kern_rows[at, :].T)
        pieces[2 * LANES :, at] = facts.astype(jnp.bfloat16)
    position = jnp.concatenate(positions, axis=1)
    acc[...] = jnp.zeros_like(acc)
    pl.semaphore_wait(barrier, nd - 1)

    def rows_to(dest):
        pairs = ((send, recv, ssem, rsem), (facts_out, facts_in, fssem, frsem))
        return [
            pltpu.make_async_remote_copy(
                src_ref=a.at[dest], dst_ref=b.at[me], send_sem=left.at[0], recv_sem=landed.at[me],
                device_id=place(dest), device_id_type=MESH,
            )
            for a, b, left, landed in pairs
        ]

    def sort_tile(k, c):
        t = lax.rem(s // g + cpg // 2 + k, cpg)
        pm = one_hot(iota((LANES, entries), 0) + (t * LANES).astype(jnp.float32) == position)
        both = lax.dot_general(
            pieces[...], pm, (((1,), (1,)), ((), ())), preferred_element_type=jnp.float32
        )
        rows = both[:LANES] + both[LANES : 2 * LANES]
        tile = both[2 * LANES : 2 * LANES + PAD]
        code = (tile[2:3] * CX + tile[0:1]) * NY + tile[1:2]
        code = jnp.broadcast_to(code, (PAD, LANES))
        for j in range(g):
            part = code if j == 0 else pltpu.roll(code, LANES - j * ps, 1)
            block = rows if j == 0 else pltpu.roll(rows, LANES - j * ps, 1)
            for i in range(ne):
                dest = i * n + t * g + j
                send[dest] = block[i * cw : (i + 1) * cw]
                facts_out[dest, 0:1] = part[0:1]
                facts_out[dest, 1:2] = delay_wide[...]

                @pl.when(dest != me)
                def _():
                    for copy in rows_to(dest):
                        copy.start()

        return c

    lax.fori_loop(0, cpg, sort_tile, 0)
    recv[me] = send[me]
    facts_in[me] = facts_out[me]

    def chunk(cc):
        delay_rows = []
        for j in range(g):
            slot = cc * g + j

            @pl.when(slot != me)
            def _():
                for ref, left, landed in ((recv, ssem, rsem), (facts_in, fssem, frsem)):
                    pltpu.make_async_remote_copy(
                        src_ref=ref.at[slot], dst_ref=ref.at[slot], send_sem=left.at[0],
                        recv_sem=landed.at[slot], device_id=(e, s), device_id_type=MESH,
                    ).wait_recv()

            delay_rows.append(facts_in[slot, 1:2])
            u_ref[pl.ds(slot, 1), :] = delay_rows[-1]
        block = recv[cc * g]
        code = jnp.broadcast_to(facts_in[cc * g, 0:1], (PAD, LANES))
        at_lane = lax.broadcasted_iota(jnp.int32, (1, LANES), 1) // ps
        for j in range(1, g):
            other = jnp.broadcast_to(facts_in[cc * g + j, 0:1], (PAD, LANES))
            block = jnp.where(at_lane == j, pltpu.roll(recv[cc * g + j], j * ps, 1), block)
            code = jnp.where(at_lane == j, pltpu.roll(other, j * ps, 1), code)
        code = code[0:1]
        ray = jnp.floor(code * (1.0 / cells))
        inside = code - ray * cells
        plane = jnp.floor(inside * (1.0 / NY))
        first = pl.multiple_of(cc * LANES, LANES)
        kt[:, pl.ds(first, LANES)] = block
        plane_ref[:, pl.ds(first, LANES)] = plane
        rr_ref[pl.ds(cc, 1), :] = ray
        hot = one_hot(iota((NY, LANES), 0) == inside - plane * NY)
        s_mat[:, pl.ds(first, LANES)] = hot
        return ray, delay_rows, hot, block, plane

    def by_plane(rows, plane):
        high = rows.astype(jnp.bfloat16).astype(jnp.float32)
        both = jnp.concatenate([high, rows - high], axis=0)
        return jnp.concatenate(
            [jnp.where(plane == float(i), both, 0.0).astype(jnp.bfloat16) for i in range(CX)], axis=0
        )

    def add_rows(terms, hot):
        acc[...] += lax.dot_general(
            terms, hot, (((1,), (1,)), ((), ())), preferred_element_type=jnp.float32
        )

    def spread(ray, weights):
        lane = lax.broadcasted_iota(jnp.int32, ray.shape, 1)
        result = jnp.zeros(ray.shape, jnp.float32)
        for j in range(g):
            mine = jnp.zeros(ray.shape, jnp.float32)
            for r in range(rays):
                mine = jnp.where(ray == float(r), weights[j][:, r : r + 1], mine)
            result = jnp.where(lane // ps == j, mine, result)
        return result

    def arrivals(k, c):
        inner = lax.rem(s // g - cpg // 2 - k + 2 * cpg, cpg)
        chunks = [lax.rem(e + j, ne) * cpg + inner for j in range(ne)]
        found = [chunk(cc) for cc in chunks]
        ray = jnp.concatenate([f[0] for f in found], axis=0)
        weights = [jnp.concatenate([f[1][j] for f in found], axis=0) for j in range(g)]
        w = spread(ray, weights)
        terms = [
            by_plane(f[3] * w[j : j + 1], f[4]) for j, f in enumerate(found)
        ]
        add_rows(jnp.concatenate(terms, axis=1), jnp.concatenate([f[2] for f in found], axis=1))
        return c

    lax.fori_loop(0, cpg, arrivals, 0)

    delays = u_ref[...]
    beta0 = jnp.sqrt(total(delays * delays) + norm_epsilon)
    u0 = delays / beta0
    lane = lax.broadcasted_iota(jnp.int32, (nc, LANES), 1)

    def rays_of(j):
        return pl.ds(j, nc, stride=g) if g > 1 else pl.ds(0, nc)

    wide = 4 * LANES

    def scatter_rays():
        w_ref[:nc] = spread(rr_ref[...], [u_ref[rays_of(j), :] for j in range(g)])
        acc[...] = jnp.zeros_like(acc)

        def block(b, c):
            at = pl.ds(pl.multiple_of(b * wide, wide), wide)
            w = jnp.concatenate([w_ref[pl.ds(b * 4 + i, 1), :] for i in range(4)], axis=1)
            add_rows(by_plane(kt[:, at] * w, plane_ref[:, at]), s_mat[:, at])
            return c

        lax.fori_loop(0, nc // 4, block, 0)

    def scattered(p):
        return acc[2 * cw * p : 2 * cw * p + cw] + acc[2 * cw * p + cw : 2 * cw * (p + 1)]

    def laplace(ref, p):
        x = ref[p, PAD : PAD + cw]
        row = lax.broadcasted_iota(jnp.int32, x.shape, 0) + e * cw
        col = lax.broadcasted_iota(jnp.int32, x.shape, 1)
        beside = ref[p + 1, PAD : PAD + cw] + ref[p - 1, PAD : PAD + cw]
        beside = beside + jnp.where(col < NY - 1, pltpu.roll(x, NY - 1, 1), 0.0)
        beside = beside + jnp.where(col > 0, pltpu.roll(x, 1, 1), 0.0)
        beside = beside + jnp.where(row < cw * ne - 1, ref[p, PAD + 1 : PAD + cw + 1], 0.0)
        beside = beside + jnp.where(row > 0, ref[p, PAD - 1 : PAD + cw - 1], 0.0)
        return 6.0 * x - beside

    def halo(ref, r):
        own, planes = pl.ds(PAD, cw), pl.ds(1, CX)
        moves = [
            (ref.at[CX, own], ref.at[0, own], (e, lax.rem(s + 1, n))),
            (ref.at[1, own], ref.at[CX + 1, own], (e, lax.rem(s - 1 + n, n))),
            (ref.at[planes, pl.ds(cw, PAD)], ref.at[planes, pl.ds(0, PAD)], (lax.rem(e + 1, ne), s)),
            (
                ref.at[planes, pl.ds(PAD, PAD)],
                ref.at[planes, pl.ds(PAD + cw, PAD)],
                (lax.rem(e - 1 + ne, ne), s),
            ),
        ]
        copies = [
            pltpu.make_async_remote_copy(
                src_ref=a, dst_ref=b, send_sem=halo_send.at[4 * r + i],
                recv_sem=halo_recv.at[4 * r + i], device_id=to, device_id_type=MESH,
            )
            for i, (a, b, to) in enumerate(moves)
        ]
        for copy in copies:
            copy.start()
        return copies

    def gather_parts(full, r):
        copies = [
            pltpu.make_async_remote_copy(
                src_ref=full.at[e], dst_ref=full.at[e], send_sem=full_send.at[ne * r + j],
                recv_sem=full_recv.at[r], device_id=(lax.rem(e + j, ne), s), device_id_type=MESH,
            )
            for j in range(1, ne)
        ]
        for copy in copies:
            copy.start()
        return copies

    def share(tiles, squares, r):
        lane = lax.broadcasted_iota(jnp.int32, (PAD, LANES), 1)
        rows = jnp.zeros((PAD, LANES), jnp.float32)
        for i, square in enumerate(squares):
            rows = jnp.where(lane == i, square, rows)
        tiles[s, packed:] = rows
        return spread_out(tiles, n, s, lambda t: (e, t), 2 * r)

    def spread_out(tiles, count, mine, device, sem):
        def copy(ref, to):
            return pltpu.make_async_remote_copy(
                src_ref=ref, dst_ref=ref, send_sem=bsend.at[sem], recv_sem=brecv.at[sem],
                device_id=to, device_id_type=MESH,
            )

        for k in range(1, count):
            copy(tiles.at[mine], device(lax.rem(mine + k, count))).start()
        return copy(tiles.at[pl.ds(0, count - 1)], (e, s))

    def finish_share(tiles, sums, r, first, after):
        first.wait_recv()
        sums[e] = tile_sum(tiles, n)
        second = spread_out(sums, ne, e, lambda t: (t, s), 2 * r + 1)
        started = after()
        second.wait_recv()
        return tile_sum(sums, ne), second, started

    def tile_sum(tiles, count):
        parts = [tiles[k] for k in range(count)]
        while len(parts) > 1:
            odd = parts[len(parts) // 2 * 2 :]
            parts = [a + b for a, b in zip(parts[::2], parts[1::2])] + odd
        return parts[0]

    def apply_rays(tiles):
        def block(b, c):
            at = pl.ds(pl.multiple_of(b * wide, wide), wide)
            picked = jnp.dot(table2[...], s_mat[:, at], preferred_element_type=jnp.float32)
            plane = plane_ref[:, at]
            mine = picked[: 2 * cw]
            for i in range(1, CX):
                mine = jnp.where(plane == float(i), picked[2 * cw * i : 2 * cw * (i + 1)], mine)
            sums = jnp.sum((mine[:cw] + mine[cw:]) * kt[:, at], axis=0, keepdims=True)
            for i in range(4):
                e_ref[pl.ds(b * 4 + i, 1), :] = sums[:, i * LANES : (i + 1) * LANES]
            return c

        lax.fori_loop(0, nc // 4, block, 0)
        ray = rr_ref[...]
        for j in range(g):
            terms = jnp.where(lane // ps == j, e_ref[...], 0.0)
            value = jnp.zeros((nc, LANES), jnp.float32)
            for r in range(rays):
                one = jnp.sum(jnp.where(ray == float(r), terms, 0.0), axis=1, keepdims=True)
                value = jnp.where(lane == r, one, value)
            w_ref[rays_of(j), :] = value
        value = w_ref[:packed]
        for q in range(1, pack):
            value = value + pltpu.roll(w_ref[q * packed : (q + 1) * packed], q * rays, 1)
        tiles[s, :packed] = value

    def ray_sums(value):
        parts = [value] + [pltpu.roll(value, LANES - q * rays, 1) for q in range(1, pack)]
        value = jnp.concatenate(parts, axis=0)
        return jnp.where(lax.broadcasted_iota(jnp.int32, value.shape, 1) < rays, value, 0.0)

    def nothing():
        return jnp.zeros((cw, NY), jnp.float32)

    square = nothing()
    for p in range(CX):
        value = scattered(p) / beta0
        d0[p + 1, PAD : PAD + cw] = value
        full0[e, p] = value
        table2[2 * cw * p : 2 * cw * (p + 1)] = two_parts(value)
        square = square + value * value
    halos0 = halo(d0, 0)
    apply_rays(y0)
    for copy in halos0:
        copy.wait()
    curved = nothing()
    for p in range(CX):
        value = laplace(d0, p + 1)
        m1[p + 1, PAD : PAD + cw] = value
        curved = curved + value * value
    shared0 = share(y0, [total(square), total(curved)], 0)
    halos1 = halo(m1, 1)
    sums, passed0, gather0 = finish_share(y0, q0, 0, shared0, lambda: gather_parts(full0, 0))
    numbers = sums[packed : packed + 1]
    alpha0 = jnp.sqrt(numbers[:, 0:1] + norm_epsilon)
    curved0 = numbers[:, 1:2]

    u1 = ray_sums(sums[:packed]) / alpha0 - alpha0 * u0
    u_ref[...] = u1
    model_square = damping * damping * (curved0 / (alpha0 * alpha0))
    beta1 = jnp.sqrt(total(u1 * u1) + model_square + norm_epsilon)
    scale1 = damping / alpha0 / beta1
    scatter_rays()
    for copy in halos1:
        copy.wait()
    square = nothing()
    for p in range(CX):
        value = scattered(p) / beta1 + damping * scale1 * laplace(m1, p + 1)
        value = value - beta1 / alpha0 * d0[p + 1, PAD : PAD + cw]
        d1[p + 1, PAD : PAD + cw] = value
        full1[e, p] = value
        table2[2 * cw * p : 2 * cw * (p + 1)] = two_parts(value)
        square = square + value * value
    halos2 = halo(d1, 2)
    gather1 = gather_parts(full1, 1)
    apply_rays(y1)
    for copy in halos2:
        copy.wait()
    curved = nothing()
    cross = nothing()
    for p in range(CX):
        value = laplace(d1, p + 1)
        curved = curved + value * value
        cross = cross + value * m1[p + 1, PAD : PAD + cw]
    shared1 = share(y1, [total(square), total(curved), total(cross)], 1)
    rho1 = jnp.sqrt(alpha0 * alpha0 + beta1 * beta1)
    cosine1 = alpha0 / rho1
    sine1 = beta1 / rho1
    phi1 = cosine1 * beta0
    phi_bar = sine1 * beta0
    sums, passed1, _ = finish_share(y1, q1, 1, shared1, lambda: None)
    numbers = sums[packed : packed + 1]
    alpha1 = jnp.sqrt(numbers[:, 0:1] + norm_epsilon)
    theta1 = sine1 * alpha1
    rho_bar = -cosine1 * alpha1

    u2 = ray_sums(sums[:packed]) / alpha1 - alpha1 * (u1 / beta1)
    a, b = damping / alpha1, alpha1 * scale1
    model_square = a * a * numbers[:, 1:2] - 2.0 * a * b * numbers[:, 2:3] + b * b * curved0
    model_square = jnp.maximum(model_square, 0.0)
    beta2 = jnp.sqrt(total(u2 * u2) + model_square + norm_epsilon)
    rho2 = jnp.sqrt(rho_bar * rho_bar + beta2 * beta2)
    phi2 = rho_bar / rho2 * phi_bar

    for r, full in enumerate((full0, full1)):
        rest = full.at[pl.ds(0, ne - 1)]
        pltpu.make_async_remote_copy(
            src_ref=rest, dst_ref=rest, send_sem=full_send.at[ne * r], recv_sem=full_recv.at[r],
            device_id=(e, s), device_id_type=MESH,
        ).wait_recv()

    def finish(p, c):
        for i in range(ne):
            first = full0[i, p] / alpha0
            search = full1[i, p] / alpha1 - theta1 / rho1 * first
            out_ref[p, i * cw : (i + 1) * cw] = phi1 / rho1 * first + phi2 / rho2 * search
        return c

    lax.fori_loop(0, CX, finish, 0)

    rest = send.at[pl.ds(0, nd - 1)]
    pltpu.make_async_remote_copy(
        src_ref=rest, dst_ref=rest, send_sem=ssem.at[0], recv_sem=rsem.at[0],
        device_id=(e, s), device_id_type=MESH,
    ).wait_send()
    rest = facts_out.at[pl.ds(0, nd - 1)]
    pltpu.make_async_remote_copy(
        src_ref=rest, dst_ref=rest, send_sem=fssem.at[0], recv_sem=frsem.at[0],
        device_id=(e, s), device_id_type=MESH,
    ).wait_send()
    for copy in gather0 + gather1 + [shared0, shared1, passed0, passed1]:
        copy.wait_send()


def solution(mesh):
    ne, n = mesh.shape["ev"], mesh.shape["slab"]

    def on_device(kernels, block_ids, delays):
        rays, per_ray, width = kernels.shape
        entries = rays * per_ray
        ps = entries // n
        nd = ne * n
        cw = width // ne
        rows = nd * ps
        cells = CX * NY
        f32, bf16 = jnp.float32, jnp.bfloat16
        vmem = pl.BlockSpec(memory_space=pltpu.VMEM)
        model = pltpu.VMEM((CX + 2, cw + 2 * PAD, NY), f32)
        full = pltpu.VMEM((ne, CX, cw, NY), f32)
        high = nd * rays // LANES + PAD
        tiles = pltpu.VMEM((n, high, LANES), f32)
        tile_sums = pltpu.VMEM((ne, high, LANES), f32)
        small = pltpu.VMEM((rows // LANES, LANES), f32)
        by_device = pltpu.VMEM((nd, LANES), f32)
        result = pl.pallas_call(
            functools.partial(kernel, ne, n, ps, rays, cw),
            out_shape=jax.ShapeDtypeStruct((CX, width, NY), f32),
            in_specs=[pl.BlockSpec(memory_space=pl.ANY), vmem, vmem],
            out_specs=vmem,
            scratch_shapes=[
                pltpu.VMEM((entries, width), f32),
                pltpu.VMEM((nd, cw, LANES), f32),
                pltpu.VMEM((nd, cw, LANES), f32),
                pltpu.VMEM((nd, 2, LANES), f32),
                pltpu.VMEM((nd, 2, LANES), f32),
                pltpu.VMEM((2 * width + 2 * PAD, entries), bf16),
                pltpu.VMEM((NY, rows), bf16),
                pltpu.VMEM((cw, rows), f32),
                pltpu.VMEM((1, rows), f32),
                pltpu.VMEM((2 * cw * CX, NY), bf16),
                pltpu.VMEM((2 * cw * CX, NY), f32),
                small,
                by_device,
                small,
                by_device,
                pltpu.VMEM((rays, LANES), f32),
                pltpu.VMEM((1, LANES), f32),
                model, model, model, full, full, tiles, tiles, tile_sums, tile_sums,
                pltpu.SemaphoreType.DMA((1,)),
                pltpu.SemaphoreType.DMA((nd,)),
                pltpu.SemaphoreType.DMA((1,)),
                pltpu.SemaphoreType.DMA((nd,)),
                pltpu.SemaphoreType.DMA((12,)),
                pltpu.SemaphoreType.DMA((12,)),
                pltpu.SemaphoreType.DMA((2 * ne,)),
                pltpu.SemaphoreType.DMA((2,)),
                pltpu.SemaphoreType.DMA((4,)),
                pltpu.SemaphoreType.DMA((4,)),
                pltpu.SemaphoreType.DMA,
            ],
            compiler_params=pltpu.CompilerParams(
                collective_id=0, has_side_effects=True, vmem_limit_bytes=24 * 1024 * 1024
            ),
        )(kernels.reshape(entries, width), block_ids, delays.reshape(1, rays))
        return jnp.swapaxes(result, 1, 2)

    in_specs = (P(("ev", "slab"), None, None), P(("ev", "slab"), None), P(("ev", "slab")))
    return jax.shard_map(
        on_device, mesh=mesh, in_specs=in_specs, out_specs=P("slab", None, None), check_vma=False
    )
```

```python
import functools

import jax
import jax.numpy as jnp
from jax import lax
from jax.experimental import pallas as pl
from jax.experimental.pallas import tpu as pltpu
from jax.sharding import PartitionSpec as P

CX = 8
NY = 128
LANES = 128
MESH = pl.DeviceIdType.MESH

damping = 0.3
norm_epsilon = 1e-06


def iota(shape, dim):
    return lax.broadcasted_iota(jnp.int32, shape, dim).astype(jnp.float32)


def total(x):
    return jnp.sum(jnp.sum(x, axis=0, keepdims=True), axis=1, keepdims=True)


def one_hot(mask):
    return jnp.where(mask, 1.0, 0.0).astype(jnp.bfloat16)


def two_parts(x):
    high = x.astype(jnp.bfloat16)
    low = (x - high.astype(jnp.float32)).astype(jnp.bfloat16)
    return jnp.concatenate([high, low], axis=0)


PAD = 8


def kernel(
    ne, n, ps, rays, cw,
    kern_ref, ids_hbm, delay_hbm, out_ref,
    ids_ref, delay_ref,
    kern_rows, send, recv, facts_out, facts_in, pieces, s_mat, kt, plane_ref, table2, acc, rr_ref, w_ref, e_ref, u_ref,
    ids_wide, delay_wide, d0, m1, d1, full0, full1, y0, y1, q0, q1,
    ssem, rsem, fssem, frsem, halo_send, halo_recv, full_send, full_recv, bsend, brecv, load_sem,
):
    nd = ne * n
    g = LANES // ps
    cpg = n // g
    nc = nd // g
    entries = n * ps
    cells = CX * NY
    pack = LANES // rays
    packed = nd // pack
    e = lax.axis_index("ev")
    s = lax.axis_index("slab")
    me = e * n + s

    loads = [
        pltpu.make_async_copy(a, b, load_sem.at[i])
        for i, (a, b) in enumerate(((ids_hbm, ids_ref), (delay_hbm, delay_ref), (kern_ref, kern_rows)))
    ]
    for load in loads:
        load.start()
    barrier = pltpu.get_barrier_semaphore()

    def each_other(act):
        if nd <= 32:
            for k in range(1, nd):
                act(lax.rem(me + k, nd))
        else:

            def step(k, c):
                act(lax.rem(me + k, nd))
                return c

            lax.fori_loop(1, nd, step, 0)

    def place(device):
        return (device // n, lax.rem(device, n))

    each_other(
        lambda other: pl.semaphore_signal(
            barrier, inc=1, device_id=place(other), device_id_type=MESH
        )
    )

    per_ray = ids_ref.shape[1]
    loads[0].wait()
    loads[1].wait()
    some = LANES // per_ray
    ids_wide[...] = jnp.zeros_like(ids_wide)
    ids_wide[:, :per_ray] = ids_ref[...].astype(jnp.float32)
    delay_wide[...] = jnp.zeros_like(delay_wide)
    delay_wide[:, :rays] = delay_ref[...]
    wide_ids = ids_wide[...]
    ray_index = lax.broadcasted_iota(jnp.int32, wide_ids.shape, 0)
    moved = wide_ids
    for i in range(1, some):
        moved = jnp.where(ray_index % some == i, pltpu.roll(wide_ids, i * per_ray, 1), moved)
    tiles_own = entries // LANES
    id_rows = [
        jnp.sum(moved[q * some : (q + 1) * some], axis=0, keepdims=True) for q in range(tiles_own)
    ]

    earlier = one_hot(iota((LANES, LANES), 0) < iota((LANES, LANES), 1))
    taken = jnp.zeros((n, 1), jnp.float32)
    positions = []
    loads[2].wait()
    for q, ids in enumerate(id_rows):
        at = slice(q * LANES, (q + 1) * LANES)
        slab_row = jnp.floor(ids * (1.0 / cells))
        inside = ids - slab_row * cells
        row_i = jnp.floor(inside * (1.0 / NY))
        owner = slab_row == iota((n, LANES), 0)
        counts = jnp.dot(one_hot(owner), earlier, preferred_element_type=jnp.float32) + taken
        rank = jnp.sum(jnp.where(owner, counts, 0.0), axis=0, keepdims=True)
        taken = taken + jnp.sum(jnp.where(owner, 1.0, 0.0), axis=1, keepdims=True)
        positions.append(slab_row * ps + rank)
        ray_row = jnp.floor(iota((1, LANES), 1) * (1.0 / per_ray)) + float(q * some)
        kind = iota((2 * PAD, LANES), 0)
        facts = jnp.where(kind == 0.0, row_i, 0.0)
        facts = jnp.where(kind == 1.0, inside - row_i * NY, facts)
        facts = jnp.where(kind == 2.0, ray_row, facts)
        pieces[: 2 * LANES, at] = two_parts(kern_rows[at, :].T)
        pieces[2 * LANES :, at] = facts.astype(jnp.bfloat16)
    position = jnp.concatenate(positions, axis=1)
    acc[...] = jnp.zeros_like(acc)
    pl.semaphore_wait(barrier, nd - 1)

    def rows_to(dest):
        pairs = ((send, recv, ssem, rsem), (facts_out, facts_in, fssem, frsem))
        return [
            pltpu.make_async_remote_copy(
                src_ref=a.at[dest], dst_ref=b.at[me], send_sem=left.at[0], recv_sem=landed.at[me],
                device_id=place(dest), device_id_type=MESH,
            )
            for a, b, left, landed in pairs
        ]

    def sort_tile(k, c):
        t = lax.rem(s // g + cpg // 2 + k, cpg)
        pm = one_hot(iota((LANES, entries), 0) + (t * LANES).astype(jnp.float32) == position)
        both = lax.dot_general(
            pieces[...], pm, (((1,), (1,)), ((), ())), preferred_element_type=jnp.float32
        )
        rows = both[:LANES] + both[LANES : 2 * LANES]
        tile = both[2 * LANES : 2 * LANES + PAD]
        code = (tile[2:3] * CX + tile[0:1]) * NY + tile[1:2]
        code = jnp.broadcast_to(code, (PAD, LANES))
        for j in range(g):
            part = code if j == 0 else pltpu.roll(code, LANES - j * ps, 1)
            block = rows if j == 0 else pltpu.roll(rows, LANES - j * ps, 1)
            for i in range(ne):
                dest = i * n + t * g + j
                send[dest] = block[i * cw : (i + 1) * cw]
                facts_out[dest, 0:1] = part[0:1]
                facts_out[dest, 1:2] = delay_wide[...]

                @pl.when(dest != me)
                def _():
                    for copy in rows_to(dest):
                        copy.start()

        return c

    lax.fori_loop(0, cpg, sort_tile, 0)
    recv[me] = send[me]
    facts_in[me] = facts_out[me]

    def chunk(cc):
        delay_rows = []
        for j in range(g):
            slot = cc * g + j

            @pl.when(slot != me)
            def _():
                for ref, left, landed in ((recv, ssem, rsem), (facts_in, fssem, frsem)):
                    pltpu.make_async_remote_copy(
                        src_ref=ref.at[slot], dst_ref=ref.at[slot], send_sem=left.at[0],
                        recv_sem=landed.at[slot], device_id=(e, s), device_id_type=MESH,
                    ).wait_recv()

            delay_rows.append(facts_in[slot, 1:2])
            u_ref[pl.ds(slot, 1), :] = delay_rows[-1]
        block = recv[cc * g]
        code = jnp.broadcast_to(facts_in[cc * g, 0:1], (PAD, LANES))
        at_lane = lax.broadcasted_iota(jnp.int32, (1, LANES), 1) // ps
        for j in range(1, g):
            other = jnp.broadcast_to(facts_in[cc * g + j, 0:1], (PAD, LANES))
            block = jnp.where(at_lane == j, pltpu.roll(recv[cc * g + j], j * ps, 1), block)
            code = jnp.where(at_lane == j, pltpu.roll(other, j * ps, 1), code)
        code = code[0:1]
        ray = jnp.floor(code * (1.0 / cells))
        inside = code - ray * cells
        plane = jnp.floor(inside * (1.0 / NY))
        first = pl.multiple_of(cc * LANES, LANES)
        kt[:, pl.ds(first, LANES)] = block
        plane_ref[:, pl.ds(first, LANES)] = plane
        rr_ref[pl.ds(cc, 1), :] = ray
        hot = one_hot(iota((NY, LANES), 0) == inside - plane * NY)
        s_mat[:, pl.ds(first, LANES)] = hot
        return ray, delay_rows, hot, block, plane

    def by_plane(rows, plane):
        high = rows.astype(jnp.bfloat16).astype(jnp.float32)
        both = jnp.concatenate([high, rows - high], axis=0)
        return jnp.concatenate(
            [jnp.where(plane == float(i), both, 0.0).astype(jnp.bfloat16) for i in range(CX)], axis=0
        )

    def add_rows(terms, hot):
        acc[...] += lax.dot_general(
            terms, hot, (((1,), (1,)), ((), ())), preferred_element_type=jnp.float32
        )

    def spread(ray, weights):
        lane = lax.broadcasted_iota(jnp.int32, ray.shape, 1)
        result = jnp.zeros(ray.shape, jnp.float32)
        for j in range(g):
            mine = jnp.zeros(ray.shape, jnp.float32)
            for r in range(rays):
                mine = jnp.where(ray == float(r), weights[j][:, r : r + 1], mine)
            result = jnp.where(lane // ps == j, mine, result)
        return result

    def arrivals(k, c):
        inner = lax.rem(s // g - cpg // 2 - k + 2 * cpg, cpg)
        chunks = [lax.rem(e + j, ne) * cpg + inner for j in range(ne)]
        found = [chunk(cc) for cc in chunks]
        ray = jnp.concatenate([f[0] for f in found], axis=0)
        weights = [jnp.concatenate([f[1][j] for f in found], axis=0) for j in range(g)]
        w = spread(ray, weights)
        terms = [
            by_plane(f[3] * w[j : j + 1], f[4]) for j, f in enumerate(found)
        ]
        add_rows(jnp.concatenate(terms, axis=1), jnp.concatenate([f[2] for f in found], axis=1))
        return c

    lax.fori_loop(0, cpg, arrivals, 0)

    delays = u_ref[...]
    beta0 = jnp.sqrt(total(delays * delays) + norm_epsilon)
    u0 = delays / beta0
    lane = lax.broadcasted_iota(jnp.int32, (nc, LANES), 1)

    def rays_of(j):
        return pl.ds(j, nc, stride=g) if g > 1 else pl.ds(0, nc)

    wide = 4 * LANES

    def scatter_rays():
        w_ref[:nc] = spread(rr_ref[...], [u_ref[rays_of(j), :] for j in range(g)])
        acc[...] = jnp.zeros_like(acc)

        def block(b, c):
            at = pl.ds(pl.multiple_of(b * wide, wide), wide)
            w = jnp.concatenate([w_ref[pl.ds(b * 4 + i, 1), :] for i in range(4)], axis=1)
            add_rows(by_plane(kt[:, at] * w, plane_ref[:, at]), s_mat[:, at])
            return c

        lax.fori_loop(0, nc // 4, block, 0, unroll=True)

    def scattered(p):
        return acc[2 * cw * p : 2 * cw * p + cw] + acc[2 * cw * p + cw : 2 * cw * (p + 1)]

    def laplace(ref, p):
        x = ref[p, PAD : PAD + cw]
        row = lax.broadcasted_iota(jnp.int32, x.shape, 0) + e * cw
        col = lax.broadcasted_iota(jnp.int32, x.shape, 1)
        beside = ref[p + 1, PAD : PAD + cw] + ref[p - 1, PAD : PAD + cw]
        beside = beside + jnp.where(col < NY - 1, pltpu.roll(x, NY - 1, 1), 0.0)
        beside = beside + jnp.where(col > 0, pltpu.roll(x, 1, 1), 0.0)
        beside = beside + jnp.where(row < cw * ne - 1, ref[p, PAD + 1 : PAD + cw + 1], 0.0)
        beside = beside + jnp.where(row > 0, ref[p, PAD - 1 : PAD + cw - 1], 0.0)
        return 6.0 * x - beside

    def halo(ref, r):
        own, planes = pl.ds(PAD, cw), pl.ds(1, CX)
        moves = [
            (ref.at[CX, own], ref.at[0, own], (e, lax.rem(s + 1, n))),
            (ref.at[1, own], ref.at[CX + 1, own], (e, lax.rem(s - 1 + n, n))),
            (ref.at[planes, pl.ds(cw, PAD)], ref.at[planes, pl.ds(0, PAD)], (lax.rem(e + 1, ne), s)),
            (
                ref.at[planes, pl.ds(PAD, PAD)],
                ref.at[planes, pl.ds(PAD + cw, PAD)],
                (lax.rem(e - 1 + ne, ne), s),
            ),
        ]
        copies = [
            pltpu.make_async_remote_copy(
                src_ref=a, dst_ref=b, send_sem=halo_send.at[4 * r + i],
                recv_sem=halo_recv.at[4 * r + i], device_id=to, device_id_type=MESH,
            )
            for i, (a, b, to) in enumerate(moves)
        ]
        for copy in copies:
            copy.start()
        return copies

    def gather_parts(full, r):
        copies = [
            pltpu.make_async_remote_copy(
                src_ref=full.at[e], dst_ref=full.at[e], send_sem=full_send.at[ne * r + j],
                recv_sem=full_recv.at[r], device_id=(lax.rem(e + j, ne), s), device_id_type=MESH,
            )
            for j in range(1, ne)
        ]
        for copy in copies:
            copy.start()
        return copies

    def share(tiles, squares, r):
        lane = lax.broadcasted_iota(jnp.int32, (PAD, LANES), 1)
        rows = jnp.zeros((PAD, LANES), jnp.float32)
        for i, square in enumerate(squares):
            rows = jnp.where(lane == i, square, rows)
        tiles[s, packed:] = rows
        return spread_out(tiles, n, s, lambda t: (e, t), 2 * r)

    def spread_out(tiles, count, mine, device, sem):
        def copy(ref, to):
            return pltpu.make_async_remote_copy(
                src_ref=ref, dst_ref=ref, send_sem=bsend.at[sem], recv_sem=brecv.at[sem],
                device_id=to, device_id_type=MESH,
            )

        for k in range(1, count):
            copy(tiles.at[mine], device(lax.rem(mine + k, count))).start()
        return copy(tiles.at[pl.ds(0, count - 1)], (e, s))

    def finish_share(tiles, sums, r, first, after):
        first.wait_recv()
        sums[e] = tile_sum(tiles, n)
        second = spread_out(sums, ne, e, lambda t: (t, s), 2 * r + 1)
        started = after()
        second.wait_recv()
        return tile_sum(sums, ne), second, started

    def tile_sum(tiles, count):
        parts = [tiles[k] for k in range(count)]
        while len(parts) > 1:
            odd = parts[len(parts) // 2 * 2 :]
            parts = [a + b for a, b in zip(parts[::2], parts[1::2])] + odd
        return parts[0]

    def apply_rays(tiles):
        def block(b, c):
            at = pl.ds(pl.multiple_of(b * wide, wide), wide)
            picked = jnp.dot(table2[...], s_mat[:, at], preferred_element_type=jnp.float32)
            plane = plane_ref[:, at]
            mine = picked[: 2 * cw]
            for i in range(1, CX):
                mine = jnp.where(plane == float(i), picked[2 * cw * i : 2 * cw * (i + 1)], mine)
            sums = jnp.sum((mine[:cw] + mine[cw:]) * kt[:, at], axis=0, keepdims=True)
            for i in range(4):
                e_ref[pl.ds(b * 4 + i, 1), :] = sums[:, i * LANES : (i + 1) * LANES]
            return c

        lax.fori_loop(0, nc // 4, block, 0, unroll=True)
        ray = rr_ref[...]
        for j in range(g):
            terms = jnp.where(lane // ps == j, e_ref[...], 0.0)
            value = jnp.zeros((nc, LANES), jnp.float32)
            for r in range(rays):
                one = jnp.sum(jnp.where(ray == float(r), terms, 0.0), axis=1, keepdims=True)
                value = jnp.where(lane == r, one, value)
            w_ref[rays_of(j), :] = value
        value = w_ref[:packed]
        for q in range(1, pack):
            value = value + pltpu.roll(w_ref[q * packed : (q + 1) * packed], q * rays, 1)
        tiles[s, :packed] = value

    def ray_sums(value):
        parts = [value] + [pltpu.roll(value, LANES - q * rays, 1) for q in range(1, pack)]
        value = jnp.concatenate(parts, axis=0)
        return jnp.where(lax.broadcasted_iota(jnp.int32, value.shape, 1) < rays, value, 0.0)

    def nothing():
        return jnp.zeros((cw, NY), jnp.float32)

    per_beta = 1.0 / beta0
    square = nothing()
    for p in range(CX):
        value = scattered(p) * per_beta
        d0[p + 1, PAD : PAD + cw] = value
        full0[e, p] = value
        table2[2 * cw * p : 2 * cw * (p + 1)] = two_parts(value)
        square = square + value * value
    halos0 = halo(d0, 0)
    apply_rays(y0)
    for copy in halos0:
        copy.wait()
    curved = nothing()
    for p in range(CX):
        value = laplace(d0, p + 1)
        m1[p + 1, PAD : PAD + cw] = value
        curved = curved + value * value
    shared0 = share(y0, [total(square), total(curved)], 0)
    halos1 = halo(m1, 1)
    sums, passed0, gather0 = finish_share(y0, q0, 0, shared0, lambda: gather_parts(full0, 0))
    numbers = sums[packed : packed + 1]
    alpha0 = jnp.sqrt(numbers[:, 0:1] + norm_epsilon)
    curved0 = numbers[:, 1:2]

    u1 = ray_sums(sums[:packed]) / alpha0 - alpha0 * u0
    u_ref[...] = u1
    model_square = damping * damping * (curved0 / (alpha0 * alpha0))
    beta1 = jnp.sqrt(total(u1 * u1) + model_square + norm_epsilon)
    scale1 = damping / alpha0 / beta1
    per_beta, curve, back = 1.0 / beta1, damping * scale1, beta1 / alpha0
    scatter_rays()
    for copy in halos1:
        copy.wait()
    square = nothing()
    for p in range(CX):
        value = scattered(p) * per_beta + curve * laplace(m1, p + 1)
        value = value - back * d0[p + 1, PAD : PAD + cw]
        d1[p + 1, PAD : PAD + cw] = value
        full1[e, p] = value
        table2[2 * cw * p : 2 * cw * (p + 1)] = two_parts(value)
        square = square + value * value
    halos2 = halo(d1, 2)
    gather1 = gather_parts(full1, 1)
    apply_rays(y1)
    for copy in halos2:
        copy.wait()
    curved = nothing()
    cross = nothing()
    for p in range(CX):
        value = laplace(d1, p + 1)
        curved = curved + value * value
        cross = cross + value * m1[p + 1, PAD : PAD + cw]
    shared1 = share(y1, [total(square), total(curved), total(cross)], 1)
    rho1 = jnp.sqrt(alpha0 * alpha0 + beta1 * beta1)
    cosine1 = alpha0 / rho1
    sine1 = beta1 / rho1
    phi1 = cosine1 * beta0
    phi_bar = sine1 * beta0
    sums, passed1, _ = finish_share(y1, q1, 1, shared1, lambda: None)
    numbers = sums[packed : packed + 1]
    alpha1 = jnp.sqrt(numbers[:, 0:1] + norm_epsilon)
    theta1 = sine1 * alpha1
    rho_bar = -cosine1 * alpha1

    u2 = ray_sums(sums[:packed]) / alpha1 - alpha1 * (u1 / beta1)
    a, b = damping / alpha1, alpha1 * scale1
    model_square = a * a * numbers[:, 1:2] - 2.0 * a * b * numbers[:, 2:3] + b * b * curved0
    model_square = jnp.maximum(model_square, 0.0)
    beta2 = jnp.sqrt(total(u2 * u2) + model_square + norm_epsilon)
    rho2 = jnp.sqrt(rho_bar * rho_bar + beta2 * beta2)
    phi2 = rho_bar / rho2 * phi_bar

    for r, full in enumerate((full0, full1)):
        rest = full.at[pl.ds(0, ne - 1)]
        pltpu.make_async_remote_copy(
            src_ref=rest, dst_ref=rest, send_sem=full_send.at[ne * r], recv_sem=full_recv.at[r],
            device_id=(e, s), device_id_type=MESH,
        ).wait_recv()

    last = phi2 / rho2
    weight0 = (phi1 / rho1 - last * (theta1 / rho1)) / alpha0
    weight1 = last / alpha1
    for p in range(CX):
        for i in range(ne):
            out_ref[p, i * cw : (i + 1) * cw] = weight0 * full0[i, p] + weight1 * full1[i, p]

    rest = send.at[pl.ds(0, nd - 1)]
    pltpu.make_async_remote_copy(
        src_ref=rest, dst_ref=rest, send_sem=ssem.at[0], recv_sem=rsem.at[0],
        device_id=(e, s), device_id_type=MESH,
    ).wait_send()
    rest = facts_out.at[pl.ds(0, nd - 1)]
    pltpu.make_async_remote_copy(
        src_ref=rest, dst_ref=rest, send_sem=fssem.at[0], recv_sem=frsem.at[0],
        device_id=(e, s), device_id_type=MESH,
    ).wait_send()
    for copy in gather0 + gather1 + [shared0, shared1, passed0, passed1]:
        copy.wait_send()


def solution(mesh):
    ne, n = mesh.shape["ev"], mesh.shape["slab"]

    def on_device(kernels, block_ids, delays):
        rays, per_ray, width = kernels.shape
        entries = rays * per_ray
        ps = entries // n
        nd = ne * n
        cw = width // ne
        rows = nd * ps
        cells = CX * NY
        f32, bf16 = jnp.float32, jnp.bfloat16
        vmem = pl.BlockSpec(memory_space=pltpu.VMEM)
        model = pltpu.VMEM((CX + 2, cw + 2 * PAD, NY), f32)
        full = pltpu.VMEM((ne, CX, cw, NY), f32)
        high = nd * rays // LANES + PAD
        tiles = pltpu.VMEM((n, high, LANES), f32)
        tile_sums = pltpu.VMEM((ne, high, LANES), f32)
        small = pltpu.VMEM((rows // LANES, LANES), f32)
        by_device = pltpu.VMEM((nd, LANES), f32)
        result = pl.pallas_call(
            functools.partial(kernel, ne, n, ps, rays, cw),
            out_shape=jax.ShapeDtypeStruct((CX, width, NY), f32),
            in_specs=[pl.BlockSpec(memory_space=pltpu.HBM)] * 3,
            out_specs=vmem,
            scratch_shapes=[
                pltpu.VMEM((rays, per_ray), jnp.int32),
                pltpu.VMEM((1, rays), f32),
                pltpu.VMEM((entries, width), f32),
                pltpu.VMEM((nd, cw, LANES), f32),
                pltpu.VMEM((nd, cw, LANES), f32),
                pltpu.VMEM((nd, 2, LANES), f32),
                pltpu.VMEM((nd, 2, LANES), f32),
                pltpu.VMEM((2 * width + 2 * PAD, entries), bf16),
                pltpu.VMEM((NY, rows), bf16),
                pltpu.VMEM((cw, rows), f32),
                pltpu.VMEM((1, rows), f32),
                pltpu.VMEM((2 * cw * CX, NY), bf16),
                pltpu.VMEM((2 * cw * CX, NY), f32),
                small,
                by_device,
                small,
                by_device,
                pltpu.VMEM((rays, LANES), f32),
                pltpu.VMEM((1, LANES), f32),
                model, model, model, full, full, tiles, tiles, tile_sums, tile_sums,
                pltpu.SemaphoreType.DMA((1,)),
                pltpu.SemaphoreType.DMA((nd,)),
                pltpu.SemaphoreType.DMA((1,)),
                pltpu.SemaphoreType.DMA((nd,)),
                pltpu.SemaphoreType.DMA((12,)),
                pltpu.SemaphoreType.DMA((12,)),
                pltpu.SemaphoreType.DMA((2 * ne,)),
                pltpu.SemaphoreType.DMA((2,)),
                pltpu.SemaphoreType.DMA((4,)),
                pltpu.SemaphoreType.DMA((4,)),
                pltpu.SemaphoreType.DMA((3,)),
            ],
            compiler_params=pltpu.CompilerParams(
                collective_id=0, has_side_effects=True, vmem_limit_bytes=60 * 1024 * 1024
            ),
        )(kernels.reshape(entries, width), block_ids, delays.reshape(1, rays))
        return jnp.swapaxes(result, 1, 2)

    in_specs = (P(("ev", "slab"), None, None), P(("ev", "slab"), None), P(("ev", "slab")))
    return jax.shard_map(
        on_device, mesh=mesh, in_specs=in_specs, out_specs=P("slab", None, None), check_vma=False
    )
```

```python
import functools

import jax
import jax.numpy as jnp
from jax import lax
from jax.experimental import pallas as pl
from jax.experimental.pallas import tpu as pltpu
from jax.sharding import PartitionSpec as P

CX = 8
NY = 128
LANES = 128
MESH = pl.DeviceIdType.MESH

damping = 0.3
norm_epsilon = 1e-06


def iota(shape, dim):
    return lax.broadcasted_iota(jnp.int32, shape, dim).astype(jnp.float32)


def total(x):
    return jnp.sum(jnp.sum(x, axis=0, keepdims=True), axis=1, keepdims=True)


def one_hot(mask):
    return jnp.where(mask, 1.0, 0.0).astype(jnp.bfloat16)


def two_parts(x):
    high = x.astype(jnp.bfloat16)
    low = (x - high.astype(jnp.float32)).astype(jnp.bfloat16)
    return jnp.concatenate([high, low], axis=0)


PAD = 8


def kernel(
    ne, n, ps, rays, cw,
    kern_ref, ids_hbm, delay_hbm, out_ref,
    ids_ref, delay_ref,
    kern_rows, send, recv, facts_out, facts_in, pieces, s_mat, kt, plane_ref, table2, acc, rr_ref, w_ref, e_ref, u_ref,
    ids_wide, delay_wide, d0, m1, d1, full0, full1, y0, y1, q0, q1,
    ssem, rsem, fssem, frsem, halo_send, halo_recv, full_send, full_recv, bsend, brecv, load_sem,
):
    nd = ne * n
    g = LANES // ps
    cpg = n // g
    nc = nd // g
    entries = n * ps
    cells = CX * NY
    pack = LANES // rays
    packed = nd // pack
    e = lax.axis_index("ev")
    s = lax.axis_index("slab")
    me = e * n + s

    loads = [
        pltpu.make_async_copy(a, b, load_sem.at[i])
        for i, (a, b) in enumerate(((ids_hbm, ids_ref), (delay_hbm, delay_ref), (kern_ref, kern_rows)))
    ]
    for load in loads:
        load.start()
    barrier = pltpu.get_barrier_semaphore()

    def each_other(act):
        if nd <= 32:
            for k in range(1, nd):
                act(lax.rem(me + k, nd))
        else:

            def step(k, c):
                act(lax.rem(me + k, nd))
                return c

            lax.fori_loop(1, nd, step, 0)

    def place(device):
        return (device // n, lax.rem(device, n))

    each_other(
        lambda other: pl.semaphore_signal(
            barrier, inc=1, device_id=place(other), device_id_type=MESH
        )
    )

    per_ray = ids_ref.shape[1]
    loads[0].wait()
    loads[1].wait()
    some = LANES // per_ray
    ids_wide[...] = jnp.zeros_like(ids_wide)
    ids_wide[:, :per_ray] = ids_ref[...].astype(jnp.float32)
    delay_wide[...] = jnp.zeros_like(delay_wide)
    delay_wide[:, :rays] = delay_ref[...]
    wide_ids = ids_wide[...]
    ray_index = lax.broadcasted_iota(jnp.int32, wide_ids.shape, 0)
    moved = wide_ids
    for i in range(1, some):
        moved = jnp.where(ray_index % some == i, pltpu.roll(wide_ids, i * per_ray, 1), moved)
    tiles_own = entries // LANES
    id_rows = [
        jnp.sum(moved[q * some : (q + 1) * some], axis=0, keepdims=True) for q in range(tiles_own)
    ]

    earlier = one_hot(iota((LANES, LANES), 0) < iota((LANES, LANES), 1))
    taken = jnp.zeros((n, 1), jnp.float32)
    positions = []
    loads[2].wait()
    for q, ids in enumerate(id_rows):
        at = slice(q * LANES, (q + 1) * LANES)
        slab_row = jnp.floor(ids * (1.0 / cells))
        inside = ids - slab_row * cells
        row_i = jnp.floor(inside * (1.0 / NY))
        owner = slab_row == iota((n, LANES), 0)
        counts = jnp.dot(one_hot(owner), earlier, preferred_element_type=jnp.float32) + taken
        rank = jnp.sum(jnp.where(owner, counts, 0.0), axis=0, keepdims=True)
        taken = taken + jnp.sum(jnp.where(owner, 1.0, 0.0), axis=1, keepdims=True)
        positions.append(slab_row * ps + rank)
        ray_row = jnp.floor(iota((1, LANES), 1) * (1.0 / per_ray)) + float(q * some)
        kind = iota((2 * PAD, LANES), 0)
        facts = jnp.where(kind == 0.0, row_i, 0.0)
        facts = jnp.where(kind == 1.0, inside - row_i * NY, facts)
        facts = jnp.where(kind == 2.0, ray_row, facts)
        pieces[: 2 * LANES, at] = two_parts(kern_rows[at, :].T)
        pieces[2 * LANES :, at] = facts.astype(jnp.bfloat16)
    position = jnp.concatenate(positions, axis=1)
    acc[...] = jnp.zeros_like(acc)
    pl.semaphore_wait(barrier, nd - 1)

    def rows_to(dest):
        pairs = ((send, recv, ssem, rsem), (facts_out, facts_in, fssem, frsem))
        return [
            pltpu.make_async_remote_copy(
                src_ref=a.at[dest], dst_ref=b.at[me], send_sem=left.at[0], recv_sem=landed.at[me],
                device_id=place(dest), device_id_type=MESH,
            )
            for a, b, left, landed in pairs
        ]

    def sort_tile(k, c):
        t = lax.rem(s // g + cpg // 2 + k, cpg)
        pm = one_hot(iota((LANES, entries), 0) + (t * LANES).astype(jnp.float32) == position)
        both = lax.dot_general(
            pieces[...], pm, (((1,), (1,)), ((), ())), preferred_element_type=jnp.float32
        )
        rows = both[:LANES] + both[LANES : 2 * LANES]
        tile = both[2 * LANES : 2 * LANES + PAD]
        code = (tile[2:3] * CX + tile[0:1]) * NY + tile[1:2]
        code = jnp.broadcast_to(code, (PAD, LANES))
        for j in range(g):
            part = code if j == 0 else pltpu.roll(code, LANES - j * ps, 1)
            block = rows if j == 0 else pltpu.roll(rows, LANES - j * ps, 1)
            for i in range(ne):
                dest = i * n + t * g + j
                send[dest] = block[i * cw : (i + 1) * cw]
                facts_out[dest, 0:1] = part[0:1]
                facts_out[dest, 1:2] = delay_wide[...]

                @pl.when(dest != me)
                def _():
                    for copy in rows_to(dest):
                        copy.start()

        return c

    lax.fori_loop(0, cpg, sort_tile, 0)
    recv[me] = send[me]
    facts_in[me] = facts_out[me]

    def chunk(cc):
        delay_rows = []
        for j in range(g):
            slot = cc * g + j

            @pl.when(slot != me)
            def _():
                for ref, left, landed in ((recv, ssem, rsem), (facts_in, fssem, frsem)):
                    pltpu.make_async_remote_copy(
                        src_ref=ref.at[slot], dst_ref=ref.at[slot], send_sem=left.at[0],
                        recv_sem=landed.at[slot], device_id=(e, s), device_id_type=MESH,
                    ).wait_recv()

            delay_rows.append(facts_in[slot, 1:2])
            u_ref[pl.ds(slot, 1), :] = delay_rows[-1]
        block = recv[cc * g]
        code = jnp.broadcast_to(facts_in[cc * g, 0:1], (PAD, LANES))
        at_lane = lax.broadcasted_iota(jnp.int32, (1, LANES), 1) // ps
        for j in range(1, g):
            other = jnp.broadcast_to(facts_in[cc * g + j, 0:1], (PAD, LANES))
            block = jnp.where(at_lane == j, pltpu.roll(recv[cc * g + j], j * ps, 1), block)
            code = jnp.where(at_lane == j, pltpu.roll(other, j * ps, 1), code)
        code = code[0:1]
        ray = jnp.floor(code * (1.0 / cells))
        inside = code - ray * cells
        plane = jnp.floor(inside * (1.0 / NY))
        first = pl.multiple_of(cc * LANES, LANES)
        kt[:, pl.ds(first, LANES)] = block
        plane_ref[:, pl.ds(first, LANES)] = plane
        rr_ref[pl.ds(cc, 1), :] = ray
        hot = one_hot(iota((NY, LANES), 0) == inside - plane * NY)
        s_mat[:, pl.ds(first, LANES)] = hot
        return ray, delay_rows, hot, block, plane

    def by_plane(rows, plane):
        high = rows.astype(jnp.bfloat16).astype(jnp.float32)
        both = jnp.concatenate([high, rows - high], axis=0)
        return jnp.concatenate(
            [jnp.where(plane == float(i), both, 0.0).astype(jnp.bfloat16) for i in range(CX)], axis=0
        )

    def add_rows(terms, hot):
        acc[...] += lax.dot_general(
            terms, hot, (((1,), (1,)), ((), ())), preferred_element_type=jnp.float32
        )

    def spread(ray, weights):
        lane = lax.broadcasted_iota(jnp.int32, ray.shape, 1)
        result = jnp.zeros(ray.shape, jnp.float32)
        for j in range(g):
            mine = jnp.zeros(ray.shape, jnp.float32)
            for r in range(rays):
                mine = jnp.where(ray == float(r), weights[j][:, r : r + 1], mine)
            result = jnp.where(lane // ps == j, mine, result)
        return result

    def arrivals(k, c):
        inner = lax.rem(s // g - cpg // 2 - k + 2 * cpg, cpg)
        chunks = [lax.rem(e + j, ne) * cpg + inner for j in range(ne)]
        found = [chunk(cc) for cc in chunks]
        ray = jnp.concatenate([f[0] for f in found], axis=0)
        weights = [jnp.concatenate([f[1][j] for f in found], axis=0) for j in range(g)]
        w = spread(ray, weights)
        terms = [
            by_plane(f[3] * w[j : j + 1], f[4]) for j, f in enumerate(found)
        ]
        add_rows(jnp.concatenate(terms, axis=1), jnp.concatenate([f[2] for f in found], axis=1))
        return c

    lax.fori_loop(0, cpg, arrivals, 0)

    delays = u_ref[...]
    beta0 = jnp.sqrt(total(delays * delays) + norm_epsilon)
    u0 = delays / beta0
    lane = lax.broadcasted_iota(jnp.int32, (nc, LANES), 1)

    def rays_of(j):
        return pl.ds(j, nc, stride=g) if g > 1 else pl.ds(0, nc)

    wide = 4 * LANES

    def scatter_rays():
        w_ref[:nc] = spread(rr_ref[...], [u_ref[rays_of(j), :] for j in range(g)])
        acc[...] = jnp.zeros_like(acc)

        def block(b, c):
            at = pl.ds(pl.multiple_of(b * wide, wide), wide)
            w = jnp.concatenate([w_ref[pl.ds(b * 4 + i, 1), :] for i in range(4)], axis=1)
            add_rows(by_plane(kt[:, at] * w, plane_ref[:, at]), s_mat[:, at])
            return c

        lax.fori_loop(0, nc // 4, block, 0, unroll=True)

    def scattered(p):
        return acc[2 * cw * p : 2 * cw * p + cw] + acc[2 * cw * p + cw : 2 * cw * (p + 1)]

    def laplace(ref, p):
        x = ref[p, PAD : PAD + cw]
        row = lax.broadcasted_iota(jnp.int32, x.shape, 0) + e * cw
        col = lax.broadcasted_iota(jnp.int32, x.shape, 1)
        beside = ref[p + 1, PAD : PAD + cw] + ref[p - 1, PAD : PAD + cw]
        beside = beside + jnp.where(col < NY - 1, pltpu.roll(x, NY - 1, 1), 0.0)
        beside = beside + jnp.where(col > 0, pltpu.roll(x, 1, 1), 0.0)
        beside = beside + jnp.where(row < cw * ne - 1, ref[p, PAD + 1 : PAD + cw + 1], 0.0)
        beside = beside + jnp.where(row > 0, ref[p, PAD - 1 : PAD + cw - 1], 0.0)
        return 6.0 * x - beside

    def halo(ref, r):
        own, planes = pl.ds(PAD, cw), pl.ds(1, CX)
        moves = [
            (ref.at[CX, own], ref.at[0, own], (e, lax.rem(s + 1, n))),
            (ref.at[1, own], ref.at[CX + 1, own], (e, lax.rem(s - 1 + n, n))),
            (ref.at[planes, pl.ds(cw, PAD)], ref.at[planes, pl.ds(0, PAD)], (lax.rem(e + 1, ne), s)),
            (
                ref.at[planes, pl.ds(PAD, PAD)],
                ref.at[planes, pl.ds(PAD + cw, PAD)],
                (lax.rem(e - 1 + ne, ne), s),
            ),
        ]
        copies = [
            pltpu.make_async_remote_copy(
                src_ref=a, dst_ref=b, send_sem=halo_send.at[4 * r + i],
                recv_sem=halo_recv.at[4 * r + i], device_id=to, device_id_type=MESH,
            )
            for i, (a, b, to) in enumerate(moves)
        ]
        for copy in copies:
            copy.start()
        return copies

    def gather_parts(full, r):
        copies = [
            pltpu.make_async_remote_copy(
                src_ref=full.at[e], dst_ref=full.at[e], send_sem=full_send.at[ne * r + j],
                recv_sem=full_recv.at[r], device_id=(lax.rem(e + j, ne), s), device_id_type=MESH,
            )
            for j in range(1, ne)
        ]
        for copy in copies:
            copy.start()
        return copies

    def share(tiles, numbers, squares, r):
        lane = lax.broadcasted_iota(jnp.int32, (1, LANES), 1)
        row = jnp.zeros((1, LANES), jnp.float32)
        for i, square in enumerate(squares):
            row = jnp.where(lane == i, square, row)
        numbers[me] = row

        def copies(a, to):
            return [
                pltpu.make_async_remote_copy(
                    src_ref=ref.at[a], dst_ref=ref.at[a], send_sem=bsend.at[2 * r + i],
                    recv_sem=brecv.at[2 * r + i], device_id=to, device_id_type=MESH,
                )
                for i, ref in enumerate((tiles, numbers))
            ]

        def act(other):
            for copy in copies(me, place(other)):
                copy.start()

        each_other(act)
        return copies(pl.ds(0, nd - 1), (e, s))

    def tile_sum(tiles, count):
        parts = [tiles[k] for k in range(count)]
        while len(parts) > 1:
            odd = parts[len(parts) // 2 * 2 :]
            parts = [a + b for a, b in zip(parts[::2], parts[1::2])] + odd
        return parts[0]

    def apply_rays(tiles):
        def block(b, c):
            at = pl.ds(pl.multiple_of(b * wide, wide), wide)
            picked = jnp.dot(table2[...], s_mat[:, at], preferred_element_type=jnp.float32)
            plane = plane_ref[:, at]
            mine = picked[: 2 * cw]
            for i in range(1, CX):
                mine = jnp.where(plane == float(i), picked[2 * cw * i : 2 * cw * (i + 1)], mine)
            sums = jnp.sum((mine[:cw] + mine[cw:]) * kt[:, at], axis=0, keepdims=True)
            for i in range(4):
                e_ref[pl.ds(b * 4 + i, 1), :] = sums[:, i * LANES : (i + 1) * LANES]
            return c

        lax.fori_loop(0, nc // 4, block, 0, unroll=True)
        ray = rr_ref[...]
        for j in range(g):
            terms = jnp.where(lane // ps == j, e_ref[...], 0.0)
            value = jnp.zeros((nc, LANES), jnp.float32)
            for r in range(rays):
                one = jnp.sum(jnp.where(ray == float(r), terms, 0.0), axis=1, keepdims=True)
                value = jnp.where(lane == r, one, value)
            w_ref[rays_of(j), :] = value
        value = w_ref[:packed]
        for q in range(1, pack):
            value = value + pltpu.roll(w_ref[q * packed : (q + 1) * packed], q * rays, 1)
        tiles[me] = value

    def ray_sums(value):
        parts = [value] + [pltpu.roll(value, LANES - q * rays, 1) for q in range(1, pack)]
        value = jnp.concatenate(parts, axis=0)
        return jnp.where(lax.broadcasted_iota(jnp.int32, value.shape, 1) < rays, value, 0.0)

    def nothing():
        return jnp.zeros((cw, NY), jnp.float32)

    per_beta = 1.0 / beta0
    square = nothing()
    for p in range(CX):
        value = scattered(p) * per_beta
        d0[p + 1, PAD : PAD + cw] = value
        full0[e, p] = value
        table2[2 * cw * p : 2 * cw * (p + 1)] = two_parts(value)
        square = square + value * value
    halos0 = halo(d0, 0)
    apply_rays(y0)
    for copy in halos0:
        copy.wait()
    curved = nothing()
    for p in range(CX):
        value = laplace(d0, p + 1)
        m1[p + 1, PAD : PAD + cw] = value
        curved = curved + value * value
    shared0 = share(y0, q0, [total(square), total(curved)], 0)
    halos1 = halo(m1, 1)
    gather0 = gather_parts(full0, 0)
    for copy in shared0:
        copy.wait_recv()
    numbers = tile_sum(q0, nd)
    alpha0 = jnp.sqrt(numbers[:, 0:1] + norm_epsilon)
    curved0 = numbers[:, 1:2]

    u1 = ray_sums(tile_sum(y0, nd)) / alpha0 - alpha0 * u0
    u_ref[...] = u1
    model_square = damping * damping * (curved0 / (alpha0 * alpha0))
    beta1 = jnp.sqrt(total(u1 * u1) + model_square + norm_epsilon)
    scale1 = damping / alpha0 / beta1
    per_beta, curve, back = 1.0 / beta1, damping * scale1, beta1 / alpha0
    scatter_rays()
    for copy in halos1:
        copy.wait()
    square = nothing()
    for p in range(CX):
        value = scattered(p) * per_beta + curve * laplace(m1, p + 1)
        value = value - back * d0[p + 1, PAD : PAD + cw]
        d1[p + 1, PAD : PAD + cw] = value
        full1[e, p] = value
        table2[2 * cw * p : 2 * cw * (p + 1)] = two_parts(value)
        square = square + value * value
    halos2 = halo(d1, 2)
    gather1 = gather_parts(full1, 1)
    apply_rays(y1)
    for copy in halos2:
        copy.wait()
    curved = nothing()
    cross = nothing()
    for p in range(CX):
        value = laplace(d1, p + 1)
        curved = curved + value * value
        cross = cross + value * m1[p + 1, PAD : PAD + cw]
    shared1 = share(y1, q1, [total(square), total(curved), total(cross)], 1)
    rho1 = jnp.sqrt(alpha0 * alpha0 + beta1 * beta1)
    cosine1 = alpha0 / rho1
    sine1 = beta1 / rho1
    phi1 = cosine1 * beta0
    phi_bar = sine1 * beta0
    for copy in shared1:
        copy.wait_recv()
    numbers = tile_sum(q1, nd)
    alpha1 = jnp.sqrt(numbers[:, 0:1] + norm_epsilon)
    theta1 = sine1 * alpha1
    rho_bar = -cosine1 * alpha1

    u2 = ray_sums(tile_sum(y1, nd)) / alpha1 - alpha1 * (u1 / beta1)
    a, b = damping / alpha1, alpha1 * scale1
    model_square = a * a * numbers[:, 1:2] - 2.0 * a * b * numbers[:, 2:3] + b * b * curved0
    model_square = jnp.maximum(model_square, 0.0)
    beta2 = jnp.sqrt(total(u2 * u2) + model_square + norm_epsilon)
    rho2 = jnp.sqrt(rho_bar * rho_bar + beta2 * beta2)
    phi2 = rho_bar / rho2 * phi_bar

    for r, full in enumerate((full0, full1)):
        rest = full.at[pl.ds(0, ne - 1)]
        pltpu.make_async_remote_copy(
            src_ref=rest, dst_ref=rest, send_sem=full_send.at[ne * r], recv_sem=full_recv.at[r],
            device_id=(e, s), device_id_type=MESH,
        ).wait_recv()

    last = phi2 / rho2
    weight0 = (phi1 / rho1 - last * (theta1 / rho1)) / alpha0
    weight1 = last / alpha1
    for p in range(CX):
        for i in range(ne):
            out_ref[p, i * cw : (i + 1) * cw] = weight0 * full0[i, p] + weight1 * full1[i, p]

    rest = send.at[pl.ds(0, nd - 1)]
    pltpu.make_async_remote_copy(
        src_ref=rest, dst_ref=rest, send_sem=ssem.at[0], recv_sem=rsem.at[0],
        device_id=(e, s), device_id_type=MESH,
    ).wait_send()
    rest = facts_out.at[pl.ds(0, nd - 1)]
    pltpu.make_async_remote_copy(
        src_ref=rest, dst_ref=rest, send_sem=fssem.at[0], recv_sem=frsem.at[0],
        device_id=(e, s), device_id_type=MESH,
    ).wait_send()
    for copy in gather0 + gather1 + shared0 + shared1:
        copy.wait_send()


def solution(mesh):
    ne, n = mesh.shape["ev"], mesh.shape["slab"]

    def on_device(kernels, block_ids, delays):
        rays, per_ray, width = kernels.shape
        entries = rays * per_ray
        ps = entries // n
        nd = ne * n
        cw = width // ne
        rows = nd * ps
        cells = CX * NY
        f32, bf16 = jnp.float32, jnp.bfloat16
        vmem = pl.BlockSpec(memory_space=pltpu.VMEM)
        model = pltpu.VMEM((CX + 2, cw + 2 * PAD, NY), f32)
        full = pltpu.VMEM((ne, CX, cw, NY), f32)
        tiles = pltpu.VMEM((nd, nd * rays // LANES, LANES), f32)
        numbers = pltpu.VMEM((nd, 1, LANES), f32)
        small = pltpu.VMEM((rows // LANES, LANES), f32)
        by_device = pltpu.VMEM((nd, LANES), f32)
        result = pl.pallas_call(
            functools.partial(kernel, ne, n, ps, rays, cw),
            out_shape=jax.ShapeDtypeStruct((CX, width, NY), f32),
            in_specs=[pl.BlockSpec(memory_space=pltpu.HBM)] * 3,
            out_specs=vmem,
            scratch_shapes=[
                pltpu.VMEM((rays, per_ray), jnp.int32),
                pltpu.VMEM((1, rays), f32),
                pltpu.VMEM((entries, width), f32),
                pltpu.VMEM((nd, cw, LANES), f32),
                pltpu.VMEM((nd, cw, LANES), f32),
                pltpu.VMEM((nd, 2, LANES), f32),
                pltpu.VMEM((nd, 2, LANES), f32),
                pltpu.VMEM((2 * width + 2 * PAD, entries), bf16),
                pltpu.VMEM((NY, rows), bf16),
                pltpu.VMEM((cw, rows), f32),
                pltpu.VMEM((1, rows), f32),
                pltpu.VMEM((2 * cw * CX, NY), bf16),
                pltpu.VMEM((2 * cw * CX, NY), f32),
                small,
                by_device,
                small,
                by_device,
                pltpu.VMEM((rays, LANES), f32),
                pltpu.VMEM((1, LANES), f32),
                model, model, model, full, full, tiles, tiles, numbers, numbers,
                pltpu.SemaphoreType.DMA((1,)),
                pltpu.SemaphoreType.DMA((nd,)),
                pltpu.SemaphoreType.DMA((1,)),
                pltpu.SemaphoreType.DMA((nd,)),
                pltpu.SemaphoreType.DMA((12,)),
                pltpu.SemaphoreType.DMA((12,)),
                pltpu.SemaphoreType.DMA((2 * ne,)),
                pltpu.SemaphoreType.DMA((2,)),
                pltpu.SemaphoreType.DMA((4,)),
                pltpu.SemaphoreType.DMA((4,)),
                pltpu.SemaphoreType.DMA((3,)),
            ],
            compiler_params=pltpu.CompilerParams(
                collective_id=0, has_side_effects=True, vmem_limit_bytes=60 * 1024 * 1024
            ),
        )(kernels.reshape(entries, width), block_ids, delays.reshape(1, rays))
        return jnp.swapaxes(result, 1, 2)

    in_specs = (P(("ev", "slab"), None, None), P(("ev", "slab"), None), P(("ev", "slab")))
    return jax.shard_map(
        on_device, mesh=mesh, in_specs=in_specs, out_specs=P("slab", None, None), check_vma=False
    )
```

```python
import functools

import jax
import jax.numpy as jnp
from jax import lax
from jax.experimental import pallas as pl
from jax.experimental.pallas import tpu as pltpu
from jax.sharding import PartitionSpec as P

CX = 8
NY = 128
LANES = 128
MESH = pl.DeviceIdType.MESH

damping = 0.3
norm_epsilon = 1e-06


def iota(shape, dim):
    return lax.broadcasted_iota(jnp.int32, shape, dim).astype(jnp.float32)


def total(x):
    return jnp.sum(jnp.sum(x, axis=0, keepdims=True), axis=1, keepdims=True)


def one_hot(mask):
    return jnp.where(mask, 1.0, 0.0).astype(jnp.bfloat16)


def two_parts(x):
    high = x.astype(jnp.bfloat16)
    low = (x - high.astype(jnp.float32)).astype(jnp.bfloat16)
    return jnp.concatenate([high, low], axis=0)


PAD = 8


def kernel(
    ne, n, ps, rays, cw,
    kern_ref, ids_hbm, delay_hbm, out_ref,
    ids_ref, delay_ref,
    kern_rows, send, recv, facts_out, facts_in, pieces, s_mat, kt, plane_ref, table2, acc, rr_ref, w_ref, e_ref, u_ref,
    ids_wide, delay_wide, d0, m1, d1, full0, full1, y0, y1, q0, q1,
    ssem, rsem, fssem, frsem, halo_send, halo_recv, full_send, full_recv, bsend, brecv, load_sem,
):
    nd = ne * n
    g = LANES // ps
    cpg = n // g
    nc = nd // g
    entries = n * ps
    cells = CX * NY
    pack = LANES // rays
    packed = nd // pack
    e = lax.axis_index("ev")
    s = lax.axis_index("slab")
    me = e * n + s

    loads = [
        pltpu.make_async_copy(a, b, load_sem.at[i])
        for i, (a, b) in enumerate(((ids_hbm, ids_ref), (delay_hbm, delay_ref), (kern_ref, kern_rows)))
    ]
    for load in loads:
        load.start()
    barrier = pltpu.get_barrier_semaphore()

    def each_other(act):
        if nd <= 32:
            for k in range(1, nd):
                act(lax.rem(me + k, nd))
        else:

            def step(k, c):
                act(lax.rem(me + k, nd))
                return c

            lax.fori_loop(1, nd, step, 0)

    def place(device):
        return (device // n, lax.rem(device, n))

    each_other(
        lambda other: pl.semaphore_signal(
            barrier, inc=1, device_id=place(other), device_id_type=MESH
        )
    )

    per_ray = ids_ref.shape[1]
    loads[0].wait()
    loads[1].wait()
    some = LANES // per_ray
    ids_wide[...] = jnp.zeros_like(ids_wide)
    ids_wide[:, :per_ray] = ids_ref[...].astype(jnp.float32)
    delay_wide[...] = jnp.zeros_like(delay_wide)
    delay_wide[:, :rays] = delay_ref[...]
    wide_ids = ids_wide[...]
    ray_index = lax.broadcasted_iota(jnp.int32, wide_ids.shape, 0)
    moved = wide_ids
    for i in range(1, some):
        moved = jnp.where(ray_index % some == i, pltpu.roll(wide_ids, i * per_ray, 1), moved)
    tiles_own = entries // LANES
    id_rows = [
        jnp.sum(moved[q * some : (q + 1) * some], axis=0, keepdims=True) for q in range(tiles_own)
    ]

    earlier = one_hot(iota((LANES, LANES), 0) < iota((LANES, LANES), 1))
    taken = jnp.zeros((n, 1), jnp.float32)
    positions = []
    loads[2].wait()
    for q, ids in enumerate(id_rows):
        at = slice(q * LANES, (q + 1) * LANES)
        slab_row = jnp.floor(ids * (1.0 / cells))
        inside = ids - slab_row * cells
        row_i = jnp.floor(inside * (1.0 / NY))
        owner = slab_row == iota((n, LANES), 0)
        counts = jnp.dot(one_hot(owner), earlier, preferred_element_type=jnp.float32) + taken
        rank = jnp.sum(jnp.where(owner, counts, 0.0), axis=0, keepdims=True)
        taken = taken + jnp.sum(jnp.where(owner, 1.0, 0.0), axis=1, keepdims=True)
        positions.append(slab_row * ps + rank)
        ray_row = jnp.floor(iota((1, LANES), 1) * (1.0 / per_ray)) + float(q * some)
        kind = iota((2 * PAD, LANES), 0)
        facts = jnp.where(kind == 0.0, row_i, 0.0)
        facts = jnp.where(kind == 1.0, inside - row_i * NY, facts)
        facts = jnp.where(kind == 2.0, ray_row, facts)
        pieces[: 2 * LANES, at] = two_parts(kern_rows[at, :].T)
        pieces[2 * LANES :, at] = facts.astype(jnp.bfloat16)
    position = jnp.concatenate(positions, axis=1)
    acc[...] = jnp.zeros_like(acc)
    pl.semaphore_wait(barrier, nd - 1)

    def rows_to(dest):
        pairs = ((send, recv, ssem, rsem), (facts_out, facts_in, fssem, frsem))
        return [
            pltpu.make_async_remote_copy(
                src_ref=a.at[dest], dst_ref=b.at[me], send_sem=left.at[0], recv_sem=landed.at[me],
                device_id=place(dest), device_id_type=MESH,
            )
            for a, b, left, landed in pairs
        ]

    def sort_tile(k, c):
        t = lax.rem(s // g + cpg // 2 + k, cpg)
        pm = one_hot(iota((LANES, entries), 0) + (t * LANES).astype(jnp.float32) == position)
        both = lax.dot_general(
            pieces[...], pm, (((1,), (1,)), ((), ())), preferred_element_type=jnp.float32
        )
        rows = both[:LANES] + both[LANES : 2 * LANES]
        tile = both[2 * LANES : 2 * LANES + PAD]
        code = (tile[2:3] * CX + tile[0:1]) * NY + tile[1:2]
        code = jnp.broadcast_to(code, (PAD, LANES))
        for j in range(g):
            part = code if j == 0 else pltpu.roll(code, LANES - j * ps, 1)
            block = rows if j == 0 else pltpu.roll(rows, LANES - j * ps, 1)
            for i in range(ne):
                dest = i * n + t * g + j
                send[dest] = block[i * cw : (i + 1) * cw]
                facts_out[dest, 0:1] = part[0:1]
                facts_out[dest, 1:2] = delay_wide[...]

                @pl.when(dest != me)
                def _():
                    for copy in rows_to(dest):
                        copy.start()

        return c

    lax.fori_loop(0, cpg, sort_tile, 0)
    recv[me] = send[me]
    facts_in[me] = facts_out[me]

    def chunk(cc):
        delay_rows = []
        for j in range(g):
            slot = cc * g + j

            @pl.when(slot != me)
            def _():
                for ref, left, landed in ((recv, ssem, rsem), (facts_in, fssem, frsem)):
                    pltpu.make_async_remote_copy(
                        src_ref=ref.at[slot], dst_ref=ref.at[slot], send_sem=left.at[0],
                        recv_sem=landed.at[slot], device_id=(e, s), device_id_type=MESH,
                    ).wait_recv()

            delay_rows.append(facts_in[slot, 1:2])
            u_ref[pl.ds(slot, 1), :] = delay_rows[-1]
        block = recv[cc * g]
        code = jnp.broadcast_to(facts_in[cc * g, 0:1], (PAD, LANES))
        at_lane = lax.broadcasted_iota(jnp.int32, (1, LANES), 1) // ps
        for j in range(1, g):
            other = jnp.broadcast_to(facts_in[cc * g + j, 0:1], (PAD, LANES))
            block = jnp.where(at_lane == j, pltpu.roll(recv[cc * g + j], j * ps, 1), block)
            code = jnp.where(at_lane == j, pltpu.roll(other, j * ps, 1), code)
        code = code[0:1]
        ray = jnp.floor(code * (1.0 / cells))
        inside = code - ray * cells
        plane = jnp.floor(inside * (1.0 / NY))
        first = pl.multiple_of(cc * LANES, LANES)
        kt[:, pl.ds(first, LANES)] = block
        plane_ref[:, pl.ds(first, LANES)] = plane
        rr_ref[pl.ds(cc, 1), :] = ray
        hot = one_hot(iota((NY, LANES), 0) == inside - plane * NY)
        s_mat[:, pl.ds(first, LANES)] = hot
        return ray, delay_rows, hot, block, plane

    def by_plane(rows, plane):
        high = rows.astype(jnp.bfloat16).astype(jnp.float32)
        both = jnp.concatenate([high, rows - high], axis=0)
        return jnp.concatenate(
            [jnp.where(plane == float(i), both, 0.0).astype(jnp.bfloat16) for i in range(CX)], axis=0
        )

    def add_rows(terms, hot):
        acc[...] += lax.dot_general(
            terms, hot, (((1,), (1,)), ((), ())), preferred_element_type=jnp.float32
        )

    def spread(ray, weights):
        lane = lax.broadcasted_iota(jnp.int32, ray.shape, 1)
        result = jnp.zeros(ray.shape, jnp.float32)
        for j in range(g):
            mine = jnp.zeros(ray.shape, jnp.float32)
            for r in range(rays):
                mine = jnp.where(ray == float(r), weights[j][:, r : r + 1], mine)
            result = jnp.where(lane // ps == j, mine, result)
        return result

    def arrivals(k, c):
        inner = lax.rem(s // g - cpg // 2 - k + 2 * cpg, cpg)
        chunks = [lax.rem(e + j, ne) * cpg + inner for j in range(ne)]
        found = [chunk(cc) for cc in chunks]
        ray = jnp.concatenate([f[0] for f in found], axis=0)
        weights = [jnp.concatenate([f[1][j] for f in found], axis=0) for j in range(g)]
        w = spread(ray, weights)
        terms = [
            by_plane(f[3] * w[j : j + 1], f[4]) for j, f in enumerate(found)
        ]
        add_rows(jnp.concatenate(terms, axis=1), jnp.concatenate([f[2] for f in found], axis=1))
        return c

    lax.fori_loop(0, cpg, arrivals, 0)

    delays = u_ref[...]
    beta0 = jnp.sqrt(total(delays * delays) + norm_epsilon)
    u0 = delays / beta0
    lane = lax.broadcasted_iota(jnp.int32, (nc, LANES), 1)

    def rays_of(j):
        return pl.ds(j, nc, stride=g) if g > 1 else pl.ds(0, nc)

    wide = 4 * LANES

    def scatter_rays():
        w_ref[:nc] = spread(rr_ref[...], [u_ref[rays_of(j), :] for j in range(g)])
        acc[...] = jnp.zeros_like(acc)

        def block(b, c):
            at = pl.ds(pl.multiple_of(b * wide, wide), wide)
            w = jnp.concatenate([w_ref[pl.ds(b * 4 + i, 1), :] for i in range(4)], axis=1)
            add_rows(by_plane(kt[:, at] * w, plane_ref[:, at]), s_mat[:, at])
            return c

        lax.fori_loop(0, nc // 4, block, 0, unroll=True)

    def scattered(p):
        return acc[2 * cw * p : 2 * cw * p + cw] + acc[2 * cw * p + cw : 2 * cw * (p + 1)]

    def laplace(ref, p):
        x = ref[p, PAD : PAD + cw]
        row = lax.broadcasted_iota(jnp.int32, x.shape, 0) + e * cw
        col = lax.broadcasted_iota(jnp.int32, x.shape, 1)
        beside = ref[p + 1, PAD : PAD + cw] + ref[p - 1, PAD : PAD + cw]
        beside = beside + jnp.where(col < NY - 1, pltpu.roll(x, NY - 1, 1), 0.0)
        beside = beside + jnp.where(col > 0, pltpu.roll(x, 1, 1), 0.0)
        beside = beside + jnp.where(row < cw * ne - 1, ref[p, PAD + 1 : PAD + cw + 1], 0.0)
        beside = beside + jnp.where(row > 0, ref[p, PAD - 1 : PAD + cw - 1], 0.0)
        return 6.0 * x - beside

    def halo(ref, r):
        own, planes = pl.ds(PAD, cw), pl.ds(1, CX)
        moves = [
            (ref.at[CX, own], ref.at[0, own], (e, lax.rem(s + 1, n))),
            (ref.at[1, own], ref.at[CX + 1, own], (e, lax.rem(s - 1 + n, n))),
            (ref.at[planes, pl.ds(cw, PAD)], ref.at[planes, pl.ds(0, PAD)], (lax.rem(e + 1, ne), s)),
            (
                ref.at[planes, pl.ds(PAD, PAD)],
                ref.at[planes, pl.ds(PAD + cw, PAD)],
                (lax.rem(e - 1 + ne, ne), s),
            ),
        ]
        copies = [
            pltpu.make_async_remote_copy(
                src_ref=a, dst_ref=b, send_sem=halo_send.at[4 * r + i],
                recv_sem=halo_recv.at[4 * r + i], device_id=to, device_id_type=MESH,
            )
            for i, (a, b, to) in enumerate(moves)
        ]
        for copy in copies:
            copy.start()
        return copies

    def gather_parts(full, r):
        copies = [
            pltpu.make_async_remote_copy(
                src_ref=full.at[e], dst_ref=full.at[e], send_sem=full_send.at[ne * r + j],
                recv_sem=full_recv.at[r], device_id=(lax.rem(e + j, ne), s), device_id_type=MESH,
            )
            for j in range(1, ne)
        ]
        for copy in copies:
            copy.start()
        return copies

    def share(ref, sem):
        def copy(a, to):
            return pltpu.make_async_remote_copy(
                src_ref=ref.at[a], dst_ref=ref.at[a], send_sem=bsend.at[sem],
                recv_sem=brecv.at[sem], device_id=to, device_id_type=MESH,
            )

        each_other(lambda other: copy(me, place(other)).start())
        return copy(pl.ds(0, nd - 1), (e, s))

    def share_squares(numbers, squares, sem):
        lane = lax.broadcasted_iota(jnp.int32, (1, LANES), 1)
        row = jnp.zeros((1, LANES), jnp.float32)
        for i, square in enumerate(squares):
            row = jnp.where(lane == i, square, row)
        numbers[me] = row
        return share(numbers, sem)

    def tile_sum(tiles, count):
        parts = [tiles[k] for k in range(count)]
        while len(parts) > 1:
            odd = parts[len(parts) // 2 * 2 :]
            parts = [a + b for a, b in zip(parts[::2], parts[1::2])] + odd
        return parts[0]

    def apply_rays(tiles):
        def block(b, c):
            at = pl.ds(pl.multiple_of(b * wide, wide), wide)
            picked = jnp.dot(table2[...], s_mat[:, at], preferred_element_type=jnp.float32)
            plane = plane_ref[:, at]
            mine = picked[: 2 * cw]
            for i in range(1, CX):
                mine = jnp.where(plane == float(i), picked[2 * cw * i : 2 * cw * (i + 1)], mine)
            sums = jnp.sum((mine[:cw] + mine[cw:]) * kt[:, at], axis=0, keepdims=True)
            for i in range(4):
                e_ref[pl.ds(b * 4 + i, 1), :] = sums[:, i * LANES : (i + 1) * LANES]
            return c

        lax.fori_loop(0, nc // 4, block, 0, unroll=True)
        ray = rr_ref[...]
        for j in range(g):
            terms = jnp.where(lane // ps == j, e_ref[...], 0.0)
            value = jnp.zeros((nc, LANES), jnp.float32)
            for r in range(rays):
                one = jnp.sum(jnp.where(ray == float(r), terms, 0.0), axis=1, keepdims=True)
                value = jnp.where(lane == r, one, value)
            w_ref[rays_of(j), :] = value
        value = w_ref[:packed]
        for q in range(1, pack):
            value = value + pltpu.roll(w_ref[q * packed : (q + 1) * packed], q * rays, 1)
        tiles[me] = value

    def ray_sums(value):
        parts = [value] + [pltpu.roll(value, LANES - q * rays, 1) for q in range(1, pack)]
        value = jnp.concatenate(parts, axis=0)
        return jnp.where(lax.broadcasted_iota(jnp.int32, value.shape, 1) < rays, value, 0.0)

    def nothing():
        return jnp.zeros((cw, NY), jnp.float32)

    per_beta = 1.0 / beta0
    square = nothing()
    for p in range(CX):
        value = scattered(p) * per_beta
        d0[p + 1, PAD : PAD + cw] = value
        full0[e, p] = value
        table2[2 * cw * p : 2 * cw * (p + 1)] = two_parts(value)
        square = square + value * value
    halos0 = halo(d0, 0)
    apply_rays(y0)
    shared0 = [share(y0, 0)]
    for copy in halos0:
        copy.wait()
    curved = nothing()
    for p in range(CX):
        value = laplace(d0, p + 1)
        m1[p + 1, PAD : PAD + cw] = value
        curved = curved + value * value
    shared0.append(share_squares(q0, [total(square), total(curved)], 1))
    halos1 = halo(m1, 1)
    gather0 = gather_parts(full0, 0)
    for copy in shared0:
        copy.wait_recv()
    numbers = tile_sum(q0, nd)
    alpha0 = jnp.sqrt(numbers[:, 0:1] + norm_epsilon)
    curved0 = numbers[:, 1:2]

    u1 = ray_sums(tile_sum(y0, nd)) / alpha0 - alpha0 * u0
    u_ref[...] = u1
    model_square = damping * damping * (curved0 / (alpha0 * alpha0))
    beta1 = jnp.sqrt(total(u1 * u1) + model_square + norm_epsilon)
    scale1 = damping / alpha0 / beta1
    per_beta, curve, back = 1.0 / beta1, damping * scale1, beta1 / alpha0
    scatter_rays()
    for copy in halos1:
        copy.wait()
    square = nothing()
    for p in range(CX):
        value = scattered(p) * per_beta + curve * laplace(m1, p + 1)
        value = value - back * d0[p + 1, PAD : PAD + cw]
        d1[p + 1, PAD : PAD + cw] = value
        full1[e, p] = value
        table2[2 * cw * p : 2 * cw * (p + 1)] = two_parts(value)
        square = square + value * value
    halos2 = halo(d1, 2)
    gather1 = gather_parts(full1, 1)
    apply_rays(y1)
    shared1 = [share(y1, 2)]
    for copy in halos2:
        copy.wait()
    curved = nothing()
    cross = nothing()
    for p in range(CX):
        value = laplace(d1, p + 1)
        curved = curved + value * value
        cross = cross + value * m1[p + 1, PAD : PAD + cw]
    shared1.append(share_squares(q1, [total(square), total(curved), total(cross)], 3))
    rho1 = jnp.sqrt(alpha0 * alpha0 + beta1 * beta1)
    cosine1 = alpha0 / rho1
    sine1 = beta1 / rho1
    phi1 = cosine1 * beta0
    phi_bar = sine1 * beta0
    for copy in shared1:
        copy.wait_recv()
    numbers = tile_sum(q1, nd)
    alpha1 = jnp.sqrt(numbers[:, 0:1] + norm_epsilon)
    theta1 = sine1 * alpha1
    rho_bar = -cosine1 * alpha1

    u2 = ray_sums(tile_sum(y1, nd)) / alpha1 - alpha1 * (u1 / beta1)
    a, b = damping / alpha1, alpha1 * scale1
    model_square = a * a * numbers[:, 1:2] - 2.0 * a * b * numbers[:, 2:3] + b * b * curved0
    model_square = jnp.maximum(model_square, 0.0)
    beta2 = jnp.sqrt(total(u2 * u2) + model_square + norm_epsilon)
    rho2 = jnp.sqrt(rho_bar * rho_bar + beta2 * beta2)
    phi2 = rho_bar / rho2 * phi_bar

    for r, full in enumerate((full0, full1)):
        rest = full.at[pl.ds(0, ne - 1)]
        pltpu.make_async_remote_copy(
            src_ref=rest, dst_ref=rest, send_sem=full_send.at[ne * r], recv_sem=full_recv.at[r],
            device_id=(e, s), device_id_type=MESH,
        ).wait_recv()

    last = phi2 / rho2
    weight0 = (phi1 / rho1 - last * (theta1 / rho1)) / alpha0
    weight1 = last / alpha1
    for p in range(CX):
        for i in range(ne):
            out_ref[p, i * cw : (i + 1) * cw] = weight0 * full0[i, p] + weight1 * full1[i, p]

    rest = send.at[pl.ds(0, nd - 1)]
    pltpu.make_async_remote_copy(
        src_ref=rest, dst_ref=rest, send_sem=ssem.at[0], recv_sem=rsem.at[0],
        device_id=(e, s), device_id_type=MESH,
    ).wait_send()
    rest = facts_out.at[pl.ds(0, nd - 1)]
    pltpu.make_async_remote_copy(
        src_ref=rest, dst_ref=rest, send_sem=fssem.at[0], recv_sem=frsem.at[0],
        device_id=(e, s), device_id_type=MESH,
    ).wait_send()
    for copy in gather0 + gather1 + shared0 + shared1:
        copy.wait_send()


def solution(mesh):
    ne, n = mesh.shape["ev"], mesh.shape["slab"]

    def on_device(kernels, block_ids, delays):
        rays, per_ray, width = kernels.shape
        entries = rays * per_ray
        ps = entries // n
        nd = ne * n
        cw = width // ne
        rows = nd * ps
        cells = CX * NY
        f32, bf16 = jnp.float32, jnp.bfloat16
        vmem = pl.BlockSpec(memory_space=pltpu.VMEM)
        model = pltpu.VMEM((CX + 2, cw + 2 * PAD, NY), f32)
        full = pltpu.VMEM((ne, CX, cw, NY), f32)
        tiles = pltpu.VMEM((nd, nd * rays // LANES, LANES), f32)
        numbers = pltpu.VMEM((nd, 1, LANES), f32)
        small = pltpu.VMEM((rows // LANES, LANES), f32)
        by_device = pltpu.VMEM((nd, LANES), f32)
        result = pl.pallas_call(
            functools.partial(kernel, ne, n, ps, rays, cw),
            out_shape=jax.ShapeDtypeStruct((CX, width, NY), f32),
            in_specs=[pl.BlockSpec(memory_space=pltpu.HBM)] * 3,
            out_specs=vmem,
            scratch_shapes=[
                pltpu.VMEM((rays, per_ray), jnp.int32),
                pltpu.VMEM((1, rays), f32),
                pltpu.VMEM((entries, width), f32),
                pltpu.VMEM((nd, cw, LANES), f32),
                pltpu.VMEM((nd, cw, LANES), f32),
                pltpu.VMEM((nd, 2, LANES), f32),
                pltpu.VMEM((nd, 2, LANES), f32),
                pltpu.VMEM((2 * width + 2 * PAD, entries), bf16),
                pltpu.VMEM((NY, rows), bf16),
                pltpu.VMEM((cw, rows), f32),
                pltpu.VMEM((1, rows), f32),
                pltpu.VMEM((2 * cw * CX, NY), bf16),
                pltpu.VMEM((2 * cw * CX, NY), f32),
                small,
                by_device,
                small,
                by_device,
                pltpu.VMEM((rays, LANES), f32),
                pltpu.VMEM((1, LANES), f32),
                model, model, model, full, full, tiles, tiles, numbers, numbers,
                pltpu.SemaphoreType.DMA((1,)),
                pltpu.SemaphoreType.DMA((nd,)),
                pltpu.SemaphoreType.DMA((1,)),
                pltpu.SemaphoreType.DMA((nd,)),
                pltpu.SemaphoreType.DMA((12,)),
                pltpu.SemaphoreType.DMA((12,)),
                pltpu.SemaphoreType.DMA((2 * ne,)),
                pltpu.SemaphoreType.DMA((2,)),
                pltpu.SemaphoreType.DMA((4,)),
                pltpu.SemaphoreType.DMA((4,)),
                pltpu.SemaphoreType.DMA((3,)),
            ],
            compiler_params=pltpu.CompilerParams(
                collective_id=0, has_side_effects=True, vmem_limit_bytes=60 * 1024 * 1024
            ),
        )(kernels.reshape(entries, width), block_ids, delays.reshape(1, rays))
        return jnp.swapaxes(result, 1, 2)

    in_specs = (P(("ev", "slab"), None, None), P(("ev", "slab"), None), P(("ev", "slab")))
    return jax.shard_map(
        on_device, mesh=mesh, in_specs=in_specs, out_specs=P("slab", None, None), check_vma=False
    )
```
